32 devices in a mesh: wide: 8 (over y, x, core), narrow: 4 (over z).
Axes of the slice: x: 2, y: 2, z: 4, core: 2. Of those that a mesh axis runs over, the one named last changes fastest.
Arguments:
- tokens: bfloat16 [64, 512, 768], P(('wide', 'narrow')), may hold values from -6 to 6
- segments: int32 [64, 512], P(('wide', 'narrow')), may hold values from 0 to 3, never falling along the last dimension, each value on 1 to 256 neighbouring positions
- exit_layer: int32 [64], P(('wide', 'narrow')), may hold values from 0 to 1, as said below
- attn_in: bfloat16 [2, 768, 2304], replicated, may hold values from -0.21875 to 0.21875
- qv_bias: bfloat16 [2, 1536], replicated, may hold values from -3 to 3
- attn_out: bfloat16 [2, 768, 768], replicated, may hold values from -0.875 to 0.875
- out_bias: bfloat16 [2, 768], replicated, may hold values from -2 to 2
- ln_gain: bfloat16 [2, 1536], replicated, may hold values from 0.25 to 1.75
- ln_bias: bfloat16 [2, 1536], replicated, may hold values from -2 to 2
- ff_in: bfloat16 [2, 768, 3072], replicated, may hold values from -0.21875 to 0.21875
- ff_in_bias: bfloat16 [2, 3072], replicated, may hold values from -3 to 3
- ff_out: bfloat16 [2, 3072, 768], replicated, may hold values from -0.109375 to 0.109375
- ff_out_bias: bfloat16 [2, 768], replicated, may hold values from -2 to 2
- stu_proj: bfloat16 [2, 768, 128], replicated, may hold values from -0.21875 to 0.21875
- stu_bias: bfloat16 [2, 128], replicated, may hold values from -3 to 3
- pool_query: bfloat16 [2, 128], replicated, may hold values from -5 to 5
- stu_dense: bfloat16 [2, 128, 128], replicated, may hold values from -1 to 1
- stu_dense_bias: bfloat16 [2, 128], replicated, may hold values from -2 to 2
- stu_cls: bfloat16 [2, 128, 14], replicated, may hold values from -1 to 1
- stu_cls_bias: bfloat16 [2, 14], replicated, may hold values from -3 to 3
- out_cot: bfloat16 [64, 512, 768], P(('wide', 'narrow')), may hold values from -6 to 6
- logit_cot: bfloat16 [64, 2, 14], P(('wide', 'narrow')), may hold values from -6 to 6
Outputs:
- activations: bfloat16 [64, 512, 768], P(('wide', 'narrow'))
- logits: bfloat16 [64, 2, 14], P(('wide', 'narrow'))
- grad_tokens: bfloat16 [64, 512, 768], P(('wide', 'narrow'))
- grad_attn_in: float32 [2, 768, 2304], P(None, 'narrow')
- grad_qv_bias: float32 [2, 1536], P(None, 'narrow')
- grad_attn_out: float32 [2, 768, 768], P(None, 'narrow')
- grad_out_bias: float32 [2, 768], P(None, 'narrow')
- grad_ln_gain: float32 [2, 1536], P(None, 'narrow')
- grad_ln_bias: float32 [2, 1536], P(None, 'narrow')
- grad_ff_in: float32 [2, 768, 3072], P(None, 'narrow')
- grad_ff_in_bias: float32 [2, 3072], P(None, 'narrow')
- grad_ff_out: float32 [2, 3072, 768], P(None, 'narrow')
- grad_ff_out_bias: float32 [2, 768], P(None, 'narrow')
- grad_stu_proj: float32 [2, 768, 128], P(None, 'narrow')
- grad_stu_bias: float32 [2, 128], P(None, 'narrow')
- grad_pool_query: float32 [2, 128], P(None, 'narrow')
- grad_stu_dense: float32 [2, 128, 128], P(None, 'narrow')
- grad_stu_dense_bias: float32 [2, 128], P(None, 'narrow')
- grad_stu_cls: float32 [2, 128, 14], P(None, 'narrow')
- grad_stu_cls_bias: float32 [2, 14], replicated
The draws below stay inside these ranges and needn't reach their ends.
Inputs may be any that keep to these rules, and one draw needn't show every extreme that they name: `exit_layer`: exactly half of the rows of each aligned block of 4 × 2 rows have exit layer 1, and in each such block all 2 rows of one device do.
All inputs are finite; a program needn't handle non-finite values.
Results may differ from the reference program's by a relative error of at most 0.022.
Values may be sent and summed in bfloat16 or wider, within the bound.
No kernel may reach another device: no remote copies, remote signals or barrier semaphores. Data moves between devices by JAX's collectives and lax.ppermute only.
A program may use at most 320 MiB of HBM per device.

```python
import math
import jax
import jax.numpy as jnp
import numpy as np
from jax import lax

D = 768
HEADS = 12
FF = 3072
SD = 128
STU_HEADS = 2
CLASSES = 14
L = 512
ROWS_DEV = 2
ROWS = 64
N_NARROW = 4


def draw_exit_layer(key, part):
    key = jax.random.fold_in(key, 7)
    pick_key, order_key = jax.random.split(key)
    block_rows = N_NARROW * ROWS_DEV
    group_count = ROWS // block_rows
    whole_dev = jax.random.randint(pick_key, (group_count, 1), 0, N_NARROW)
    positions = jnp.arange(block_rows)[None, :]
    whole_rows = positions // ROWS_DEV == whole_dev
    order_keys = jax.random.split(order_key, group_count)
    shuffled = jax.vmap(lambda key_item: jax.random.permutation(key_item, block_rows))(order_keys)
    priority = jnp.where(whole_rows, block_rows + shuffled, shuffled)
    placing = jnp.argsort(jnp.argsort(priority, axis=1, stable=True), axis=1, stable=True)
    extra_alive = (N_NARROW - 2) * ROWS_DEV // 2
    alive_rows = whole_rows | (placing < extra_alive)
    return alive_rows.astype(jnp.int32).reshape(ROWS)


def steps_of(key, extent, pieces, smallest, top_value):
    factor_of, own = 1.0, jax.random.fold_in(key, 6)
    for dim, parts in pieces:
        steps = jnp.exp(jax.random.uniform(jax.random.fold_in(own, dim), (parts,), jnp.float32, smallest / len(pieces), top_value / len(pieces)))
        factor_of = factor_of * jnp.repeat(steps, extent[dim] // parts).reshape([-1 if axis == dim else 1 for axis in range(len(extent))])
    return factor_of


def profile(number_of, total, reach, lean):
    loads = [(1 << 20) // math.isqrt(rank ** lean) + 1 for rank in range(2, number_of + 1)]
    rest, holding = total - reach - (number_of - 1), [1] * (number_of - 1)
    while rest > 0:
        candidates = [i for i in range(number_of - 1) if holding[i] < reach]
        whole, remaining = sum([loads[i] for i in candidates]), rest
        for i in candidates:
            more = min(reach - holding[i], max(1, remaining * loads[i] // whole), rest)
            holding[i] = holding[i] + more
            rest = rest - more
    return np.array([reach] + holding)


def uneven_parts(rng, amount, total, limit, skew):
    if amount == 2:
        one = jax.random.randint(rng, (), max(1, total - limit), min(limit, total - 1) + 1)
        return jnp.stack([one, total - one])
    lengths = jnp.asarray(profile(amount, total, limit, skew), jnp.int32)
    pairs = (amount - 1) // 2
    donor, sink = lengths[1:1 + 2 * pairs:2], lengths[2:2 + 2 * pairs:2]
    room = jnp.minimum(donor - 1, limit - sink)
    moved = jax.random.randint(jax.random.fold_in(rng, 1), (pairs,), 0, 1 << 20) % (room + 1)
    lengths = lengths.at[1:1 + 2 * pairs:2].set(donor - moved).at[2:2 + 2 * pairs:2].set(sink + moved)
    return lengths[jax.random.permutation(jax.random.fold_in(rng, 2), amount)]


def bell_draw(key, shape, scale, bound, cuts=(), held_as=jnp.bfloat16):
    result = jax.random.normal(key, shape, jnp.float32) * scale
    if len(cuts) > 0:
        result = steps_of(key, shape, cuts, -0.22, 0.18) * result
    return jnp.clip(result, min=-bound, max=bound).astype(held_as)


def setup_inputs(seed: int = 0) -> dict:
    key_list = jax.random.split(jax.random.key(seed), 23)
    tokens = bell_draw(key_list[0], (ROWS, L, D), 1.0, 6.0, ((0, 32),))
    segments = jax.vmap(lambda own: jnp.searchsorted(jnp.cumsum(uneven_parts(own, 4, L, L // 2, 0)), jnp.arange(L), side="right"))(jax.random.split(key_list[1], ROWS)).reshape((ROWS, L)).astype(jnp.int32)
    exit_layer = draw_exit_layer(jax.random.fold_in(key_list[22], 71), 0)
    attn_in = bell_draw(key_list[3], (2, D, 3 * D), D ** -0.5, 0.21875)
    qv_bias = bell_draw(key_list[4], (2, 2 * D), 0.5, 3.0)
    attn_out = bell_draw(key_list[5], (2, D, D), (D // 16) ** -0.5, 0.875)
    out_bias = bell_draw(key_list[6], (2, D), 0.3, 2.0)
    ln_gain = jnp.clip(1.0 + 0.15 * jax.random.normal(key_list[7], (2, 2 * D), jnp.float32), 0.25, 1.75).astype(jnp.bfloat16)
    ln_bias = bell_draw(key_list[8], (2, 2 * D), 0.3, 2.0)
    ff_in = bell_draw(key_list[9], (2, D, FF), D ** -0.5, 0.21875)
    ff_in_bias = bell_draw(key_list[10], (2, FF), 0.5, 3.0)
    ff_out = bell_draw(key_list[11], (2, FF, D), FF ** -0.5, 0.109375)
    ff_out_bias = bell_draw(key_list[12], (2, D), 0.3, 2.0)
    stu_proj = bell_draw(key_list[13], (2, D, SD), D ** -0.5, 0.21875)
    stu_bias = bell_draw(key_list[14], (2, SD), 0.5, 3.0)
    pool_query = bell_draw(key_list[15], (2, SD), 1.0, 5.0)
    stu_dense = bell_draw(key_list[16], (2, SD, SD), (SD // 4) ** -0.5, 1.0)
    stu_dense_bias = bell_draw(key_list[17], (2, SD), 0.3, 2.0)
    stu_cls = bell_draw(key_list[18], (2, SD, CLASSES), (SD // 4) ** -0.5, 1.0)
    stu_cls_bias = bell_draw(key_list[19], (2, CLASSES), 0.5, 3.0)
    out_cot = bell_draw(key_list[20], (ROWS, L, D), 1.0, 6.0, ((0, 32),))
    logit_cot = bell_draw(key_list[21], (ROWS, 2, CLASSES), 1.0, 6.0, ((0, 32),))
    return {"tokens": tokens, "segments": segments, "exit_layer": exit_layer, "attn_in": attn_in, "qv_bias": qv_bias, "attn_out": attn_out, "out_bias": out_bias, "ln_gain": ln_gain, "ln_bias": ln_bias, "ff_in": ff_in, "ff_in_bias": ff_in_bias, "ff_out": ff_out, "ff_out_bias": ff_out_bias, "stu_proj": stu_proj, "stu_bias": stu_bias, "pool_query": pool_query, "stu_dense": stu_dense, "stu_dense_bias": stu_dense_bias, "stu_cls": stu_cls, "stu_cls_bias": stu_cls_bias, "out_cot": out_cot, "logit_cot": logit_cot}


eps_norm = 1e-12
highest = lax.Precision.HIGHEST

@jax.custom_vjp
def low(v):
    return lax.optimization_barrier(v.astype(jnp.bfloat16)).astype(jnp.float32)

@jax.custom_vjp
def low_back(v):
    return v

def low_keep(v):
    return (low(v), None)

def low_pass(kept, grad):
    return (grad,)

def back_keep(v):
    return (v, None)

def back_low(kept, grad):
    return (low(grad),)
low.defvjp(low_keep, low_pass)
low_back.defvjp(back_keep, back_low)

def low_both(values):
    return low(low_back(values))

def norm(values, gain_vec, shift_vec):
    mean_val = lax.optimization_barrier(jnp.mean(values, -1, keepdims=True))
    centered = values - mean_val
    variance = lax.optimization_barrier(jnp.mean(centered * centered, -1, keepdims=True))
    return centered * lax.rsqrt(variance + eps_norm) * gain_vec + shift_vec

def student_head(proj_rows, pool_query, dense, dense_bias, classes_w, classes_bias):
    row_count, seq_len, stu_width = proj_rows.shape
    head_width = stu_width // STU_HEADS
    head_split = proj_rows.reshape(row_count, seq_len, STU_HEADS, head_width)
    queries = pool_query.reshape(STU_HEADS, head_width)
    pool_scores = lax.optimization_barrier(jnp.sum(head_split * queries, -1)) * head_width ** (-0.5)
    weights = jax.nn.softmax(pool_scores, axis=1)
    pooled = lax.optimization_barrier(jnp.sum(weights[..., None] * head_split, 1)).reshape(row_count, stu_width)
    dense_out = jnp.tanh(jnp.dot(pooled, dense, precision=highest) + dense_bias)
    return jnp.dot(dense_out, classes_w, precision=highest) + classes_bias

def layer_row(layer_in, seg_row, weights):
    attn_in, qv_bias, attn_out, out_bias, gain_vec, shift_vec, ff_in, ff_in_bias, ff_out, ff_out_bias = weights
    seq_len, model_width = layer_in.shape
    head_width = model_width // HEADS
    zero_bias = jnp.zeros((model_width,), jnp.float32)
    full_bias = jnp.concatenate([qv_bias[:model_width], zero_bias, qv_bias[model_width:]])
    qkv_rows = low_both(jnp.dot(layer_in, attn_in, precision=highest) + full_bias)
    qkv_rows = qkv_rows.reshape(seq_len, 3, HEADS, head_width)
    scores = jnp.einsum('qhd,khd->hqk', qkv_rows[:, 0], qkv_rows[:, 1], precision=highest) * head_width ** (-0.5)
    scores = low_back(scores)
    same_doc = seg_row[:, None] == seg_row[None, :]
    scores = jnp.where(same_doc[None], scores, -1e+30)
    prob_rows = low(jax.nn.softmax(scores, axis=-1))
    mix_out = jnp.einsum('hqk,khd->qhd', prob_rows, qkv_rows[:, 2], precision=highest)
    mix_out = low_both(mix_out).reshape(seq_len, model_width)
    branch = low_back(jnp.dot(mix_out, attn_out, precision=highest) + out_bias)
    first_norm = norm(layer_in + branch, gain_vec[:model_width], shift_vec[:model_width])
    ff_inner = low_back(jnp.dot(low(first_norm), ff_in, precision=highest) + ff_in_bias)
    active = low(jax.nn.gelu(ff_inner, approximate=False))
    second = low_back(jnp.dot(active, ff_out, precision=highest) + ff_out_bias)
    return low(norm(first_norm + second, gain_vec[model_width:], shift_vec[model_width:]))

def apply_layer(layer_in, segments, weights):
    row_step = jax.checkpoint(layer_row)
    return lax.map(lambda row_pair: row_step(row_pair[0], row_pair[1], weights), (layer_in, segments))

def student(hidden, weights):
    proj, proj_bias, pool_query, dense, dense_bias, classes_w, classes_bias = weights
    proj_rows = low_back(jnp.einsum('rld,ds->rls', hidden, proj, precision=highest) + proj_bias)
    return student_head(proj_rows, pool_query, dense, dense_bias, classes_w, classes_bias)

def reference(tokens, segments, exit_layer, attn_in, qv_bias, attn_out, out_bias, ln_gain, ln_bias, ff_in, ff_in_bias, ff_out, ff_out_bias, stu_proj, stu_bias, pool_query, stu_dense, stu_dense_bias, stu_cls, stu_cls_bias, out_cot, logit_cot):
    params = tuple((item.astype(jnp.float32) for item in (attn_in, qv_bias, attn_out, out_bias, ln_gain, ln_bias, ff_in, ff_in_bias, ff_out, ff_out_bias, stu_proj, stu_bias, pool_query, stu_dense, stu_dense_bias, stu_cls, stu_cls_bias)))
    alive_mask = exit_layer == 1

    def forward(layer_in, weights):
        layer_zero = tuple((item[0] for item in weights[:10]))
        layer_one = tuple((item[1] for item in weights[:10]))
        head_zero = tuple((item[0] for item in weights[10:]))
        head_one = tuple((item[1] for item in weights[10:]))
        hidden_zero = apply_layer(layer_in, segments, layer_zero)
        logits_zero = student(hidden_zero, head_zero)
        hidden_one = apply_layer(low_back(hidden_zero), segments, layer_one)
        logits_one = student(hidden_one, head_one)
        activations = jnp.where(alive_mask[:, None, None], hidden_one, hidden_zero)
        logit_pair = jnp.stack([logits_zero, jnp.where(alive_mask[:, None], logits_one, 0.0)], 1)
        return (activations, logit_pair)
    (activations, logit_pair), back_fn = jax.vjp(forward, tokens.astype(jnp.float32), params)
    grad_in, gradients = back_fn((out_cot.astype(jnp.float32), logit_cot.astype(jnp.float32)))
    return (activations.astype(jnp.bfloat16), logit_pair.astype(jnp.bfloat16), grad_in.astype(jnp.bfloat16), gradients[0], gradients[1], gradients[2], gradients[3], gradients[4], gradients[5], gradients[6], gradients[7], gradients[8], gradients[9], gradients[10], gradients[11], gradients[12], gradients[13], gradients[14], gradients[15], gradients[16])
```

```python
from functools import partial

import jax
import jax.numpy as jnp
import numpy as np
from jax import lax
from jax.experimental import pallas as pl
from jax.experimental.pallas import tpu as pltpu
from jax.sharding import PartitionSpec as P

HEADS = 12
HEAD = 64
STU_HEADS = 2
LANES = 128
CHUNK = 128
REACH = 256
EPS = 1e-12
MASKED = -1e30
HIGH = lax.Precision.HIGHEST
F32 = jnp.float32
BF16 = jnp.bfloat16
LIMIT = 52 * 1024 * 1024

NN = (((1,), (0,)), ((), ()))
NT = (((1,), (1,)), ((), ()))
TN = (((0,), (0,)), ((), ()))


def mm(left, right, dims=NN):
    return lax.dot_general(left, right, dims, preferred_element_type=F32)


def mm_high(left, right, dims=NN):
    return lax.dot_general(left, right, dims, precision=HIGH, preferred_element_type=F32)


def vec(ref, layer, start, size):
    return ref[...].astype(F32)[layer : layer + 1, start : start + size]


def gelu_pair(value):
    dist = jnp.abs(value) * (0.5**0.5)
    den = 1.0 + 0.3275911 * dist
    part = pl.reciprocal(den, approx=True)
    part = part * (2.0 - den * part)
    series = 0.5 * 1.061405429
    for term in (-1.453152027, 1.421413741, -0.284496736, 0.254829592):
        series = series * part + 0.5 * term
    bell = jnp.exp(-(dist * dist))
    tail = series * part * bell
    below = jnp.where(value >= 0, 1.0 - tail, tail)
    return value * below, below + value * bell * ((2.0 * np.pi) ** -0.5)


def row_norm(value):
    mean = jnp.mean(value, -1, keepdims=True)
    centered = value - mean
    spread = lax.rsqrt(jnp.mean(centered * centered, -1, keepdims=True) + EPS)
    return centered * spread, spread


def norm_back(grad, hat, spread, gain):
    scaled = grad * gain
    low = jnp.mean(scaled, -1, keepdims=True)
    high = jnp.mean(scaled * hat, -1, keepdims=True)
    return spread * (scaled - low - hat * high)


def window(place, length):
    start = max(0, (place - REACH + 1) // CHUNK * CHUNK)
    stop = min(length, -(-(place + CHUNK + REACH - 1) // CHUNK) * CHUNK)
    return start, stop


def fill_bias(seg_ref, row, bias_ref):
    length = bias_ref.shape[0]
    seg_row = seg_ref[pl.ds(row, 1), :].astype(F32)
    seg_cols = jnp.broadcast_to(seg_row, (LANES, length)).T
    for start in range(0, length, LANES):
        same = seg_cols == seg_row[:, start : start + LANES]
        bias_ref[:, start : start + LANES] = jnp.where(same, 0.0, MASKED)


ANY = pl.BlockSpec(memory_space=pl.ANY)
WHOLE = pl.BlockSpec(memory_space=pltpu.VMEM)
SCALAR = pl.BlockSpec(memory_space=pltpu.SMEM)


def low(*shape):
    return jax.ShapeDtypeStruct(shape, BF16)


def full(*shape):
    return jax.ShapeDtypeStruct(shape, F32)


def vm(like):
    return pltpu.VMEM(like.shape, like.dtype)


def call(kernel, name, outs, out_specs, inputs, in_specs, scratch, after, flops, moved):
    count, extra = len(inputs), len(after)

    def body(*refs):
        kernel(*refs[:count], *refs[count + extra :])

    return pl.pallas_call(
        body,
        out_shape=outs,
        in_specs=list(in_specs) + [ANY] * extra,
        out_specs=out_specs,
        scratch_shapes=scratch,
        compiler_params=pltpu.CompilerParams(vmem_limit_bytes=LIMIT),
        cost_estimate=pl.CostEstimate(flops=flops, bytes_accessed=moved, transcendentals=0),
        name=name,
    )(*inputs, *after)


def copier(sems):
    def copy(src, dst, number):
        made = pltpu.make_async_copy(src, dst, sems.at[number])
        made.start()
        return made

    return copy


def chunks(length):
    return [slice(place, place + CHUNK) for place in range(0, length, CHUNK)]


def forward_attention_kernel(
    layer,
    scale,
    row_ref,
    x_hbm,
    seg_ref,
    w_in_hbm,
    w_out_hbm,
    qv_ref,
    out_b_ref,
    gain_ref,
    shift_ref,
    qkv_hbm,
    lse_ref,
    mixed_hbm,
    hat_hbm,
    first_hbm,
    full_hbm,
    spread_ref,
    x_ref,
    w_in,
    w_out,
    qkv,
    mixed,
    hat,
    first,
    full,
    bias,
    terms_ref,
    sems,
):
    row = row_ref[0]
    length, width = x_ref.shape
    copy = copier(sems)
    get_x = copy(x_hbm.at[row], x_ref, 0)
    get_in = copy(w_in_hbm.at[layer], w_in, 1)
    get_out = copy(w_out_hbm.at[layer], w_out, 2)
    fill_bias(seg_ref, row, bias)
    terms_ref[...] = jnp.zeros_like(terms_ref)
    lse_ref[...] = jnp.zeros_like(lse_ref)
    get_x.wait()
    get_in.wait()

    x = x_ref[...]
    qkv[:, :width] = (
        (mm(x, w_in[:, :width]) + vec(qv_ref, layer, 0, width)).astype(BF16).astype(F32) * scale
    ).astype(BF16)
    qkv[:, width : 2 * width] = mm(x, w_in[:, width : 2 * width]).astype(BF16)
    qkv[:, 2 * width :] = (
        mm(x, w_in[:, 2 * width :]) + vec(qv_ref, layer, width, width)
    ).astype(BF16)
    put_qkv = copy(qkv, qkv_hbm, 3)

    low_half = lax.broadcasted_iota(jnp.int32, (length, LANES), 1) < HEAD
    low_rows = lax.broadcasted_iota(jnp.int32, (LANES, length), 0) < HEAD

    def pair(number, carry):
        at = pl.multiple_of(number * LANES, LANES)
        queries = qkv[:, pl.ds(at, LANES)]
        keys = qkv[:, pl.ds(at + width, LANES)]
        values_t = qkv[:, pl.ds(at + 2 * width, LANES)].T
        outs = []
        for sub in range(2):
            mine = jnp.where(low_half == (sub == 0), keys, jnp.zeros_like(keys))
            scores = mm(mine, queries, NT)
            tops = []
            for cols in chunks(length):
                start, stop = window(cols.start, length)
                part = scores[start:stop, cols] + bias[start:stop, cols]
                top = jnp.max(part, 0, keepdims=True)
                terms_ref[sub, start:stop, cols] = jnp.exp(part - top).astype(BF16)
                tops.append(top)
            mine_t = jnp.where(low_rows == (sub == 0), values_t, jnp.ones_like(values_t))
            product = mm(mine_t, terms_ref[sub])
            beside = HEAD * (1 - sub)
            total = product[beside : beside + 1, :]
            lse_ref[pl.ds(2 * number + sub, 1), :] = jnp.concatenate(tops, 1) + jnp.log(total)
            outs.append(product * (1.0 / total))
        mixed[:, pl.ds(at, LANES)] = jnp.where(low_rows, outs[0], outs[1]).T.astype(BF16)
        return carry

    lax.fori_loop(0, HEADS * HEAD // LANES, pair, 0)
    put_mixed = copy(mixed, mixed_hbm, 4)

    get_out.wait()
    gain, shift = vec(gain_ref, layer, 0, width), vec(shift_ref, layer, 0, width)
    out_b = vec(out_b_ref, layer, 0, width)
    branch = mm(mixed[...], w_out[...])
    for rows in chunks(length):
        normed, spread = row_norm(x_ref[rows, :].astype(F32) + branch[rows] + out_b)
        hat[rows, :] = normed.astype(BF16)
        normed = normed * gain + shift
        full[rows, :] = normed
        first[rows, :] = normed.astype(BF16)
        spread_ref[rows, :] = jnp.broadcast_to(spread, (CHUNK, LANES))
    puts = (copy(hat, hat_hbm, 5), copy(first, first_hbm, 6), copy(full, full_hbm, 7))
    for made in (put_qkv, put_mixed) + puts:
        made.wait()


def forward_attention(layer, row, x, seg, weights, after=()):
    w_in, qv, w_out, out_b, gain, shift = weights[:6]
    length, width = x.shape[-2], x.shape[-1]
    outs = (
        low(length, 3 * width),
        full(16, length),
        low(length, width),
        low(length, width),
        low(length, width),
        full(length, width),
        full(length, LANES),
    )
    return call(
        partial(forward_attention_kernel, layer, HEAD**-0.5),
        f"forward_attention{layer}",
        outs,
        (ANY, WHOLE) + (ANY,) * 4 + (WHOLE,),
        (row, x, seg, w_in, w_out, qv, out_b, gain, shift),
        [SCALAR, ANY, WHOLE, ANY, ANY] + [WHOLE] * 4,
        [
            pltpu.VMEM((length, width), BF16),
            pltpu.VMEM(w_in.shape[1:], BF16),
            pltpu.VMEM(w_out.shape[1:], BF16),
            vm(outs[0]),
            vm(outs[2]),
            vm(outs[3]),
            vm(outs[4]),
            vm(outs[5]),
            pltpu.VMEM((length, length), F32),
            pltpu.VMEM((2, length, length), BF16),
            pltpu.SemaphoreType.DMA((8,)),
        ],
        after,
        14 * 10**9,
        16 * 10**6,
    )


def forward_ff_kernel(
    layer,
    row_ref,
    first_hbm,
    full_hbm,
    cot_ref,
    w_fi_hbm,
    w_fo_hbm,
    gain_ref,
    shift_ref,
    fi_b_ref,
    fo_b_ref,
    proj_ref,
    proj_b_ref,
    query_ref,
    dense_ref,
    dense_b_ref,
    cls_ref,
    cls_b_ref,
    slope_hbm,
    active_hbm,
    hat_hbm,
    h_hbm,
    spread_ref,
    d_upper_ref,
    logit_ref,
    small_ref,
    first,
    full,
    w_fi,
    w_fo,
    slope,
    active,
    hat,
    h,
    even,
    odd,
    sems,
):
    length, width = first.shape
    ff = w_fi.shape[1]
    copy = copier(sems)
    get_first = copy(first_hbm, first, 0)
    get_fi = copy(w_fi_hbm.at[layer], w_fi, 1)
    get_full = copy(full_hbm, full, 2)
    get_fo = copy(w_fo_hbm.at[layer], w_fo, 3)
    get_first.wait()
    get_fi.wait()
    part = even.shape[1]

    def multiply(at, into):
        into[...] = mm(first[...], w_fi[:, pl.ds(at, part)])

    def bend(at, source):
        bias_part = fi_b_ref[:, pl.ds(at, part)].astype(F32)[layer : layer + 1]
        for rows in chunks(length):
            out, grad = gelu_pair(source[rows, :] + bias_part)
            active[rows, pl.ds(at, part)] = out.astype(BF16)
            slope[rows, pl.ds(at, part)] = grad.astype(BF16)

    multiply(0, even)
    steps = ff // part // 2

    def inner(number, carry):
        at = pl.multiple_of(number * (2 * part), 2 * part)
        multiply(at + part, odd)
        bend(at, even)
        later = pl.multiple_of(jnp.minimum(at + 2 * part, ff - part), part)
        multiply(later, even)
        bend(at + part, odd)
        return carry

    lax.fori_loop(0, steps, inner, 0)
    put_slope = copy(slope, slope_hbm, 4)
    put_active = copy(active, active_hbm, 5)

    get_fo.wait()
    get_full.wait()
    gain, shift = vec(gain_ref, layer, width, width), vec(shift_ref, layer, width, width)
    fo_b = vec(fo_b_ref, layer, 0, width)
    second = mm(active[...], w_fo[...])
    for rows in chunks(length):
        normed, spread = row_norm(full[rows, :] + second[rows] + fo_b)
        hat[rows, :] = normed.astype(BF16)
        h[rows, :] = (normed * gain + shift).astype(BF16)
        spread_ref[rows, :] = jnp.broadcast_to(spread, (CHUNK, LANES))
    put_hat = copy(hat, hat_hbm, 6)
    put_h = copy(h, h_hbm, 7)

    stu_width = proj_ref.shape[2]
    stu_scale = (stu_width // STU_HEADS) ** -0.5
    hidden = h[...]
    upper = mm(hidden, proj_ref[layer]) + vec(proj_b_ref, layer, 0, stu_width)
    query = vec(query_ref, layer, 0, stu_width)
    lane_full = lax.broadcasted_iota(jnp.int32, (length, stu_width), 1)
    left = lane_full < stu_width // STU_HEADS

    def both(value):
        zero = jnp.zeros_like(value)
        return (
            jnp.sum(jnp.where(left, value, zero), -1, keepdims=True),
            jnp.sum(jnp.where(left, zero, value), -1, keepdims=True),
        )

    weights = []
    for score in both(upper * query):
        score = score * stu_scale
        terms = jnp.exp(score - jnp.max(score, 0, keepdims=True))
        weights.append(terms / jnp.sum(terms, 0, keepdims=True))
    weight = jnp.where(left, weights[0], weights[1])
    pooled = jnp.sum(weight * upper, 0, keepdims=True)
    dense = dense_ref[layer].astype(F32)
    cls = cls_ref[layer].astype(F32)
    eight = (8, stu_width)
    z = jnp.tanh(
        mm_high(jnp.broadcast_to(pooled, eight), dense) + vec(dense_b_ref, layer, 0, stu_width)
    )
    logit_ref[...] = mm_high(z, cls) + vec(cls_b_ref, layer, 0, LANES)
    cot = cot_ref[pl.ds(row_ref[0], 1), :]
    d_pre = mm_high(jnp.broadcast_to(cot, (8, LANES)), cls, NT) * (1.0 - z * z)
    d_pooled = mm_high(d_pre, dense, NT)[:1]
    d_pre = d_pre[:1]

    def column(value):
        return jnp.broadcast_to(value, (value.shape[1], value.shape[1])).T

    d_scores = []
    for weight_col, d_weight in zip(weights, both(upper * d_pooled)):
        mean = jnp.sum(weight_col * d_weight, 0, keepdims=True)
        d_scores.append(weight_col * (d_weight - mean) * stu_scale)
    d_score = jnp.where(left, d_scores[0], d_scores[1])
    d_upper = (weight * d_pooled + d_score * query).astype(BF16)
    d_upper_ref[...] = d_upper
    small_ref[:width, :] = mm(hidden, d_upper, TN)
    small_ref[width : width + stu_width, :] = column(pooled) * d_pre
    small_ref[width + stu_width : width + 2 * stu_width, :] = column(z[:1]) * cot
    base = width + 2 * stu_width
    small_ref[base : base + 1, :] = jnp.sum(d_upper.astype(F32), 0, keepdims=True)
    small_ref[base + 1 : base + 2, :] = jnp.sum(d_score * upper, 0, keepdims=True)
    small_ref[base + 2 : base + 3, :] = d_pre
    small_ref[base + 3 : base + 4, :] = cot
    small_ref[base + 4 :, :] = jnp.zeros((4, LANES), F32)

    for made in (put_slope, put_active, put_hat, put_h):
        made.wait()


def forward_ff(layer, row, first, first_full, cot, weights, after=()):
    gain, shift, w_fi, fi_b, w_fo, fo_b = weights[4:10]
    length, width = first.shape
    ff = w_fi.shape[2]
    stu = weights[10].shape[2]
    outs = (
        low(length, ff),
        low(length, ff),
        low(length, width),
        low(length, width),
        full(length, LANES),
        low(length, stu),
        full(8, LANES),
        full(width + 2 * stu + 8, LANES),
    )
    return call(
        partial(forward_ff_kernel, layer),
        f"forward_ff{layer}",
        outs,
        (ANY,) * 4 + (WHOLE,) * 4,
        (row, first, first_full, cot, w_fi, w_fo, gain, shift, fi_b, fo_b) + tuple(weights[10:]),
        [SCALAR, ANY, ANY, WHOLE, ANY, ANY] + [WHOLE] * 11,
        [
            pltpu.VMEM((length, width), BF16),
            pltpu.VMEM((length, width), F32),
            pltpu.VMEM(w_fi.shape[1:], BF16),
            pltpu.VMEM(w_fo.shape[1:], BF16),
            vm(outs[0]),
            vm(outs[1]),
            vm(outs[2]),
            vm(outs[3]),
            pltpu.VMEM((length, 512), F32),
            pltpu.VMEM((length, 512), F32),
            pltpu.SemaphoreType.DMA((8,)),
        ],
        after,
        18 * 10**9,
        20 * 10**6,
    )


def backward_ff_kernel(
    layer,
    grad_ref,
    d_upper_ref,
    spread1_ref,
    spread2_ref,
    proj_ref,
    gain_ref,
    w_fi_hbm,
    w_fo_hbm,
    hat1_hbm,
    slope_hbm,
    hat2_hbm,
    second_hbm,
    inner_hbm,
    branch_hbm,
    resid_hbm,
    sums_ref,
    w_fi,
    w_fo,
    hat1,
    slope,
    hat2,
    second,
    inner,
    branch,
    d_resid,
    sems,
):
    length, width = grad_ref.shape
    ff = w_fi.shape[1]
    copy = copier(sems)
    get_hat2 = copy(hat2_hbm, hat2, 0)
    get_fo = copy(w_fo_hbm.at[layer], w_fo, 1)
    get_slope = copy(slope_hbm, slope, 2)
    get_fi = copy(w_fi_hbm.at[layer], w_fi, 3)
    get_hat1 = copy(hat1_hbm, hat1, 4)
    sums_ref[...] = jnp.zeros_like(sums_ref)
    get_hat2.wait()
    gain1, gain2 = vec(gain_ref, layer, 0, width), vec(gain_ref, layer, width, width)
    total = lambda value: jnp.sum(value.astype(F32), 0, keepdims=True)

    def through_norm(grads, hat_ref, spread_ref, gain, out_ref):
        d_gain = jnp.zeros((1, width), F32)
        d_shift = jnp.zeros((1, width), F32)
        d_bias = jnp.zeros((1, width), F32)
        for rows in chunks(length):
            grad = grads(rows)
            hat = hat_ref[rows, :].astype(F32)
            d_gain += total(grad * hat)
            d_shift += total(grad)
            moved = norm_back(grad, hat, spread_ref[rows, 0:1], gain)
            d_resid[rows, :] = moved
            out_ref[rows, :] = moved.astype(BF16)
            d_bias += total(moved.astype(BF16))
        return d_gain, d_shift, d_bias

    from_student = mm(d_upper_ref[...], proj_ref[layer], NT)
    d_gain, d_shift, d_bias = through_norm(
        lambda rows: grad_ref[rows, :].astype(F32) + from_student[rows],
        hat2,
        spread2_ref,
        gain2,
        second,
    )
    sums_ref[1:2, 3 * width : 4 * width] = d_gain
    sums_ref[2:3, width : 2 * width] = d_shift
    sums_ref[2:3, 3 * width : 4 * width] = d_bias
    put_second = copy(second, second_hbm, 5)

    get_fo.wait()
    get_slope.wait()
    part = 512

    def ff_part(number, carry):
        at = pl.multiple_of(number * part, part)
        column = jnp.zeros((1, part), F32)
        d_active = mm(second[...], w_fo[pl.ds(at, part), :], NT)
        for rows in chunks(length):
            d_inner = (d_active[rows] * slope[rows, pl.ds(at, part)].astype(F32)).astype(BF16)
            inner[rows, pl.ds(at, part)] = d_inner
            column += total(d_inner)
        sums_ref[0:1, pl.ds(at, part)] = column
        return carry

    lax.fori_loop(0, ff // part, ff_part, 0)
    put_inner = copy(inner, inner_hbm, 6)

    get_fi.wait()
    get_hat1.wait()
    d_first = mm(inner[...], w_fi[...], NT)
    d_gain, d_shift, d_bias = through_norm(
        lambda rows: d_resid[rows, :] + d_first[rows], hat1, spread1_ref, gain1, branch
    )
    sums_ref[1:2, 2 * width : 3 * width] = d_gain
    sums_ref[2:3, :width] = d_shift
    sums_ref[2:3, 2 * width : 3 * width] = d_bias
    for made in (
        put_second,
        put_inner,
        copy(branch, branch_hbm, 7),
        copy(d_resid, resid_hbm, 8),
    ):
        made.wait()


def backward_ff(layer, grad, saved1, saved2, weights, after=()):
    _, _, _, hat1, _, _, spread1 = saved1
    slope, _, hat2, _, spread2, d_upper, _, _ = saved2
    gain, _, w_fi, _, w_fo, _ = weights[4:10]
    length, width = grad.shape
    ff = w_fi.shape[2]
    outs = (
        low(length, width),
        low(length, ff),
        low(length, width),
        full(length, width),
        full(8, ff),
    )
    return call(
        partial(backward_ff_kernel, layer),
        f"backward_ff{layer}",
        outs,
        (ANY,) * 4 + (WHOLE,),
        (grad, d_upper, spread1, spread2, weights[10], gain, w_fi, w_fo, hat1, slope, hat2),
        [WHOLE] * 6 + [ANY] * 5,
        [
            pltpu.VMEM(w_fi.shape[1:], BF16),
            pltpu.VMEM(w_fo.shape[1:], BF16),
            vm(hat1),
            vm(slope),
            vm(hat2),
            vm(outs[0]),
            vm(outs[1]),
            vm(outs[2]),
            vm(outs[3]),
            pltpu.SemaphoreType.DMA((9,)),
        ],
        after,
        16 * 10**9,
        22 * 10**6,
    )


def backward_attention_kernel(
    layer,
    scale,
    row_ref,
    seg_ref,
    lse_ref,
    w_in_hbm,
    w_out_hbm,
    qkv_hbm,
    mixed_hbm,
    branch_hbm,
    resid_hbm,
    d_qkv_hbm,
    d_x_ref,
    sums_ref,
    w_in,
    w_out,
    qkv,
    mixed,
    branch,
    d_resid,
    d_qkv,
    d_mix,
    bias,
    delta_ref,
    probs_ref,
    ds_ref,
    sems,
):
    length, width = branch.shape
    copy = copier(sems)
    get_branch = copy(branch_hbm, branch, 0)
    get_out = copy(w_out_hbm.at[layer], w_out, 1)
    get_mixed = copy(mixed_hbm, mixed, 2)
    get_qkv = copy(qkv_hbm, qkv, 3)
    get_in = copy(w_in_hbm.at[layer], w_in, 4)
    get_resid = copy(resid_hbm, d_resid, 5)
    fill_bias(seg_ref, row_ref[0], bias)
    probs_ref[...] = jnp.zeros_like(probs_ref)
    ds_ref[...] = jnp.zeros_like(ds_ref)
    sums_ref[...] = jnp.zeros_like(sums_ref)
    total = lambda value: jnp.sum(value.astype(F32), 0, keepdims=True)
    head_of = lax.broadcasted_iota(jnp.int32, (16, width), 1) // HEAD
    ones = (head_of == lax.broadcasted_iota(jnp.int32, (16, width), 0)).astype(F32).astype(BF16)
    get_branch.wait()
    get_out.wait()
    d_mix[...] = mm(branch[...], w_out[...], NT).astype(BF16)
    get_mixed.wait()
    product = d_mix[...].astype(F32) * mixed[...].astype(F32)
    high = product.astype(BF16)
    rest = (product - high.astype(F32)).astype(BF16)
    delta_ref[...] = mm(ones, high, NT) + mm(ones, rest, NT)

    get_qkv.wait()
    low_half = lax.broadcasted_iota(jnp.int32, (length, LANES), 1) < HEAD
    low_rows = lax.broadcasted_iota(jnp.int32, (LANES, length), 0) < HEAD

    def pair(number, carry):
        at = pl.multiple_of(number * LANES, LANES)
        cols = pl.ds(at, LANES)
        key_cols = pl.ds(at + width, LANES)
        value_cols = pl.ds(at + 2 * width, LANES)
        queries, keys, values, mix = qkv[:, cols], qkv[:, key_cols], qkv[:, value_cols], d_mix[:, cols]
        keys_t = keys.T
        d_query = jnp.zeros((LANES, length), F32)
        d_keys, d_values = [], []
        zero = jnp.zeros_like(keys)
        for sub in range(2):
            head = 2 * number + sub
            lse = lse_ref[pl.ds(head, 1), :]
            delta = delta_ref[pl.ds(head, 1), :]
            mine = low_half == (sub == 0)
            scores = mm(jnp.where(mine, keys, zero), queries, NT)
            d_probs = mm(jnp.where(mine, values, zero), mix, NT)
            for rows in chunks(length):
                start, stop = window(rows.start, length)
                probs = jnp.exp(
                    scores[rows, start:stop] + bias[rows, start:stop] - lse[:, start:stop]
                )
                probs_ref[sub, rows, start:stop] = probs.astype(BF16)
                ds_ref[sub, rows, start:stop] = (
                    probs * (d_probs[rows, start:stop] - delta[:, start:stop])
                ).astype(BF16)
            d_values.append(mm(probs_ref[sub], mix))
            d_keys.append(mm(ds_ref[sub], queries))
            mine_t = jnp.where(low_rows == (sub == 0), keys_t, jnp.zeros_like(keys_t))
            d_query += mm(mine_t, ds_ref[sub])
        dq = (d_query.T * scale).astype(BF16)
        d_qkv[:, cols] = dq
        sums_ref[1:2, cols] = total(dq)
        d_qkv[:, key_cols] = jnp.where(low_half, d_keys[0], d_keys[1]).astype(BF16)
        dv = jnp.where(low_half, d_values[0], d_values[1]).astype(BF16)
        d_qkv[:, value_cols] = dv
        sums_ref[1:2, key_cols] = total(dv)
        return carry

    lax.fori_loop(0, HEADS * HEAD // LANES, pair, 0)
    put_qkv = copy(d_qkv, d_qkv_hbm, 6)
    get_in.wait()
    get_resid.wait()
    d_x = mm(d_qkv[...], w_in[...], NT)
    for rows in chunks(length):
        d_x_ref[rows, :] = (d_resid[rows, :] + d_x[rows]).astype(BF16)
    put_qkv.wait()


def backward_attention(layer, row, seg, saved1, branch, d_resid, weights, after=()):
    qkv, lse, mixed = saved1[:3]
    w_in, _, w_out = weights[:3]
    ff = weights[6].shape[2]
    length, width = mixed.shape
    outs = (low(length, 3 * width), low(length, width), full(8, ff))
    return call(
        partial(backward_attention_kernel, layer, HEAD**-0.5),
        f"backward_attention{layer}",
        outs,
        (ANY, WHOLE, WHOLE),
        (row, seg, lse, w_in, w_out, qkv, mixed, branch, d_resid),
        [SCALAR, WHOLE, WHOLE] + [ANY] * 6,
        [
            pltpu.VMEM(w_in.shape[1:], BF16),
            pltpu.VMEM(w_out.shape[1:], BF16),
            vm(qkv),
            vm(mixed),
            vm(branch),
            vm(d_resid),
            vm(outs[0]),
            vm(outs[1]),
            pltpu.VMEM((length, length), F32),
            pltpu.VMEM((16, length), F32),
            pltpu.VMEM((2, length, length), BF16),
            pltpu.VMEM((2, length, length), BF16),
            pltpu.SemaphoreType.DMA((7,)),
        ],
        after,
        20 * 10**9,
        16 * 10**6,
    )


def pick_cols_kernel(half_ref, *refs, rows, recv):
    lefts, rights = refs[:rows], refs[rows : 2 * rows]
    out_ref, turned = refs[-2], refs[-1]
    length = lefts[0].shape[0]

    @pl.when(pl.program_id(0) == 0)
    def _():
        for number, left in enumerate(lefts):
            turned[:, number * length : (number + 1) * length] = left[...].T

    found = None
    for number, right in enumerate(rights):
        part = mm(turned[:, number * length : (number + 1) * length], right[...])
        found = part if found is None else found + part
    found = found.reshape(out_ref.shape)
    if recv:
        found = found + refs[2 * rows][...].astype(F32)
    out_ref[...] = found.astype(BF16)


def weight_grad_cols(half, lefts, rights, narrow, recv=None, after=()):
    rows = len(lefts)
    length, width = lefts[0].shape
    cols = rights[0].shape[1] // 2
    tile = next((size for size in (512, 384) if cols % size == 0), cols)
    steps = cols // tile
    out_block = pl.BlockSpec((narrow, width // narrow, tile), lambda j, half: (0, 0, j))
    return pl.pallas_call(
        partial(pick_cols_kernel, rows=rows, recv=recv is not None),
        out_shape=jax.ShapeDtypeStruct((narrow, width // narrow, cols), BF16),
        grid_spec=pltpu.PrefetchScalarGridSpec(
            num_scalar_prefetch=1,
            grid=(steps,),
            in_specs=[pl.BlockSpec((length, width), lambda j, half: (0, 0))] * rows
            + [pl.BlockSpec((length, tile), lambda j, half: (0, half[0] * steps + j))] * rows
            + [out_block] * (recv is not None)
            + [ANY] * len(after),
            out_specs=out_block,
            scratch_shapes=[pltpu.VMEM((width, rows * length), BF16)],
        ),
        compiler_params=pltpu.CompilerParams(vmem_limit_bytes=LIMIT),
        cost_estimate=pl.CostEstimate(
            flops=2 * rows * length * width * cols,
            bytes_accessed=2 * (rows * length * (width + cols) + width * cols),
            transcendentals=0,
        ),
        name="weight_grad_cols",
    )(half, *lefts, *rights, *(() if recv is None else (recv,)), *after)


def pick_rows_kernel(half_ref, *refs, rows, recv):
    lefts, rights = refs[:rows], refs[rows : 2 * rows]
    out_ref = refs[-1]
    unit = out_ref.shape[1]
    width = rights[0].shape[1]
    found = None
    for left, right in zip(lefts, rights):
        part = mm(left[...], right[...], TN)
        found = part if found is None else found + part
    for block in range(out_ref.shape[2] // width):
        cols = slice(block * width, (block + 1) * width)
        part = found[block * unit : (block + 1) * unit]
        if recv:
            part = part + refs[2 * rows][0, :, cols].astype(F32)
        out_ref[0, :, cols] = part.astype(BF16)


def weight_grad_rows(half, lefts, rights, narrow, recv=None, after=()):
    rows = len(lefts)
    length, deep = lefts[0].shape
    width = rights[0].shape[1]
    unit = width // narrow
    part = deep // narrow // 2
    cols = part // unit * width
    out_block = pl.BlockSpec((1, unit, cols), lambda j, half: (j, 0, 0))
    return pl.pallas_call(
        partial(pick_rows_kernel, rows=rows, recv=recv is not None),
        out_shape=jax.ShapeDtypeStruct((narrow, unit, cols), BF16),
        grid_spec=pltpu.PrefetchScalarGridSpec(
            num_scalar_prefetch=1,
            grid=(narrow,),
            in_specs=[pl.BlockSpec((length, part), lambda j, half: (0, 2 * j + half[0]))] * rows
            + [pl.BlockSpec((length, width), lambda j, half: (0, 0))] * rows
            + [out_block] * (recv is not None)
            + [ANY] * len(after),
            out_specs=out_block,
        ),
        compiler_params=pltpu.CompilerParams(vmem_limit_bytes=LIMIT),
        cost_estimate=pl.CostEstimate(
            flops=rows * length * deep * width,
            bytes_accessed=rows * length * (deep + 2 * width) + deep * width,
            transcendentals=0,
        ),
        name="weight_grad_rows",
    )(half, *lefts, *rights, *(() if recv is None else (recv,)), *after)


def swap(value, bit):
    size = lax.axis_size("wide")
    return lax.ppermute(value, "wide", [(i, i ^ bit) for i in range(size)])


def tie(values, on):
    return lax.optimization_barrier((values, on))[0]


def add_low(left, right):
    return (left.astype(F32) + right.astype(F32)).astype(BF16)


def halves(value, side, axis):
    half = value.shape[axis] // 2
    keep = lax.dynamic_slice_in_dim(value, side * half, half, axis)
    give = lax.dynamic_slice_in_dim(value, (1 - side) * half, half, axis)
    return keep, give


def wide_bits():
    return [1 << i for i in range((lax.axis_size("wide") - 1).bit_length())]


def bit_order(turn):
    rest = wide_bits()[1:]
    return rest[::-1] if turn else rest


class Halving:
    def __init__(self, groups):
        self.place = lax.axis_index("wide")
        self.bits = list(zip(*(bit_order(turn) for turn in range(2))))
        self.groups = groups
        self.flying = None

    def step(self, on=None):
        if self.flying is not None:
            if on is not None:
                self.flying = [(keep, tie(recv, on)) for keep, recv in self.flying]
            self.groups = [[add_low(keep, recv)] for keep, recv in self.flying]
            self.flying = None
        if not self.bits:
            return [group[0] for group in self.groups]
        flying, gives = [], []
        for bit, group in zip(self.bits.pop(0), self.groups):
            split = [halves(part, (self.place // bit) % 2, 1) for part in group]
            keep = jnp.concatenate([pair[0] for pair in split], -1)
            give = jnp.concatenate([pair[1] for pair in split], -1)
            gives.append(give)
            flying.append((keep, swap(give, bit)))
        self.flying = flying
        return gives

    def finish(self, on=None):
        mine = self.step(on)
        while self.flying is not None:
            mine = self.step()
        return jnp.concatenate(mine, -1)


def narrow_sum_swaps(mine):
    size = lax.axis_size("narrow")
    place = lax.axis_index("narrow")
    cur = mine.reshape((2,) * (size.bit_length() - 1) + mine.shape[1:])
    depth = size.bit_length() - 1
    for level in range(depth):
        bit = 1 << level
        axis = depth - 1 - level
        keep, give = halves(cur, (place // bit) % 2, axis)
        cur = add_low(
            keep, lax.ppermute(give, "narrow", [(i, i ^ bit) for i in range(size)])
        )
    return cur.reshape(mine.shape[1:])


def wide_gather_swaps(mine):
    place = lax.axis_index("wide")
    cur = mine[None]
    for bit in wide_bits()[::-1]:
        other = swap(cur, bit)
        upper = (place // bit) % 2 == 1
        cur = jnp.stack([jnp.where(upper, other, cur), jnp.where(upper, cur, other)])
        cur = cur.reshape((-1,) + mine.shape)
    return cur


def narrow_sum(mine):
    return lax.psum_scatter(mine, "narrow", scatter_dimension=0, tiled=True)[0]


def small_pack(small, sums, narrow):
    stu = small.shape[1]
    width = small.shape[0] - 2 * stu - 8
    deep = sums.shape[1]
    unit = width // narrow
    proj = small[:width].reshape(narrow, unit, stu)
    split = small[width : width + 2 * stu].reshape(2, narrow, stu // narrow, stu)
    own = small[width + 2 * stu :]
    vectors = [
        sums[1, : 2 * width],
        sums[2, 2 * width : 3 * width],
        sums[1, 2 * width :],
        sums[2, : 2 * width],
        sums[0],
        sums[2, 3 * width :],
    ]
    vectors = [value.reshape(narrow, -1) for value in vectors]
    vectors += [own[i].reshape(narrow, -1) for i in range(3)]
    vectors += [jnp.broadcast_to(own[3], (narrow, stu))]
    rows = [
        jnp.pad(value, ((0, 0), (0, -value.shape[1] % LANES))).reshape(narrow, -1, LANES)
        for value in vectors
    ]
    rest = jnp.concatenate([split[0], split[1]] + rows, 1)
    rest = jnp.pad(rest, ((0, 0), (0, unit - rest.shape[1]), (0, 0)))
    return jnp.stack([proj, rest]).astype(BF16)


def place_kernel(layer, orders, turned, aliased, ff_ref, at_ref, *refs):
    outs, small = refs[aliased : aliased + 4], refs[aliased + 4]
    ai, ao, fi, fo, sems = refs[aliased + 5 :]
    unit, deep = fi.shape
    width = ao.shape[1]
    total, rows, _ = ff_ref.shape
    count = (total - 1).bit_length()
    half_in, half_out = ai.shape[1] // 2, width // 2
    cut = at_ref.shape[2] // 2
    rest = half_in - cut
    blocks = fo.shape[0] // unit // 2

    def put(number, src):
        made = pltpu.make_async_copy(src, outs[number].at[layer], sems.at[number])
        made.start()
        return made

    def starts(place):
        found = []
        for order in orders:
            at = 0
            for bit in order:
                at = 2 * at + (place // bit) % 2
            found.append(at * rows)
        return found

    for place in range(total):
        core = place % 2
        x_at, y_at = starts(place)
        get = lambda start, size: ff_ref[place, :, start : start + size].astype(F32)
        fi[x_at : x_at + rows, core * deep // 2 : (core + 1) * deep // 2] = get(0, deep // 2)
        for block in range(blocks):
            at = (core * blocks + block) * unit + y_at
            fo[at : at + rows, :] = get(deep // 2 + block * width, width)
        ao[y_at : y_at + rows, core * half_out : (core + 1) * half_out] = get(deep, half_out)
    puts = [put(2, fi), put(3, fo), put(1, ao)]
    for place in range(total):
        core = place % 2
        x_at, y_at = starts(place)
        held = place
        if turned:
            held = sum(((place >> i) & 1) << (count - 1 - i) for i in range(count))
        get = lambda start, size: at_ref[held, :, start : start + size].astype(F32)
        start = core * half_in
        ai[x_at : x_at + rows, start : start + cut] = get(0, cut)
        ai[y_at : y_at + rows, start + cut : start + half_in] = get(cut, rest)
        small[y_at : y_at + rows, core * LANES : (core + 1) * LANES] = get(cut + rest, LANES)
    puts.append(put(0, ai))
    for made in puts:
        made.wait()


def place_layer(layer, ff, at, turned, shapes, previous=()):
    unit = shapes[0].shape[1]
    held = len(previous)
    return pl.pallas_call(
        partial(place_kernel, layer, [bit_order(turn) for turn in range(2)], turned, held),
        out_shape=tuple(shapes) + (full(unit, 2 * LANES),),
        in_specs=[WHOLE, WHOLE] + [ANY] * held,
        out_specs=(ANY,) * 4 + (WHOLE,),
        scratch_shapes=[pltpu.VMEM(shape.shape[1:], F32) for shape in shapes]
        + [pltpu.SemaphoreType.DMA((4,))],
        input_output_aliases={2 + i: i for i in range(held)},
        compiler_params=pltpu.CompilerParams(vmem_limit_bytes=LIMIT),
        cost_estimate=pl.CostEstimate(flops=10**6, bytes_accessed=11 * 10**6, transcendentals=0),
        name=f"place_layer{layer}",
    )(ff, at, *previous)


def place_small_kernel(first_ref, second_ref, proj_ref, dense_ref, cls_ref, *vec_refs):
    for layer, ref in enumerate((first_ref, second_ref)):
        stu = dense_ref.shape[1]
        proj_ref[layer] = ref[:, :LANES]
        dense_ref[layer] = ref[:stu, LANES:]
        cls_ref[layer] = ref[stu : 2 * stu, LANES : LANES + cls_ref.shape[2]]
        row = 2 * stu
        for out in vec_refs:
            size = out.shape[1]
            for start in range(0, size, LANES):
                part = min(LANES, size - start)
                out[layer : layer + 1, start : start + part] = ref[
                    row : row + 1, LANES : LANES + part
                ]
                row += 1


def place_small(first, second, width, deep, classes, narrow):
    sizes = [2 * width, width, 2 * width, 2 * width, deep, width, LANES, LANES, LANES]
    stu = LANES // narrow
    outs = (
        full(2, width // narrow, LANES),
        full(2, stu, LANES),
        full(2, stu, classes),
    ) + tuple(full(2, size // narrow) for size in sizes)
    return pl.pallas_call(
        place_small_kernel,
        out_shape=outs + (full(2, classes),),
        in_specs=[WHOLE, WHOLE],
        out_specs=(WHOLE,) * 13,
        name="place_small",
    )(first, second)


def route_kernel(me_ref, *refs):
    around, out_ref, held = refs[:-2], refs[-2], refs[-1]
    me, size = me_ref[0], len(around)
    for step, ref in enumerate(around):
        held[lax.rem(me + (size - step), size)] = ref[0]
    counts = [held[i] for i in range(size)]
    flow, before = [], []
    total = jnp.int32(0)
    for value in counts:
        before.append(total)
        total = total + value - 1
        flow.append(total)
    right1 = [(f >= 1) & (c >= 1) for f, c in zip(flow, counts)]
    left1 = [(f <= -1) & (c >= 1) for f, c in zip(before, counts)]
    right2 = [(f >= 1) & ((f >= 2) | (c == 0)) for f, c in zip(flow, counts)]
    left2 = [(f <= -1) & ((f <= -2) | (c == 0)) for f, c in zip(before, counts)]

    def at(values, shift):
        found = jnp.int32(0)
        for i, value in enumerate(values):
            found = jnp.where(me + shift == i, value.astype(jnp.int32), found)
        return found

    count = at(counts, 0)
    from_left2, from_right2 = at(right2, -1), at(left2, 1)
    sent_right, sent_left = at(right1, 0), at(left1, 0)
    results = (
        at(right1, -1),
        from_left2,
        from_left2 | from_right2,
        (count == 2).astype(jnp.int32),
        ((count == 1) & (sent_right + sent_left == 0)).astype(jnp.int32),
        at(right2, 0),
        sent_left,
        (sent_right & at(right2, 1)) | (sent_left & at(left2, -1)),
        (count >= 1).astype(jnp.int32),
        (count >= 2).astype(jnp.int32),
    )
    for i, value in enumerate(results):
        out_ref[i] = value
    for i in range(len(results), out_ref.shape[0]):
        out_ref[i] = 0


def route(me, around):
    return pl.pallas_call(
        route_kernel,
        out_shape=jax.ShapeDtypeStruct((16,), jnp.int32),
        in_specs=[SCALAR] * (1 + len(around)),
        out_specs=SCALAR,
        scratch_shapes=[pltpu.SMEM((len(around),), jnp.int32)],
        name="route",
    )(me, *around)


def shards(
    tokens,
    segments,
    exit_layer,
    attn_in,
    qv_bias,
    attn_out,
    out_bias,
    ln_gain,
    ln_bias,
    ff_in,
    ff_in_bias,
    ff_out,
    ff_out_bias,
    stu_proj,
    stu_bias,
    pool_query,
    stu_dense,
    stu_dense_bias,
    stu_cls,
    stu_cls_bias,
    out_cot,
    logit_cot,
):
    row_count, length, width = tokens.shape
    classes = stu_cls.shape[-1]
    blank = LANES - classes
    narrow = lax.axis_size("narrow")
    me = lax.axis_index("narrow")
    core = lax.axis_index("wide") % 2
    weights = (
        attn_in,
        qv_bias,
        attn_out,
        out_bias,
        ln_gain,
        ln_bias,
        ff_in,
        ff_in_bias,
        ff_out,
        ff_out_bias,
        stu_proj,
        stu_bias,
        pool_query,
        stu_dense,
        stu_dense_bias,
        jnp.pad(stu_cls, ((0, 0), (0, 0), (0, blank))),
        jnp.pad(stu_cls_bias, ((0, 0), (0, blank))),
    )
    wide_cot = jnp.pad(logit_cot.astype(F32), ((0, 0), (0, 0), (0, blank)))

    alive = exit_layer == 1
    mine = jnp.sum(alive.astype(jnp.int32)).reshape(1)
    around = [mine] + [
        lax.ppermute(mine, "narrow", [(i, (i + step) % narrow) for i in range(narrow)])
        for step in range(1, narrow)
    ]
    flags = route(me.reshape(1), around)
    from_left1, from_left2, use_two, use_b, use_a, on_right, sent_left, is_far, a_alive, b_alive = (
        flags[i] == 1 for i in range(10)
    )
    row_a = jnp.where(alive[0], 0, jnp.where(alive[1], 1, 0)).astype(jnp.int32)
    row_b = 1 - row_a

    even = me % 2 == 0
    inner = [(i, i ^ 1) for i in range(narrow)]
    outer = []
    for i in range(lax.axis_size("wide") * narrow):
        place, line = i // narrow, i % narrow
        other = ((line + 1) ^ 1) - 1
        inside = 0 <= other < narrow
        outer.append((i, place * narrow + other if inside else (place ^ 1) * narrow + line))

    def shift(value):
        return (
            lax.ppermute(value, "narrow", inner),
            lax.ppermute(value, ("wide", "narrow"), outer),
        )

    def pick(pair, is_left):
        return jnp.where(is_left == even, pair[1], pair[0])

    def out_one(pair):
        return pick(pair, from_left1)

    def out_two(pair, one, own_a, own_b):
        two = pick(pair, from_left2)
        return jnp.where(use_b, own_b, jnp.where(use_a, own_a, jnp.where(use_two, two, one)))

    def back_one(pair):
        return pick(pair, ~on_right)

    def back_two(value, pair, pair2):
        return jnp.where(
            use_a, value, jnp.where(is_far, pick(pair2, sent_left), pick(pair, sent_left))
        )

    def row_of(value, row):
        return lax.dynamic_index_in_dim(value, row, 0, False)

    def cot_pack(row):
        tail = jnp.zeros((16, width), BF16)
        tail = tail.at[0, :length].set(row_of(segments, row).astype(BF16))
        tail = tail.at[1, :classes].set(row_of(logit_cot[:, 1], row))
        return jnp.concatenate([row_of(out_cot, row), tail], 0)

    index = lambda row: row.reshape(1)
    first_row = jnp.zeros((1,), jnp.int32)
    own, other = index(core), index(1 - core)
    ia, ib = index(row_a), index(row_b)
    early_cot = wide_cot[:, 0]

    pack_a, pack_b = cot_pack(row_a), cot_pack(row_b)
    pair = shift(pack_a)
    a1 = forward_attention(0, ia, tokens, segments, weights, (pack_a,))
    pack_one = out_one(tie(pair, a1[4]))
    pair = shift(pack_one)
    a2 = forward_ff(0, ia, a1[4], a1[5], early_cot, weights, (pack_one,))
    work_pack = out_two(tie(pair, a2[3]), pack_one, pack_a, pack_b)
    pair = shift(a2[3])
    b1 = forward_attention(0, ib, tokens, segments, weights, (a2[3], work_pack))
    one = out_one(tie(pair, b1[4]))
    pair = shift(one)
    b2 = forward_ff(0, ib, b1[4], b1[5], early_cot, weights, (one,))
    work_in = out_two(tie(pair, b2[3]), one, a2[3], b2[3])
    work_seg = work_pack[length : length + 1, :length].astype(jnp.int32)
    work_cot = work_pack[length + 1 : length + 2, :LANES].astype(F32)

    w1 = forward_attention(1, first_row, work_in[None], work_seg, weights)
    w2 = forward_ff(1, first_row, w1[4], w1[5], work_cot, weights)
    sent_h = jnp.concatenate(
        [w2[3], jnp.pad(w2[6], ((0, 8), (0, width - LANES))).astype(BF16)], 0
    )
    pair_h = shift(sent_h)
    w3 = backward_ff(1, work_pack[:length], w1, w2, weights, (sent_h,))

    def ff_jobs(saved1, saved2, back):
        first = [s[4] for s in saved1]
        mixed = [s[2] for s in saved1]
        active = [s[1] for s in saved2]
        second, inner, branch = ([b[i] for b in back] for i in range(3))
        return (
            (weight_grad_cols, first, inner),
            (weight_grad_rows, active, second),
            (weight_grad_cols, mixed, branch),
        )

    def give_half(jobs, after=()):
        return [job(other, lefts, rights, narrow, None, after) for job, lefts, rights in jobs]

    def own_half(jobs, sent, after=()):
        return [
            job(own, lefts, rights, narrow, swap(value, 1), after)
            for (job, lefts, rights), value in zip(jobs, sent)
        ]

    def ff_halving(parts):
        return Halving([[parts[0]], [parts[1], parts[2]]])

    def attn_halving(part, small):
        keep, give = halves(small, core, 0)
        small = add_low(keep, swap(give, 1))[0]
        cut = (part.shape[-1] + LANES) // 2
        return Halving([[part[..., :cut]], [part[..., cut:], small]])

    jobs = ff_jobs([w1], [w2], [w3])
    forth_h = back_one(tie(pair_h, w3[2]))
    pair_h2 = shift(forth_h)
    sent = give_half(jobs, (forth_h,))
    w4 = backward_attention(1, first_row, work_seg, w1, w3[2], w3[3], weights, tuple(sent))
    pair_x = shift(w4[1])
    parts = own_half(jobs, sent, (w4[1],))
    ff1 = ff_halving(parts)
    flying = ff1.step()
    jobs1 = ((weight_grad_cols, [work_in], [w4[0]]),)
    sent1 = give_half(jobs1, tuple(flying))
    forth_x = back_one(tie(pair_x, sent1[0]))
    pair_x2 = shift(forth_x)
    far_h = back_two(sent_h, pair_h, tie(pair_h2, w4[1]))

    base_b = jnp.where(b_alive, w4[1], row_of(out_cot, row_b))
    b3 = backward_ff(0, base_b, b1, b2, weights, (*sent1, forth_x, far_h))
    far_x = back_two(w4[1], pair_x, tie(pair_x2, b3[2]))
    part1 = own_half(jobs1, sent1, (b3[0],))[0]
    at1 = attn_halving(part1, small_pack(w2[7], w3[4] + w4[2], narrow))
    flying = at1.step() + ff1.step(b3[2])
    base_a = jnp.where(a_alive, far_x, row_of(out_cot, row_a))
    a3 = backward_ff(0, base_a, a1, a2, weights, tuple(flying))
    mine_ff1 = ff1.finish(a3[2])
    flying = at1.step(a3[2])
    jobs = ff_jobs([a1, b1], [a2, b2], [a3, b3])
    sent = give_half(jobs, (mine_ff1, *flying))
    sum_ff1 = narrow_sum(mine_ff1)
    ff0 = ff_halving(own_half(jobs, sent))
    flying = ff0.step()
    mine_at1 = at1.finish(flying[0])
    b4 = backward_attention(
        0, ib, segments, b1, b3[2], b3[3], weights, (*flying, sum_ff1, mine_at1)
    )
    every = lambda value: lax.all_gather(value, "wide", axis=0, tiled=False)
    sum_at1 = narrow_sum(mine_at1)
    all_ff1 = every(sum_ff1)
    a4 = backward_attention(
        0, ia, segments, a1, a3[2], a3[3], weights, (b4[1],)
    )
    flying = ff0.step(a4[1])
    jobs0 = (
        (
            weight_grad_cols,
            [row_of(tokens, row_a), row_of(tokens, row_b)],
            [a4[0], b4[0]],
        ),
    )
    sent0 = give_half(jobs0, tuple(flying))
    part0 = own_half(jobs0, sent0, (all_ff1, sum_at1))[0]
    at0 = attn_halving(
        part0, small_pack(a2[7] + b2[7], a3[4] + b3[4] + a4[2] + b4[2], narrow)
    )
    flying = at0.step()
    sum_ff0 = narrow_sum(ff0.finish(flying[0]))
    all_at0 = wide_gather_swaps(narrow_sum_swaps(at0.finish()))

    deep = ff_in.shape[2]
    shapes = [
        full(2, width // narrow, 3 * width),
        full(2, width // narrow, width),
        full(2, width // narrow, deep),
        full(2, deep // narrow, width),
    ]
    *large, small1 = place_layer(1, all_ff1, wide_gather_swaps(tie(sum_at1, part0)), True, shapes)
    *large, small0 = place_layer(0, every(sum_ff0), all_at0, True, shapes, large)
    (d_proj, d_dense, d_cls, d_qv, d_out_b, d_gain, d_shift, d_fi_b, d_fo_b, *rest) = place_small(
        small0, small1, width, deep, classes, narrow
    )
    d_stu_b, d_query, d_dense_b, d_cls_b = rest
    totals = (
        large[0],
        d_qv,
        large[1],
        d_out_b,
        d_gain,
        d_shift,
        large[2],
        d_fi_b,
        large[3],
        d_fo_b,
        d_proj,
        d_stu_b,
        d_query,
        d_dense,
        d_dense_b,
        d_cls,
        d_cls_b,
    )

    in_order = lambda for_a, for_b: jnp.where(
        row_a == 0, jnp.stack([for_a, for_b]), jnp.stack([for_b, for_a])
    )
    act_a = jnp.where(a_alive, far_h[:length], a2[3])
    act_b = jnp.where(b_alive, w2[3], b2[3])
    logit_a = jnp.where(a_alive, far_h[length, :classes], jnp.zeros((classes,), BF16))
    logit_b = jnp.where(b_alive, w2[6][0, :classes].astype(BF16), jnp.zeros((classes,), BF16))
    early = in_order(a2[6][0, :classes], b2[6][0, :classes]).astype(BF16)
    logits = jnp.stack([early, in_order(logit_a, logit_b)], 1)
    return (in_order(act_a, act_b), logits, in_order(a4[1], b4[1])) + totals


def solution(mesh):
    rows = ("wide", "narrow")
    return jax.shard_map(
        shards,
        mesh=mesh,
        in_specs=(P(rows, None, None), P(rows, None), P(rows))
        + (P(),) * 17
        + (P(rows, None, None), P(rows, None, None)),
        out_specs=(P(rows, None, None),) * 3
        + (
            P(None, "narrow", None),
            P(None, "narrow"),
            P(None, "narrow", None),
            P(None, "narrow"),
            P(None, "narrow"),
            P(None, "narrow"),
            P(None, "narrow", None),
            P(None, "narrow"),
            P(None, "narrow", None),
            P(None, "narrow"),
            P(None, "narrow", None),
            P(None, "narrow"),
            P(None, "narrow"),
            P(None, "narrow", None),
            P(None, "narrow"),
            P(None, "narrow", None),
            P(),
        ),
        check_vma=False,
    )
```

```python
from functools import partial

import jax
import jax.numpy as jnp
import numpy as np
from jax import lax
from jax.experimental import pallas as pl
from jax.experimental.pallas import tpu as pltpu
from jax.sharding import PartitionSpec as P

HEADS = 12
HEAD = 64
STU_HEADS = 2
LANES = 128
CHUNK = 128
REACH = 256
EPS = 1e-12
MASKED = -1e30
SEGMENTS = 4
HIGH = lax.Precision.HIGHEST
F32 = jnp.float32
BF16 = jnp.bfloat16
LIMIT = 52 * 1024 * 1024
BRIEF = pl.CostEstimate(flops=10**6, bytes_accessed=10**5, transcendentals=0)

NN = (((1,), (0,)), ((), ()))
NT = (((1,), (1,)), ((), ()))
TN = (((0,), (0,)), ((), ()))


def mm(left, right, dims=NN):
    return lax.dot_general(left, right, dims, preferred_element_type=F32)


def mm_high(left, right, dims=NN):
    return lax.dot_general(left, right, dims, precision=HIGH, preferred_element_type=F32)


def vec(ref, layer, start, size):
    return ref[...].astype(F32)[layer : layer + 1, start : start + size]


def gelu_pair(value):
    dist = jnp.abs(value) * (0.5**0.5)
    den = 1.0 + 0.3275911 * dist
    part = pl.reciprocal(den, approx=True)
    part = part * (2.0 - den * part)
    series = 0.5 * 1.061405429
    for term in (-1.453152027, 1.421413741, -0.284496736, 0.254829592):
        series = series * part + 0.5 * term
    bell = jnp.exp(-(dist * dist))
    tail = series * part * bell
    below = jnp.where(value >= 0, 1.0 - tail, tail)
    return value * below, below + value * bell * ((2.0 * np.pi) ** -0.5)


def row_norm(value):
    mean = jnp.mean(value, -1, keepdims=True)
    centered = value - mean
    spread = lax.rsqrt(jnp.mean(centered * centered, -1, keepdims=True) + EPS)
    return centered * spread, spread


def norm_back(grad, hat, spread, gain):
    scaled = grad * gain
    low = jnp.mean(scaled, -1, keepdims=True)
    high = jnp.mean(scaled * hat, -1, keepdims=True)
    return spread * (scaled - low - hat * high)


def window(place, length):
    start = max(0, (place - REACH + 1) // CHUNK * CHUNK)
    stop = min(length, -(-(place + CHUNK + REACH - 1) // CHUNK) * CHUNK)
    return start, stop


def fill_codes(seg_ref, row, code_q, code_k):
    length = code_q.shape[0]
    seg_row = seg_ref[pl.ds(row, 1), :].astype(F32)
    seg_cols = jnp.broadcast_to(seg_row, (LANES, length)).T
    lane = lax.broadcasted_iota(jnp.int32, (length, LANES), 1) % HEAD
    same = seg_cols == lane.astype(F32)
    code_q[...] = jnp.where(same, 1.0, 0.0).astype(BF16)
    code_k[...] = jnp.where(same | (lane >= SEGMENTS), 0.0, MASKED).astype(BF16)


ANY = pl.BlockSpec(memory_space=pl.ANY)
WHOLE = pl.BlockSpec(memory_space=pltpu.VMEM)
SCALAR = pl.BlockSpec(memory_space=pltpu.SMEM)


def low(*shape):
    return jax.ShapeDtypeStruct(shape, BF16)


def full(*shape):
    return jax.ShapeDtypeStruct(shape, F32)


def vm(like):
    return pltpu.VMEM(like.shape, like.dtype)


def call(kernel, name, outs, out_specs, inputs, in_specs, scratch, after, flops, moved):
    count, extra = len(inputs), len(after)

    def body(*refs):
        kernel(*refs[:count], *refs[count + extra :])

    return pl.pallas_call(
        body,
        out_shape=outs,
        in_specs=list(in_specs) + [ANY] * extra,
        out_specs=out_specs,
        scratch_shapes=scratch,
        compiler_params=pltpu.CompilerParams(vmem_limit_bytes=LIMIT),
        cost_estimate=pl.CostEstimate(flops=flops, bytes_accessed=moved, transcendentals=0),
        name=name,
    )(*inputs, *after)


def copier(sems):
    def copy(src, dst, number):
        made = pltpu.make_async_copy(src, dst, sems.at[number])
        made.start()
        return made

    return copy


def chunks(length):
    return [slice(place, place + CHUNK) for place in range(0, length, CHUNK)]


def forward_attention_kernel(
    layer,
    scale,
    row_ref,
    x_hbm,
    seg_ref,
    w_in_hbm,
    w_out_hbm,
    qv_ref,
    out_b_ref,
    gain_ref,
    shift_ref,
    qkv_hbm,
    lse_ref,
    mixed_hbm,
    hat_hbm,
    first_hbm,
    full_hbm,
    spread_ref,
    x_ref,
    w_in,
    w_out,
    qkv,
    mixed,
    hat,
    first,
    full,
    code_q,
    code_k,
    terms_ref,
    sems,
):
    row = row_ref[0]
    length, width = x_ref.shape
    copy = copier(sems)
    get_x = copy(x_hbm.at[row, pl.ds(0, length)], x_ref, 0)
    get_in = copy(w_in_hbm.at[layer], w_in, 1)
    get_out = copy(w_out_hbm.at[layer], w_out, 2)
    fill_codes(seg_ref, row, code_q, code_k)
    terms_ref[...] = jnp.zeros_like(terms_ref)
    lse_ref[...] = jnp.zeros_like(lse_ref)
    get_x.wait()
    get_in.wait()

    x = x_ref[...]
    qkv[:, :width] = (
        (mm(x, w_in[:, :width]) + vec(qv_ref, layer, 0, width)).astype(BF16).astype(F32) * scale
    ).astype(BF16)
    qkv[:, width : 2 * width] = mm(x, w_in[:, width : 2 * width]).astype(BF16)
    qkv[:, 2 * width :] = (
        mm(x, w_in[:, 2 * width :]) + vec(qv_ref, layer, width, width)
    ).astype(BF16)
    put_qkv = copy(qkv, qkv_hbm, 3)

    low_half = lax.broadcasted_iota(jnp.int32, (length, LANES), 1) < HEAD
    low_rows = lax.broadcasted_iota(jnp.int32, (LANES, length), 0) < HEAD

    def pair(number, carry):
        at = pl.multiple_of(number * LANES, LANES)
        queries = qkv[:, pl.ds(at, LANES)]
        keys = qkv[:, pl.ds(at + width, LANES)]
        values_t = qkv[:, pl.ds(at + 2 * width, LANES)].T
        outs = []
        for sub in range(2):
            mine = low_half == (sub == 0)
            scores = mm(
                jnp.where(mine, keys, code_k[...]), jnp.where(mine, queries, code_q[...]), NT
            )
            tops = []
            for cols in chunks(length):
                start, stop = window(cols.start, length)
                part = scores[start:stop, cols]
                top = jnp.max(part, 0, keepdims=True)
                terms_ref[sub, start:stop, cols] = jnp.exp(part - top).astype(BF16)
                tops.append(top)
            mine_t = jnp.where(low_rows == (sub == 0), values_t, jnp.ones_like(values_t))
            product = mm(mine_t, terms_ref[sub])
            beside = HEAD * (1 - sub)
            total = product[beside : beside + 1, :]
            lse_ref[pl.ds(2 * number + sub, 1), :] = jnp.concatenate(tops, 1) + jnp.log(total)
            outs.append(product * (1.0 / total))
        mixed[:, pl.ds(at, LANES)] = jnp.where(low_rows, outs[0], outs[1]).T.astype(BF16)
        return carry

    lax.fori_loop(0, HEADS * HEAD // LANES, pair, 0)
    put_mixed = copy(mixed, mixed_hbm, 4)

    get_out.wait()
    gain, shift = vec(gain_ref, layer, 0, width), vec(shift_ref, layer, 0, width)
    out_b = vec(out_b_ref, layer, 0, width)
    branch = mm(mixed[...], w_out[...])
    for rows in chunks(length):
        normed, spread = row_norm(x_ref[rows, :].astype(F32) + branch[rows] + out_b)
        hat[rows, :] = normed.astype(BF16)
        normed = normed * gain + shift
        full[rows, :] = normed
        first[rows, :] = normed.astype(BF16)
        spread_ref[rows, :] = jnp.broadcast_to(spread, (CHUNK, LANES))
    puts = (copy(hat, hat_hbm, 5), copy(first, first_hbm, 6), copy(full, full_hbm, 7))
    for made in (put_qkv, put_mixed) + puts:
        made.wait()


def forward_attention(layer, row, x, seg, weights, after=()):
    w_in, qv, w_out, out_b, gain, shift = weights[:6]
    length, width = seg.shape[-1], x.shape[-1]
    outs = (
        low(length, 3 * width),
        full(16, length),
        low(length, width),
        low(length, width),
        low(length, width),
        full(length, width),
        full(length, LANES),
    )
    return call(
        partial(forward_attention_kernel, layer, HEAD**-0.5),
        f"forward_attention{layer}",
        outs,
        (ANY, WHOLE) + (ANY,) * 4 + (WHOLE,),
        (row, x, seg, w_in, w_out, qv, out_b, gain, shift),
        [SCALAR, ANY, WHOLE, ANY, ANY] + [WHOLE] * 4,
        [
            pltpu.VMEM((length, width), BF16),
            pltpu.VMEM(w_in.shape[1:], BF16),
            pltpu.VMEM(w_out.shape[1:], BF16),
            vm(outs[0]),
            vm(outs[2]),
            vm(outs[3]),
            vm(outs[4]),
            vm(outs[5]),
            pltpu.VMEM((length, LANES), BF16),
            pltpu.VMEM((length, LANES), BF16),
            pltpu.VMEM((2, length, length), BF16),
            pltpu.SemaphoreType.DMA((8,)),
        ],
        after,
        14 * 10**9,
        16 * 10**6,
    )


def forward_ff_kernel(
    layer,
    row_ref,
    first_hbm,
    full_hbm,
    cot_ref,
    seg_ref,
    later_ref,
    w_fi_hbm,
    w_fo_hbm,
    gain_ref,
    shift_ref,
    fi_b_ref,
    fo_b_ref,
    proj_ref,
    proj_b_ref,
    query_ref,
    dense_ref,
    dense_b_ref,
    cls_ref,
    cls_b_ref,
    slope_hbm,
    active_hbm,
    hat_hbm,
    h_hbm,
    spread_ref,
    d_upper_ref,
    small_ref,
    first,
    full,
    w_fi,
    w_fo,
    slope,
    active,
    hat,
    h,
    even,
    odd,
    sems,
):
    length, width = first.shape
    ff = w_fi.shape[1]
    copy = copier(sems)
    get_first = copy(first_hbm, first, 0)
    part = even.shape[1]
    get_fi = [
        copy(w_fi_hbm.at[layer, :, pl.ds(at, part)], w_fi.at[:, pl.ds(at, part)], 8 + at // part)
        for at in range(0, ff, part)
    ]
    get_full = copy(full_hbm, full, 2)
    get_fo = copy(w_fo_hbm.at[layer], w_fo, 3)
    get_first.wait()
    get_fi[0].wait()

    def multiply(at, into):
        into[...] = mm(first[...], w_fi[:, pl.ds(at, part)])

    def bend(at, source):
        bias_part = fi_b_ref[:, pl.ds(at, part)].astype(F32)[layer : layer + 1]
        for rows in chunks(length):
            out, grad = gelu_pair(source[rows, :] + bias_part)
            active[rows, pl.ds(at, part)] = out.astype(BF16)
            slope[rows, pl.ds(at, part)] = grad.astype(BF16)

    multiply(0, even)
    for made in get_fi[1:]:
        made.wait()
    steps = ff // part // 2

    def inner(number, carry):
        at = pl.multiple_of(number * (2 * part), 2 * part)
        multiply(at + part, odd)
        bend(at, even)
        later = pl.multiple_of(jnp.minimum(at + 2 * part, ff - part), part)
        multiply(later, even)
        bend(at + part, odd)
        return carry

    lax.fori_loop(0, steps, inner, 0)
    put_slope = copy(slope, slope_hbm, 4)
    put_active = copy(active, active_hbm, 5)

    get_fo.wait()
    get_full.wait()
    gain, shift = vec(gain_ref, layer, width, width), vec(shift_ref, layer, width, width)
    fo_b = vec(fo_b_ref, layer, 0, width)
    second = mm(active[...], w_fo[...])
    for rows in chunks(length):
        normed, spread = row_norm(full[rows, :] + second[rows] + fo_b)
        hat[rows, :] = normed.astype(BF16)
        h[rows, :] = (normed * gain + shift).astype(BF16)
        spread_ref[rows, :] = jnp.broadcast_to(spread, (CHUNK, LANES))
    put_hat = copy(hat, hat_hbm, 6)

    stu_width = proj_ref.shape[2]
    stu_scale = (stu_width // STU_HEADS) ** -0.5
    hidden = h[:length, :]
    upper = mm(hidden, proj_ref[layer]) + vec(proj_b_ref, layer, 0, stu_width)
    query = vec(query_ref, layer, 0, stu_width)
    lane_full = lax.broadcasted_iota(jnp.int32, (length, stu_width), 1)
    left = lane_full < stu_width // STU_HEADS

    def both(value):
        zero = jnp.zeros_like(value)
        return (
            jnp.sum(jnp.where(left, value, zero), -1, keepdims=True),
            jnp.sum(jnp.where(left, zero, value), -1, keepdims=True),
        )

    weights = []
    for score in both(upper * query):
        score = score * stu_scale
        terms = jnp.exp(score - jnp.max(score, 0, keepdims=True))
        weights.append(terms / jnp.sum(terms, 0, keepdims=True))
    weight = jnp.where(left, weights[0], weights[1])
    pooled = jnp.sum(weight * upper, 0, keepdims=True)
    dense = dense_ref[layer].astype(F32)
    cls = cls_ref[layer].astype(F32)
    eight = (8, stu_width)
    z = jnp.tanh(
        mm_high(jnp.broadcast_to(pooled, eight), dense) + vec(dense_b_ref, layer, 0, stu_width)
    )
    logits = mm_high(z, cls) + vec(cls_b_ref, layer, 0, LANES)
    below = lax.broadcasted_iota(jnp.int32, (16, length), 0)
    segments = jnp.broadcast_to(seg_ref[pl.ds(row_ref[0], 1), :].astype(F32), (16, length))
    later = jnp.broadcast_to(later_ref[pl.ds(row_ref[0], 1), :], (16, LANES))
    tail = jnp.where(below == 1, segments, 0.0)
    narrow_tail = jnp.where(below[:, :LANES] == 2, later, tail[:, :LANES])
    narrow_tail = jnp.where(below[:, :LANES] == 0, jnp.concatenate([logits, logits], 0), narrow_tail)
    h[length:, :LANES] = narrow_tail.astype(BF16)
    h[length:, LANES:length] = tail[:, LANES:].astype(BF16)
    h[length:, length:] = jnp.zeros((16, width - length), BF16)
    put_h = copy(h, h_hbm, 7)
    cot = cot_ref[pl.ds(row_ref[0], 1), :]
    d_pre = mm_high(jnp.broadcast_to(cot, (8, LANES)), cls, NT) * (1.0 - z * z)
    d_pooled = mm_high(d_pre, dense, NT)[:1]
    d_pre = d_pre[:1]

    def column(value):
        return jnp.broadcast_to(value, (value.shape[1], value.shape[1])).T

    d_scores = []
    for weight_col, d_weight in zip(weights, both(upper * d_pooled)):
        mean = jnp.sum(weight_col * d_weight, 0, keepdims=True)
        d_scores.append(weight_col * (d_weight - mean) * stu_scale)
    d_score = jnp.where(left, d_scores[0], d_scores[1])
    d_upper = (weight * d_pooled + d_score * query).astype(BF16)
    d_upper_ref[...] = d_upper
    small_ref[:width, :] = mm(hidden, d_upper, TN)
    small_ref[width : width + stu_width, :] = column(pooled) * d_pre
    small_ref[width + stu_width : width + 2 * stu_width, :] = column(z[:1]) * cot
    base = width + 2 * stu_width
    small_ref[base : base + 1, :] = jnp.sum(d_upper.astype(F32), 0, keepdims=True)
    small_ref[base + 1 : base + 2, :] = jnp.sum(d_score * upper, 0, keepdims=True)
    small_ref[base + 2 : base + 3, :] = d_pre
    small_ref[base + 3 : base + 4, :] = cot
    small_ref[base + 4 :, :] = jnp.zeros((4, LANES), F32)

    for made in (put_slope, put_active, put_hat, put_h):
        made.wait()


def forward_ff(layer, row, first, first_full, cot, seg, later, weights, after=()):
    gain, shift, w_fi, fi_b, w_fo, fo_b = weights[4:10]
    length, width = first.shape
    ff = w_fi.shape[2]
    stu = weights[10].shape[2]
    outs = (
        low(length, ff),
        low(length, ff),
        low(length, width),
        low(length + 16, width),
        full(length, LANES),
        low(length, stu),
        full(width + 2 * stu + 8, LANES),
    )
    return call(
        partial(forward_ff_kernel, layer),
        f"forward_ff{layer}",
        outs,
        (ANY,) * 4 + (WHOLE,) * 3,
        (row, first, first_full, cot, seg, later, w_fi, w_fo, gain, shift, fi_b, fo_b)
        + tuple(weights[10:]),
        [SCALAR, ANY, ANY, WHOLE, WHOLE, WHOLE, ANY, ANY] + [WHOLE] * 11,
        [
            pltpu.VMEM((length, width), BF16),
            pltpu.VMEM((length, width), F32),
            pltpu.VMEM(w_fi.shape[1:], BF16),
            pltpu.VMEM(w_fo.shape[1:], BF16),
            vm(outs[0]),
            vm(outs[1]),
            vm(outs[2]),
            vm(outs[3]),
            pltpu.VMEM((length, 512), F32),
            pltpu.VMEM((length, 512), F32),
            pltpu.SemaphoreType.DMA((8 + ff // 512,)),
        ],
        after,
        18 * 10**9,
        20 * 10**6,
    )


def backward_ff_kernel(
    layer,
    grad_ref,
    d_upper_ref,
    spread1_ref,
    spread2_ref,
    proj_ref,
    gain_ref,
    w_fi_hbm,
    w_fo_hbm,
    hat1_hbm,
    slope_hbm,
    hat2_hbm,
    second_hbm,
    inner_hbm,
    branch_hbm,
    resid_hbm,
    sums_ref,
    w_fi,
    w_fo,
    hat1,
    slope,
    hat2,
    second,
    inner,
    branch,
    d_resid,
    sems,
):
    length, width = grad_ref.shape
    ff = w_fi.shape[1]
    copy = copier(sems)
    get_hat2 = copy(hat2_hbm, hat2, 0)
    get_fo = copy(w_fo_hbm.at[layer], w_fo, 1)
    get_slope = copy(slope_hbm, slope, 2)
    get_fi = copy(w_fi_hbm.at[layer], w_fi, 3)
    get_hat1 = copy(hat1_hbm, hat1, 4)
    sums_ref[...] = jnp.zeros_like(sums_ref)
    get_hat2.wait()
    gain1, gain2 = vec(gain_ref, layer, 0, width), vec(gain_ref, layer, width, width)
    total = lambda value: jnp.sum(value.astype(F32), 0, keepdims=True)

    def through_norm(grads, hat_ref, spread_ref, gain, out_ref):
        d_gain = jnp.zeros((1, width), F32)
        d_shift = jnp.zeros((1, width), F32)
        d_bias = jnp.zeros((1, width), F32)
        for rows in chunks(length):
            grad = grads(rows)
            hat = hat_ref[rows, :].astype(F32)
            d_gain += total(grad * hat)
            d_shift += total(grad)
            moved = norm_back(grad, hat, spread_ref[rows, 0:1], gain)
            d_resid[rows, :] = moved
            out_ref[rows, :] = moved.astype(BF16)
            d_bias += total(moved.astype(BF16))
        return d_gain, d_shift, d_bias

    from_student = mm(d_upper_ref[...], proj_ref[layer], NT)
    d_gain, d_shift, d_bias = through_norm(
        lambda rows: grad_ref[rows, :].astype(F32) + from_student[rows],
        hat2,
        spread2_ref,
        gain2,
        second,
    )
    sums_ref[1:2, 3 * width : 4 * width] = d_gain
    sums_ref[2:3, width : 2 * width] = d_shift
    sums_ref[2:3, 3 * width : 4 * width] = d_bias
    put_second = copy(second, second_hbm, 5)

    get_fo.wait()
    get_slope.wait()
    part = 512

    def ff_part(number, carry):
        at = pl.multiple_of(number * part, part)
        column = jnp.zeros((1, part), F32)
        d_active = mm(second[...], w_fo[pl.ds(at, part), :], NT)
        for rows in chunks(length):
            d_inner = (d_active[rows] * slope[rows, pl.ds(at, part)].astype(F32)).astype(BF16)
            inner[rows, pl.ds(at, part)] = d_inner
            column += total(d_inner)
        sums_ref[0:1, pl.ds(at, part)] = column
        return carry

    lax.fori_loop(0, ff // part, ff_part, 0)
    put_inner = copy(inner, inner_hbm, 6)

    get_fi.wait()
    get_hat1.wait()
    d_first = mm(inner[...], w_fi[...], NT)
    d_gain, d_shift, d_bias = through_norm(
        lambda rows: d_resid[rows, :] + d_first[rows], hat1, spread1_ref, gain1, branch
    )
    sums_ref[1:2, 2 * width : 3 * width] = d_gain
    sums_ref[2:3, :width] = d_shift
    sums_ref[2:3, 2 * width : 3 * width] = d_bias
    for made in (
        put_second,
        put_inner,
        copy(branch, branch_hbm, 7),
        copy(d_resid, resid_hbm, 8),
    ):
        made.wait()


def backward_ff(layer, grad, saved1, saved2, weights, after=()):
    _, _, _, hat1, _, _, spread1 = saved1
    slope, _, hat2, _, spread2, d_upper, _ = saved2
    gain, _, w_fi, _, w_fo, _ = weights[4:10]
    length, width = grad.shape
    ff = w_fi.shape[2]
    outs = (
        low(length, width),
        low(length, ff),
        low(length, width),
        full(length, width),
        full(8, ff),
    )
    return call(
        partial(backward_ff_kernel, layer),
        f"backward_ff{layer}",
        outs,
        (ANY,) * 4 + (WHOLE,),
        (grad, d_upper, spread1, spread2, weights[10], gain, w_fi, w_fo, hat1, slope, hat2),
        [WHOLE] * 6 + [ANY] * 5,
        [
            pltpu.VMEM(w_fi.shape[1:], BF16),
            pltpu.VMEM(w_fo.shape[1:], BF16),
            vm(hat1),
            vm(slope),
            vm(hat2),
            vm(outs[0]),
            vm(outs[1]),
            vm(outs[2]),
            vm(outs[3]),
            pltpu.SemaphoreType.DMA((9,)),
        ],
        after,
        16 * 10**9,
        22 * 10**6,
    )


def backward_attention_kernel(
    layer,
    scale,
    row_ref,
    seg_ref,
    lse_ref,
    w_in_hbm,
    w_out_hbm,
    qkv_hbm,
    mixed_hbm,
    branch_hbm,
    resid_hbm,
    d_qkv_hbm,
    d_x_ref,
    sums_ref,
    w_in,
    w_out,
    qkv,
    mixed,
    branch,
    d_resid,
    d_qkv,
    d_mix,
    code_q,
    code_k,
    delta_ref,
    probs_ref,
    ds_ref,
    sems,
):
    length, width = branch.shape
    copy = copier(sems)
    get_branch = copy(branch_hbm, branch, 0)
    get_out = copy(w_out_hbm.at[layer], w_out, 1)
    get_mixed = copy(mixed_hbm, mixed, 2)
    get_qkv = copy(qkv_hbm, qkv, 3)
    get_in = copy(w_in_hbm.at[layer], w_in, 4)
    get_resid = copy(resid_hbm, d_resid, 5)
    fill_codes(seg_ref, row_ref[0], code_q, code_k)
    probs_ref[...] = jnp.zeros_like(probs_ref)
    ds_ref[...] = jnp.zeros_like(ds_ref)
    sums_ref[...] = jnp.zeros_like(sums_ref)
    total = lambda value: jnp.sum(value.astype(F32), 0, keepdims=True)
    head_of = lax.broadcasted_iota(jnp.int32, (16, width), 1) // HEAD
    ones = (head_of == lax.broadcasted_iota(jnp.int32, (16, width), 0)).astype(F32).astype(BF16)
    get_branch.wait()
    get_out.wait()
    d_mix[...] = mm(branch[...], w_out[...], NT).astype(BF16)
    get_mixed.wait()
    product = d_mix[...].astype(F32) * mixed[...].astype(F32)
    high = product.astype(BF16)
    rest = (product - high.astype(F32)).astype(BF16)
    delta_ref[...] = mm(ones, high, NT) + mm(ones, rest, NT)

    get_qkv.wait()
    low_half = lax.broadcasted_iota(jnp.int32, (length, LANES), 1) < HEAD
    low_rows = lax.broadcasted_iota(jnp.int32, (LANES, length), 0) < HEAD

    def pair(number, carry):
        at = pl.multiple_of(number * LANES, LANES)
        cols = pl.ds(at, LANES)
        key_cols = pl.ds(at + width, LANES)
        value_cols = pl.ds(at + 2 * width, LANES)
        queries, keys, values, mix = qkv[:, cols], qkv[:, key_cols], qkv[:, value_cols], d_mix[:, cols]
        keys_t = keys.T
        d_query = jnp.zeros((LANES, length), F32)
        d_keys, d_values = [], []
        zero = jnp.zeros_like(keys)
        for sub in range(2):
            head = 2 * number + sub
            lse = lse_ref[pl.ds(head, 1), :]
            delta = delta_ref[pl.ds(head, 1), :]
            mine = low_half == (sub == 0)
            scores = mm(
                jnp.where(mine, keys, code_k[...]), jnp.where(mine, queries, code_q[...]), NT
            )
            d_probs = mm(jnp.where(mine, values, zero), mix, NT)
            for rows in chunks(length):
                start, stop = window(rows.start, length)
                probs = jnp.exp(scores[rows, start:stop] - lse[:, start:stop])
                probs_ref[sub, rows, start:stop] = probs.astype(BF16)
                ds_ref[sub, rows, start:stop] = (
                    probs * (d_probs[rows, start:stop] - delta[:, start:stop])
                ).astype(BF16)
            d_values.append(mm(probs_ref[sub], mix))
            d_keys.append(mm(ds_ref[sub], queries))
            mine_t = jnp.where(low_rows == (sub == 0), keys_t, jnp.zeros_like(keys_t))
            d_query += mm(mine_t, ds_ref[sub])
        dq = (d_query.T * scale).astype(BF16)
        d_qkv[:, cols] = dq
        sums_ref[1:2, cols] = total(dq)
        d_qkv[:, key_cols] = jnp.where(low_half, d_keys[0], d_keys[1]).astype(BF16)
        dv = jnp.where(low_half, d_values[0], d_values[1]).astype(BF16)
        d_qkv[:, value_cols] = dv
        sums_ref[1:2, key_cols] = total(dv)
        return carry

    lax.fori_loop(0, HEADS * HEAD // LANES, pair, 0)
    put_qkv = copy(d_qkv, d_qkv_hbm, 6)
    get_in.wait()
    get_resid.wait()
    d_x = mm(d_qkv[...], w_in[...], NT)
    for rows in chunks(length):
        d_x_ref[rows, :] = (d_resid[rows, :] + d_x[rows]).astype(BF16)
    put_qkv.wait()


def backward_attention(layer, row, seg, saved1, branch, d_resid, weights, after=()):
    qkv, lse, mixed = saved1[:3]
    w_in, _, w_out = weights[:3]
    ff = weights[6].shape[2]
    length, width = mixed.shape
    outs = (low(length, 3 * width), low(length, width), full(8, ff))
    return call(
        partial(backward_attention_kernel, layer, HEAD**-0.5),
        f"backward_attention{layer}",
        outs,
        (ANY, WHOLE, WHOLE),
        (row, seg, lse, w_in, w_out, qkv, mixed, branch, d_resid),
        [SCALAR, WHOLE, WHOLE] + [ANY] * 6,
        [
            pltpu.VMEM(w_in.shape[1:], BF16),
            pltpu.VMEM(w_out.shape[1:], BF16),
            vm(qkv),
            vm(mixed),
            vm(branch),
            vm(d_resid),
            vm(outs[0]),
            vm(outs[1]),
            pltpu.VMEM((length, LANES), BF16),
            pltpu.VMEM((length, LANES), BF16),
            pltpu.VMEM((16, length), F32),
            pltpu.VMEM((2, length, length), BF16),
            pltpu.VMEM((2, length, length), BF16),
            pltpu.SemaphoreType.DMA((7,)),
        ],
        after,
        20 * 10**9,
        16 * 10**6,
    )


def grad_cols_kernel(half_ref, *refs, rows, steps):
    lefts, rights = refs[:rows], refs[rows : 2 * rows]
    other_ref, own_ref, turned = refs[-3:]
    length = lefts[0].shape[0]
    step = pl.program_id(0)

    @pl.when(step == 0)
    def _():
        for number, left in enumerate(lefts):
            turned[:, number * length : (number + 1) * length] = left[...].T

    found = None
    for number, right in enumerate(rights):
        part = mm(turned[:, number * length : (number + 1) * length], right[...])
        found = part if found is None else found + part
    found = found.reshape(own_ref.shape).astype(BF16)

    @pl.when(step < steps)
    def _():
        other_ref[...] = found

    @pl.when(step >= steps)
    def _():
        own_ref[...] = found


def weight_grad_cols(half, lefts, rights, narrow, after=()):
    rows = len(lefts)
    length, width = lefts[0].shape
    cols = rights[0].shape[1] // 2
    tile = next((size for size in (768, 384) if cols % size == 0), cols)
    steps = cols // tile
    shape = jax.ShapeDtypeStruct((narrow, width // narrow, cols), BF16)
    block = (narrow, width // narrow, tile)

    def right_at(j, half):
        mine = jnp.where(j < steps, 1 - half[0], half[0])
        return (0, mine * steps + jnp.where(j < steps, j, j - steps))

    return pl.pallas_call(
        partial(grad_cols_kernel, rows=rows, steps=steps),
        out_shape=(shape, shape),
        grid_spec=pltpu.PrefetchScalarGridSpec(
            num_scalar_prefetch=1,
            grid=(2 * steps,),
            in_specs=[pl.BlockSpec((length, width), lambda j, half: (0, 0))] * rows
            + [pl.BlockSpec((length, tile), right_at)] * rows
            + [ANY] * len(after),
            out_specs=(
                pl.BlockSpec(block, lambda j, half: (0, 0, jnp.minimum(j, steps - 1))),
                pl.BlockSpec(block, lambda j, half: (0, 0, jnp.maximum(j - steps, 0))),
            ),
            scratch_shapes=[pltpu.VMEM((width, rows * length), BF16)],
        ),
        compiler_params=pltpu.CompilerParams(vmem_limit_bytes=LIMIT),
        cost_estimate=BRIEF,
        name="weight_grad_cols",
    )(half, *lefts, *rights, *after)


def grad_rows_kernel(half_ref, *refs, rows, narrow):
    lefts, rights = refs[:rows], refs[rows : 2 * rows]
    other_ref, own_ref = refs[-2:]
    unit = own_ref.shape[1]
    width = rights[0].shape[1]
    found = None
    for left, right in zip(lefts, rights):
        part = mm(left[...], right[...], TN)
        found = part if found is None else found + part
    found = found.astype(BF16)

    def write(ref):
        for block in range(ref.shape[2] // width):
            ref[0, :, block * width : (block + 1) * width] = found[
                block * unit : (block + 1) * unit
            ]

    @pl.when(pl.program_id(0) < narrow)
    def _():
        write(other_ref)

    @pl.when(pl.program_id(0) >= narrow)
    def _():
        write(own_ref)


def weight_grad_rows(half, lefts, rights, narrow, after=()):
    rows = len(lefts)
    length, deep = lefts[0].shape
    width = rights[0].shape[1]
    unit = width // narrow
    part = deep // narrow // 2
    cols = part // unit * width
    shape = jax.ShapeDtypeStruct((narrow, unit, cols), BF16)

    def left_at(j, half):
        first = j < narrow
        return (0, 2 * jnp.where(first, j, j - narrow) + jnp.where(first, 1 - half[0], half[0]))

    return pl.pallas_call(
        partial(grad_rows_kernel, rows=rows, narrow=narrow),
        out_shape=(shape, shape),
        grid_spec=pltpu.PrefetchScalarGridSpec(
            num_scalar_prefetch=1,
            grid=(2 * narrow,),
            in_specs=[pl.BlockSpec((length, part), left_at)] * rows
            + [pl.BlockSpec((length, width), lambda j, half: (0, 0))] * rows
            + [ANY] * len(after),
            out_specs=(
                pl.BlockSpec((1, unit, cols), lambda j, half: (jnp.minimum(j, narrow - 1), 0, 0)),
                pl.BlockSpec((1, unit, cols), lambda j, half: (jnp.maximum(j - narrow, 0), 0, 0)),
            ),
        ),
        compiler_params=pltpu.CompilerParams(vmem_limit_bytes=LIMIT),
        cost_estimate=BRIEF,
        name="weight_grad_rows",
    )(half, *lefts, *rights, *after)


def swap(value, bit):
    size = lax.axis_size("wide")
    return lax.ppermute(value, "wide", [(i, i ^ bit) for i in range(size)])


def tie(values, on):
    return lax.optimization_barrier((values, on))[0]


def add_low(left, right):
    return (left.astype(F32) + right.astype(F32)).astype(BF16)


def halves(value, side, axis):
    half = value.shape[axis] // 2
    keep = lax.dynamic_slice_in_dim(value, side * half, half, axis)
    give = lax.dynamic_slice_in_dim(value, (1 - side) * half, half, axis)
    return keep, give


def wide_bits():
    return [1 << i for i in range((lax.axis_size("wide") - 1).bit_length())]


def bit_order(turn):
    rest = wide_bits()[1:]
    return rest[::-1] if turn else rest


class Halving:
    def __init__(self, groups):
        self.place = lax.axis_index("wide")
        self.bits = list(zip(*(bit_order(turn) for turn in range(2))))
        self.groups = groups
        self.flying = None

    def step(self, on=None):
        if self.flying is not None:
            if on is not None:
                self.flying = [(keep, tie(recv, on)) for keep, recv in self.flying]
            self.groups = [[add_low(keep, recv)] for keep, recv in self.flying]
            self.flying = None
        if not self.bits:
            return [group[0] for group in self.groups]
        flying, gives = [], []
        for bit, group in zip(self.bits.pop(0), self.groups):
            split = [halves(part, (self.place // bit) % 2, 1) for part in group]
            keep = jnp.concatenate([pair[0] for pair in split], -1)
            give = jnp.concatenate([pair[1] for pair in split], -1)
            gives.append(give)
            flying.append((keep, swap(give, bit)))
        self.flying = flying
        return gives

    def finish(self, on=None):
        mine = self.step(on)
        while self.flying is not None:
            mine = self.step()
        return jnp.concatenate(mine, -1)


def narrow_sum_swaps(mine, ons=(None, None)):
    size = lax.axis_size("narrow")
    place = lax.axis_index("narrow")
    cur = mine.reshape((2,) * (size.bit_length() - 1) + mine.shape[1:])
    depth = size.bit_length() - 1
    for level in range(depth):
        bit = 1 << level
        axis = depth - 1 - level
        keep, give = halves(cur, (place // bit) % 2, axis)
        recv = lax.ppermute(give, "narrow", [(i, i ^ bit) for i in range(size)])
        if level < len(ons) and ons[level] is not None:
            recv = tie(recv, ons[level])
        cur = add_low(keep, recv)
    return cur.reshape(mine.shape[1:])


def wide_gather_swaps(mine, got=None):
    place = lax.axis_index("wide")
    cur = mine[None]
    for number, bit in enumerate(wide_bits()[::-1]):
        other = got[None] if number == 0 and got is not None else swap(cur, bit)
        upper = (place // bit) % 2 == 1
        cur = jnp.stack([jnp.where(upper, other, cur), jnp.where(upper, cur, other)])
        cur = cur.reshape((-1,) + mine.shape)
    return cur


def narrow_sum(mine):
    return lax.psum_scatter(mine, "narrow", scatter_dimension=0, tiled=True)[0]


def small_pack_kernel(smalls, *refs):
    small_refs, sums_refs = refs[:smalls], refs[smalls:-4]
    out_ref, small, sums, rest = refs[-4:]
    _, narrow, unit, lanes = out_ref.shape
    width = narrow * unit
    stu = lanes
    share = stu // narrow
    deep = sums.shape[1]
    small[...] = sum(ref[...] for ref in small_refs)
    sums[...] = sum(ref[...] for ref in sums_refs)
    own = width + 2 * stu
    vectors = [
        (sums, 1, 0, 2 * width),
        (sums, 2, 2 * width, width),
        (sums, 1, 2 * width, 2 * width),
        (sums, 2, 0, 2 * width),
        (sums, 0, 0, deep),
        (sums, 2, 3 * width, width),
        (small, own, 0, stu),
        (small, own + 1, 0, stu),
        (small, own + 2, 0, stu),
    ]
    for place in range(narrow):
        out_ref[0, place] = small[place * unit : (place + 1) * unit, :].astype(BF16)
        rest[...] = jnp.zeros_like(rest)
        for number in range(2):
            start = width + number * stu + place * share
            rest[number * share : (number + 1) * share, :] = small[start : start + share, :]
        row = 2 * share
        for ref, line, start, size in vectors:
            size = size // narrow
            value = ref[line : line + 1, :][:, start + place * size : start + (place + 1) * size]
            for at in range(0, size, lanes):
                part = min(lanes, size - at)
                rest[row : row + 1, :part] = value[:, at : at + part]
                row += 1
        rest[row : row + 1, :] = small[own + 3 : own + 4, :]
        out_ref[1, place] = rest[...].astype(BF16)


def small_pack(smalls, sums, narrow):
    stu = smalls[0].shape[1]
    width = smalls[0].shape[0] - 2 * stu - 8
    unit = width // narrow
    return pl.pallas_call(
        partial(small_pack_kernel, len(smalls)),
        out_shape=low(2, narrow, unit, stu),
        in_specs=[WHOLE] * (len(smalls) + len(sums)),
        out_specs=WHOLE,
        scratch_shapes=[vm(smalls[0]), vm(sums[0]), pltpu.VMEM((unit, stu), F32)],
        cost_estimate=BRIEF,
        name="small_pack",
    )(*smalls, *sums)


def place_rows(orders, place, rows):
    found = []
    for order in orders:
        at = 0
        for bit in order:
            at = 2 * at + (place // bit) % 2
        found.append(at * rows)
    return found


def turn_bits(place, total):
    count = (total - 1).bit_length()
    return sum(((place >> i) & 1) << (count - 1 - i) for i in range(count))


def place_ff_kernel(layer, orders, turned, held, got_ref, *refs):
    outs = refs[held : held + 3]
    fi, fo, ao, sems = refs[held + 3 :]
    unit, deep = fi.shape
    width = ao.shape[1]
    half = width // 2
    total, rows, _ = got_ref.shape
    blocks = fo.shape[0] // unit // 2
    for place in range(total):
        core = place % 2
        x_at, y_at = place_rows(orders, place, rows)
        at = turn_bits(place, total) if turned else place
        get = lambda start, size, at=at: got_ref[at, :, start : start + size].astype(F32)
        fi[x_at : x_at + rows, core * deep // 2 : (core + 1) * deep // 2] = get(0, deep // 2)
        for block in range(blocks):
            at = (core * blocks + block) * unit + y_at
            fo[at : at + rows, :] = get(deep // 2 + block * width, width)
        ao[y_at : y_at + rows, core * half : (core + 1) * half] = get(deep, half)
    puts = []
    for number, (src, dst) in enumerate(zip((fi, fo, ao), outs)):
        puts.append(pltpu.make_async_copy(src, dst.at[layer], sems.at[number]))
        puts[-1].start()
    for made in puts:
        made.wait()


def place_attn_kernel(layer, orders, held, got_ref, *refs):
    out, small = refs[held], refs[held + 1]
    ai, sem = refs[held + 2 :]
    total, rows, cols = got_ref.shape
    half = ai.shape[1] // 2
    cut = cols // 2
    rest = half - cut
    for place in range(total):
        core = place % 2
        x_at, y_at = place_rows(orders, place, rows)
        at = turn_bits(place, total)
        get = lambda start, size: got_ref[at, :, start : start + size].astype(F32)
        start = core * half
        ai[x_at : x_at + rows, start : start + cut] = get(0, cut)
        ai[y_at : y_at + rows, start + cut : start + half] = get(cut, rest)
        small[y_at : y_at + rows, core * LANES : (core + 1) * LANES] = get(cut + rest, LANES)
    made = pltpu.make_async_copy(ai, out.at[layer], sem)
    made.start()
    made.wait()


def place_ff(layer, got, turned, shapes, previous=()):
    held = len(previous)
    return pl.pallas_call(
        partial(place_ff_kernel, layer, [bit_order(turn) for turn in range(2)], turned, held),
        out_shape=tuple(shapes),
        in_specs=[WHOLE] + [ANY] * held,
        out_specs=(ANY,) * 3,
        scratch_shapes=[pltpu.VMEM(shape.shape[1:], F32) for shape in shapes]
        + [pltpu.SemaphoreType.DMA((3,))],
        input_output_aliases={1 + i: i for i in range(held)},
        compiler_params=pltpu.CompilerParams(vmem_limit_bytes=LIMIT),
        cost_estimate=pl.CostEstimate(flops=10**6, bytes_accessed=8 * 10**6, transcendentals=0),
        name=f"place_ff{layer}",
    )(got, *previous)


def place_attn(layer, got, shape, previous=(), after=()):
    held = len(previous)

    def body(got_ref, *refs):
        kept = refs[:held] + refs[held + len(after) :]
        place_attn_kernel(layer, orders, held, got_ref, *kept)

    orders = [bit_order(turn) for turn in range(2)]
    return pl.pallas_call(
        body,
        out_shape=(shape, full(shape.shape[1], 2 * LANES)),
        in_specs=[WHOLE] + [ANY] * (held + len(after)),
        out_specs=(ANY, WHOLE),
        scratch_shapes=[pltpu.VMEM(shape.shape[1:], F32), pltpu.SemaphoreType.DMA],
        input_output_aliases={1 + i: i for i in range(held)},
        compiler_params=pltpu.CompilerParams(vmem_limit_bytes=LIMIT),
        cost_estimate=pl.CostEstimate(flops=10**6, bytes_accessed=3 * 10**6, transcendentals=0),
        name=f"place_attn{layer}",
    )(got, *previous, *after)


def place_small_kernel(first_ref, second_ref, proj_ref, dense_ref, cls_ref, *vec_refs):
    for layer, ref in enumerate((first_ref, second_ref)):
        stu = dense_ref.shape[1]
        proj_ref[layer] = ref[:, :LANES]
        dense_ref[layer] = ref[:stu, LANES:]
        cls_ref[layer] = ref[stu : 2 * stu, LANES : LANES + cls_ref.shape[2]]
        row = 2 * stu
        for out in vec_refs:
            size = out.shape[1]
            for start in range(0, size, LANES):
                part = min(LANES, size - start)
                out[layer : layer + 1, start : start + part] = ref[
                    row : row + 1, LANES : LANES + part
                ]
                row += 1


def place_small(first, second, width, deep, classes, narrow):
    sizes = [2 * width, width, 2 * width, 2 * width, deep, width, LANES, LANES, LANES]
    stu = LANES // narrow
    outs = (
        full(2, width // narrow, LANES),
        full(2, stu, LANES),
        full(2, stu, classes),
    ) + tuple(full(2, size // narrow) for size in sizes)
    return pl.pallas_call(
        place_small_kernel,
        out_shape=outs + (full(2, classes),),
        in_specs=[WHOLE, WHOLE],
        out_specs=(WHOLE,) * 13,
        name="place_small",
    )(first, second)


def route_kernel(me_ref, *refs):
    around, out_ref, held = refs[:-2], refs[-2], refs[-1]
    me, size = me_ref[0], len(around)
    for step, ref in enumerate(around):
        held[lax.rem(me + (size - step), size)] = ref[0]
    counts = [held[i] for i in range(size)]
    flow, before = [], []
    total = jnp.int32(0)
    for value in counts:
        before.append(total)
        total = total + value - 1
        flow.append(total)
    right1 = [(f >= 1) & (c >= 1) for f, c in zip(flow, counts)]
    left1 = [(f <= -1) & (c >= 1) for f, c in zip(before, counts)]
    right2 = [(f >= 1) & ((f >= 2) | (c == 0)) for f, c in zip(flow, counts)]
    left2 = [(f <= -1) & ((f <= -2) | (c == 0)) for f, c in zip(before, counts)]

    def at(values, shift):
        found = jnp.int32(0)
        for i, value in enumerate(values):
            found = jnp.where(me + shift == i, value.astype(jnp.int32), found)
        return found

    count = at(counts, 0)
    from_left2, from_right2 = at(right2, -1), at(left2, 1)
    sent_right, sent_left = at(right1, 0), at(left1, 0)
    results = (
        at(right1, -1),
        from_left2,
        from_left2 | from_right2,
        (count == 2).astype(jnp.int32),
        ((count == 1) & (sent_right + sent_left == 0)).astype(jnp.int32),
        at(right2, 0),
        sent_left,
        (sent_right & at(right2, 1)) | (sent_left & at(left2, -1)),
        (count >= 1).astype(jnp.int32),
        (count >= 2).astype(jnp.int32),
    )
    for i, value in enumerate(results):
        out_ref[i] = value
    for i in range(len(results), out_ref.shape[0]):
        out_ref[i] = 0


def route(me, around):
    return pl.pallas_call(
        route_kernel,
        out_shape=jax.ShapeDtypeStruct((16,), jnp.int32),
        in_specs=[SCALAR] * (1 + len(around)),
        out_specs=SCALAR,
        scratch_shapes=[pltpu.SMEM((len(around),), jnp.int32)],
        name="route",
    )(me, *around)


def shards(
    tokens,
    segments,
    exit_layer,
    attn_in,
    qv_bias,
    attn_out,
    out_bias,
    ln_gain,
    ln_bias,
    ff_in,
    ff_in_bias,
    ff_out,
    ff_out_bias,
    stu_proj,
    stu_bias,
    pool_query,
    stu_dense,
    stu_dense_bias,
    stu_cls,
    stu_cls_bias,
    out_cot,
    logit_cot,
):
    row_count, length, width = tokens.shape
    classes = stu_cls.shape[-1]
    blank = LANES - classes
    narrow = lax.axis_size("narrow")
    me = lax.axis_index("narrow")
    core = lax.axis_index("wide") % 2
    weights = (
        attn_in,
        qv_bias,
        attn_out,
        out_bias,
        ln_gain,
        ln_bias,
        ff_in,
        ff_in_bias,
        ff_out,
        ff_out_bias,
        stu_proj,
        stu_bias,
        pool_query,
        stu_dense,
        stu_dense_bias,
        jnp.pad(stu_cls, ((0, 0), (0, 0), (0, blank))),
        jnp.pad(stu_cls_bias, ((0, 0), (0, blank))),
    )
    wide_cot = jnp.pad(logit_cot.astype(F32), ((0, 0), (0, 0), (0, blank)))

    alive = exit_layer == 1
    row_a = jnp.where(alive[0], 0, jnp.where(alive[1], 1, 0)).astype(jnp.int32)
    row_b = 1 - row_a

    index = lambda row: row.reshape(1)
    first_row = jnp.zeros((1,), jnp.int32)
    own = index(core)
    ia, ib = index(row_a), index(row_b)
    early_cot, late_cot = wide_cot[:, 0], wide_cot[:, 1]
    a1 = forward_attention(0, ia, tokens, segments, weights)

    mine = tie(jnp.sum(alive.astype(jnp.int32)).reshape(1), a1[4])
    around = [mine] + [
        lax.ppermute(mine, "narrow", [(i, (i + step) % narrow) for i in range(narrow)])
        for step in range(1, narrow)
    ]
    flags = route(me.reshape(1), around)
    from_left1, from_left2, use_two, use_b, use_a, on_right, sent_left, is_far, a_alive, b_alive = (
        flags[i] == 1 for i in range(10)
    )

    even = me % 2 == 0
    inner = [(i, i ^ 1) for i in range(narrow)]
    outer = []
    for i in range(lax.axis_size("wide") * narrow):
        place, line = i // narrow, i % narrow
        other = ((line + 1) ^ 1) - 1
        inside = 0 <= other < narrow
        outer.append((i, place * narrow + other if inside else (place ^ 1) * narrow + line))

    def shift(value):
        return (
            lax.ppermute(value, "narrow", inner),
            lax.ppermute(value, ("wide", "narrow"), outer),
        )

    def pick(pair, is_left):
        return jnp.where(is_left == even, pair[1], pair[0])

    def out_one(pair):
        return pick(pair, from_left1)

    def out_two(pair, one, own_a, own_b):
        two = pick(pair, from_left2)
        return jnp.where(use_b, own_b, jnp.where(use_a, own_a, jnp.where(use_two, two, one)))

    def back_one(pair):
        return pick(pair, ~on_right)

    def back_two(value, pair, pair2):
        return jnp.where(
            use_a, value, jnp.where(is_far, pick(pair2, sent_left), pick(pair, sent_left))
        )

    def row_of(value, row):
        return lax.dynamic_index_in_dim(value, row, 0, False)

    cot_a, cot_b = row_of(out_cot, row_a), row_of(out_cot, row_b)
    pair = shift(tie(cot_a, a1[4]))
    a2 = forward_ff(0, ia, a1[4], a1[5], early_cot, segments, late_cot, weights, (cot_a,))
    cot_one = out_one(tie(pair, a2[3]))
    pair = shift(a2[3])
    b1 = forward_attention(0, ib, tokens, segments, weights, (a2[3], cot_one))
    one = out_one(tie(pair, b1[4]))
    pair = shift(one)
    b2 = forward_ff(0, ib, b1[4], b1[5], early_cot, segments, late_cot, weights, (one,))
    work_in = out_two(tie(pair, b2[3]), one, a2[3], b2[3])
    work_seg = work_in[length + 1 : length + 2, :length].astype(jnp.int32)
    work_late = work_in[length + 2 : length + 3, :LANES].astype(F32)

    pair = shift(tie(cot_one, b2[3]))
    w1 = forward_attention(1, first_row, work_in[None], work_seg, weights)
    work_cot = out_two(tie(pair, w1[4]), cot_one, cot_a, cot_b)
    w2 = forward_ff(
        1, first_row, w1[4], w1[5], work_late, work_seg, work_late, weights, (work_cot,)
    )
    sent_h = w2[3]
    pair_h = shift(sent_h)
    w3 = backward_ff(1, work_cot, w1, w2, weights, (sent_h,))

    def ff_jobs(saved1, saved2, back):
        first = [s[4] for s in saved1]
        mixed = [s[2] for s in saved1]
        active = [s[1] for s in saved2]
        second, inner, branch = ([b[i] for b in back] for i in range(3))
        return (
            (weight_grad_cols, first, inner),
            (weight_grad_rows, active, second),
            (weight_grad_cols, mixed, branch),
        )

    def weight_grads(jobs, after=()):
        return [job(own, lefts, rights, narrow, after) for job, lefts, rights in jobs]

    def core_sum(pairs, on=None):
        received = [swap(other, 1) for other, _ in pairs]
        if on is not None:
            received = tie(received, on)
        return [add_low(mine, recv) for (_, mine), recv in zip(pairs, received)]

    def ff_halving(parts):
        return Halving([[parts[0]], [parts[1], parts[2]]])

    def attn_halving(part, small):
        keep, give = halves(small, core, 0)
        small = add_low(keep, swap(give, 1))[0]
        cut = (part.shape[-1] + LANES) // 2
        return Halving([[part[..., :cut]], [part[..., cut:], small]])

    halves1 = weight_grads(ff_jobs([w1], [w2], [w3]))
    sent = tuple(pair[0] for pair in halves1)
    w4 = backward_attention(1, first_row, work_seg, w1, w3[2], w3[3], weights, sent)
    pair_x = shift(w4[1])
    ff1 = ff_halving(core_sum(halves1))
    flying = ff1.step()
    half1 = weight_grads(((weight_grad_cols, [work_in[:length]], [w4[0]]),), tuple(flying))
    small1 = small_pack([w2[6]], [w3[4], w4[2]], narrow)
    forth_x = back_one(tie(pair_x, half1[0][0]))
    pair_x2 = shift(forth_x)

    base_b = jnp.where(b_alive, w4[1], row_of(out_cot, row_b))
    b3 = backward_ff(0, base_b, b1, b2, weights, (half1[0][0], forth_x, small1))
    far_x = back_two(w4[1], pair_x, tie(pair_x2, b3[2]))
    forth_h = back_one(tie(pair_h, far_x))
    pair_h2 = shift(forth_h)
    at1 = attn_halving(core_sum(half1)[0], small1)
    flying = at1.step() + ff1.step(b3[2])
    base_a = jnp.where(a_alive, far_x, row_of(out_cot, row_a))
    a3 = backward_ff(0, base_a, a1, a2, weights, (*flying, forth_h))
    mine_ff1 = ff1.finish(a3[2])
    flying = at1.step(a3[2])
    halves0 = weight_grads(ff_jobs([a1, b1], [a2, b2], [a3, b3]), (mine_ff1, *flying))
    ff0 = ff_halving(core_sum(halves0))
    flying = ff0.step()
    mine_at1 = at1.finish(halves0[-1][0])
    far_h = back_two(sent_h, pair_h, tie(pair_h2, a3[2]))
    b4 = backward_attention(
        0, ib, segments, b1, b3[2], b3[3], weights, (*flying, mine_at1, far_h)
    )
    sum_at1 = narrow_sum(mine_at1)
    sum_ff1 = narrow_sum_swaps(mine_ff1, (halves0[1][0], b4[1]))
    flying = ff0.step(b4[1])
    a4 = backward_attention(
        0, ia, segments, a1, a3[2], a3[3], weights, (b4[1], sum_at1, sum_ff1, *flying)
    )
    mine_ff0 = ff0.finish(a4[1])
    sum_ff0 = narrow_sum(mine_ff0)
    half0 = weight_grads(
        (
            (
                weight_grad_cols,
                [row_of(tokens, row_a), row_of(tokens, row_b)],
                [a4[0], b4[0]],
            ),
        ),
        (mine_ff0,),
    )
    small0 = small_pack([a2[6], b2[6]], [a3[4], b3[4], a4[2], b4[2]], narrow)
    at0 = attn_halving(core_sum(half0)[0], small0)
    flying = at0.step()
    all_ff1 = wide_gather_swaps(tie(sum_ff1, flying[0]))
    got = swap(tie(sum_at1, flying), wide_bits()[-1])
    all_at1 = wide_gather_swaps(sum_at1, got)
    all_ff0 = lax.all_gather(tie(sum_ff0, got), "wide", axis=0, tiled=False)
    all_at0 = wide_gather_swaps(narrow_sum_swaps(at0.finish(), (sum_ff0,)))

    deep = ff_in.shape[2]
    unit = width // narrow
    shapes = [full(2, unit, deep), full(2, deep // narrow, width), full(2, unit, width)]
    attn_shape = full(2, unit, 3 * width)
    placed = place_ff(1, all_ff1, True, shapes)
    d_attn_in, small1 = place_attn(1, all_at1, attn_shape)
    placed = place_ff(0, all_ff0, False, shapes, placed)
    d_attn_in, small0 = place_attn(0, all_at0, attn_shape, (d_attn_in,), (placed[2],))
    d_ff_in, d_ff_out, d_attn_out = placed
    (d_proj, d_dense, d_cls, d_qv, d_out_b, d_gain, d_shift, d_fi_b, d_fo_b, *rest) = place_small(
        small0, small1, width, deep, classes, narrow
    )
    d_stu_b, d_query, d_dense_b, d_cls_b = rest
    totals = (
        d_attn_in,
        d_qv,
        d_attn_out,
        d_out_b,
        d_gain,
        d_shift,
        d_ff_in,
        d_fi_b,
        d_ff_out,
        d_fo_b,
        d_proj,
        d_stu_b,
        d_query,
        d_dense,
        d_dense_b,
        d_cls,
        d_cls_b,
    )

    in_order = lambda for_a, for_b: jnp.where(
        row_a == 0, jnp.stack([for_a, for_b]), jnp.stack([for_b, for_a])
    )
    act_a = jnp.where(a_alive, far_h, a2[3])
    act_b = jnp.where(b_alive, w2[3], b2[3])
    cut = lambda value: value[length, :classes]
    logits = jnp.where(jnp.stack([a_alive, b_alive])[:, None], jnp.stack([cut(act_a), cut(act_b)]), 0)
    early = in_order(cut(a2[3]), cut(b2[3]))
    logits = jnp.stack([early, in_order(logits[0], logits[1])], 1).astype(BF16)
    act_a, act_b = act_a[:length], act_b[:length]
    return (in_order(act_a, act_b), logits, in_order(a4[1], b4[1])) + totals


def solution(mesh):
    rows = ("wide", "narrow")
    return jax.shard_map(
        shards,
        mesh=mesh,
        in_specs=(P(rows, None, None), P(rows, None), P(rows))
        + (P(),) * 17
        + (P(rows, None, None), P(rows, None, None)),
        out_specs=(P(rows, None, None),) * 3
        + (
            P(None, "narrow", None),
            P(None, "narrow"),
            P(None, "narrow", None),
            P(None, "narrow"),
            P(None, "narrow"),
            P(None, "narrow"),
            P(None, "narrow", None),
            P(None, "narrow"),
            P(None, "narrow", None),
            P(None, "narrow"),
            P(None, "narrow", None),
            P(None, "narrow"),
            P(None, "narrow"),
            P(None, "narrow", None),
            P(None, "narrow"),
            P(None, "narrow", None),
            P(),
        ),
        check_vma=False,
    )
```

```python
from functools import partial

import jax
import jax.numpy as jnp
import numpy as np
from jax import lax
from jax.experimental import pallas as pl
from jax.experimental.pallas import tpu as pltpu
from jax.sharding import PartitionSpec as P

HEADS = 12
HEAD = 64
STU_HEADS = 2
LANES = 128
CHUNK = 128
REACH = 256
EPS = 1e-12
MASKED = -1e30
SEGMENTS = 4
HIGH = lax.Precision.HIGHEST
F32 = jnp.float32
BF16 = jnp.bfloat16
LIMIT = 52 * 1024 * 1024
BRIEF = pl.CostEstimate(flops=10**6, bytes_accessed=10**5, transcendentals=0)

NN = (((1,), (0,)), ((), ()))
NT = (((1,), (1,)), ((), ()))
TN = (((0,), (0,)), ((), ()))


def mm(left, right, dims=NN):
    return lax.dot_general(left, right, dims, preferred_element_type=F32)


def mm_high(left, right, dims=NN):
    return lax.dot_general(left, right, dims, precision=HIGH, preferred_element_type=F32)


def vec(ref, layer, start, size):
    return ref[...].astype(F32)[layer : layer + 1, start : start + size]


def gelu_pair(value):
    dist = jnp.abs(value) * (0.5**0.5)
    den = 1.0 + 0.3275911 * dist
    part = pl.reciprocal(den, approx=True)
    part = part * (2.0 - den * part)
    series = 0.5 * 1.061405429
    for term in (-1.453152027, 1.421413741, -0.284496736, 0.254829592):
        series = series * part + 0.5 * term
    bell = jnp.exp(-(dist * dist))
    tail = series * part * bell
    below = jnp.where(value >= 0, 1.0 - tail, tail)
    return value * below, below + value * bell * ((2.0 * np.pi) ** -0.5)


def row_norm(value):
    mean = jnp.mean(value, -1, keepdims=True)
    centered = value - mean
    spread = lax.rsqrt(jnp.mean(centered * centered, -1, keepdims=True) + EPS)
    return centered * spread, spread


def norm_back(grad, hat, spread, gain):
    scaled = grad * gain
    low = jnp.mean(scaled, -1, keepdims=True)
    high = jnp.mean(scaled * hat, -1, keepdims=True)
    return spread * (scaled - low - hat * high)


def window(place, length):
    start = max(0, (place - REACH + 1) // CHUNK * CHUNK)
    stop = min(length, -(-(place + CHUNK + REACH - 1) // CHUNK) * CHUNK)
    return start, stop


def fill_codes(seg_ref, row, code_q, code_k):
    length = code_q.shape[0]
    seg_row = seg_ref[pl.ds(row, 1), :].astype(F32)
    seg_cols = jnp.broadcast_to(seg_row, (LANES, length)).T
    lane = lax.broadcasted_iota(jnp.int32, (length, LANES), 1) % HEAD
    same = seg_cols == lane.astype(F32)
    code_q[...] = jnp.where(same, 1.0, 0.0).astype(BF16)
    code_k[...] = jnp.where(same | (lane >= SEGMENTS), 0.0, MASKED).astype(BF16)


ANY = pl.BlockSpec(memory_space=pl.ANY)
WHOLE = pl.BlockSpec(memory_space=pltpu.VMEM)
SCALAR = pl.BlockSpec(memory_space=pltpu.SMEM)


def low(*shape):
    return jax.ShapeDtypeStruct(shape, BF16)


def full(*shape):
    return jax.ShapeDtypeStruct(shape, F32)


def vm(like):
    return pltpu.VMEM(like.shape, like.dtype)


def call(kernel, name, outs, out_specs, inputs, in_specs, scratch, after, flops, moved):
    count, extra = len(inputs), len(after)

    def body(*refs):
        kernel(*refs[:count], *refs[count + extra :])

    return pl.pallas_call(
        body,
        out_shape=outs,
        in_specs=list(in_specs) + [ANY] * extra,
        out_specs=out_specs,
        scratch_shapes=scratch,
        compiler_params=pltpu.CompilerParams(vmem_limit_bytes=LIMIT),
        cost_estimate=pl.CostEstimate(flops=flops, bytes_accessed=moved, transcendentals=0),
        name=name,
    )(*inputs, *after)


def copier(sems):
    def copy(src, dst, number):
        made = pltpu.make_async_copy(src, dst, sems.at[number])
        made.start()
        return made

    return copy


def chunks(length):
    return [slice(place, place + CHUNK) for place in range(0, length, CHUNK)]


def forward_attention_kernel(
    layer,
    scale,
    row_ref,
    x_hbm,
    seg_ref,
    w_in_hbm,
    w_out_hbm,
    qv_ref,
    out_b_ref,
    gain_ref,
    shift_ref,
    qkv_hbm,
    lse_ref,
    mixed_hbm,
    hat_hbm,
    first_hbm,
    full_hbm,
    spread_ref,
    x_ref,
    w_in,
    w_out,
    qkv,
    mixed,
    hat,
    first,
    full,
    code_q,
    code_k,
    terms_ref,
    sems,
):
    row = row_ref[0]
    length, width = x_ref.shape
    copy = copier(sems)
    get_x = copy(x_hbm.at[row, pl.ds(0, length)], x_ref, 0)
    get_in = copy(w_in_hbm.at[layer], w_in, 1)
    get_out = copy(w_out_hbm.at[layer], w_out, 2)
    fill_codes(seg_ref, row, code_q, code_k)
    terms_ref[...] = jnp.zeros_like(terms_ref)
    lse_ref[...] = jnp.zeros_like(lse_ref)
    get_x.wait()
    get_in.wait()

    x = x_ref[...]
    qkv[:, :width] = (
        (mm(x, w_in[:, :width]) + vec(qv_ref, layer, 0, width)).astype(BF16).astype(F32) * scale
    ).astype(BF16)
    qkv[:, width : 2 * width] = mm(x, w_in[:, width : 2 * width]).astype(BF16)
    qkv[:, 2 * width :] = (
        mm(x, w_in[:, 2 * width :]) + vec(qv_ref, layer, width, width)
    ).astype(BF16)
    put_qkv = copy(qkv, qkv_hbm, 3)

    low_half = lax.broadcasted_iota(jnp.int32, (length, LANES), 1) < HEAD
    low_rows = lax.broadcasted_iota(jnp.int32, (LANES, length), 0) < HEAD

    def pair(number, carry):
        at = pl.multiple_of(number * LANES, LANES)
        queries = qkv[:, pl.ds(at, LANES)]
        keys = qkv[:, pl.ds(at + width, LANES)]
        values_t = qkv[:, pl.ds(at + 2 * width, LANES)].T
        outs = []
        for sub in range(2):
            mine = low_half == (sub == 0)
            scores = mm(
                jnp.where(mine, keys, code_k[...]), jnp.where(mine, queries, code_q[...]), NT
            )
            tops = []
            for cols in chunks(length):
                start, stop = window(cols.start, length)
                part = scores[start:stop, cols]
                top = jnp.max(part, 0, keepdims=True)
                terms_ref[sub, start:stop, cols] = jnp.exp(part - top).astype(BF16)
                tops.append(top)
            mine_t = jnp.where(low_rows == (sub == 0), values_t, jnp.ones_like(values_t))
            product = mm(mine_t, terms_ref[sub])
            beside = HEAD * (1 - sub)
            total = product[beside : beside + 1, :]
            lse_ref[pl.ds(2 * number + sub, 1), :] = jnp.concatenate(tops, 1) + jnp.log(total)
            outs.append(product * (1.0 / total))
        mixed[:, pl.ds(at, LANES)] = jnp.where(low_rows, outs[0], outs[1]).T.astype(BF16)
        return carry

    lax.fori_loop(0, HEADS * HEAD // LANES, pair, 0)
    put_mixed = copy(mixed, mixed_hbm, 4)

    get_out.wait()
    gain, shift = vec(gain_ref, layer, 0, width), vec(shift_ref, layer, 0, width)
    out_b = vec(out_b_ref, layer, 0, width)
    branch = mm(mixed[...], w_out[...])
    for rows in chunks(length):
        normed, spread = row_norm(x_ref[rows, :].astype(F32) + branch[rows] + out_b)
        hat[rows, :] = normed.astype(BF16)
        normed = normed * gain + shift
        full[rows, :] = normed
        first[rows, :] = normed.astype(BF16)
        spread_ref[rows, :] = jnp.broadcast_to(spread, (CHUNK, LANES))
    puts = (copy(hat, hat_hbm, 5), copy(first, first_hbm, 6), copy(full, full_hbm, 7))
    for made in (put_qkv, put_mixed) + puts:
        made.wait()


def forward_attention(layer, row, x, seg, weights, after=()):
    w_in, qv, w_out, out_b, gain, shift = weights[:6]
    length, width = seg.shape[-1], x.shape[-1]
    outs = (
        low(length, 3 * width),
        full(16, length),
        low(length, width),
        low(length, width),
        low(length, width),
        full(length, width),
        full(length, LANES),
    )
    return call(
        partial(forward_attention_kernel, layer, HEAD**-0.5),
        f"forward_attention{layer}",
        outs,
        (ANY, WHOLE) + (ANY,) * 4 + (WHOLE,),
        (row, x, seg, w_in, w_out, qv, out_b, gain, shift),
        [SCALAR, ANY, WHOLE, ANY, ANY] + [WHOLE] * 4,
        [
            pltpu.VMEM((length, width), BF16),
            pltpu.VMEM(w_in.shape[1:], BF16),
            pltpu.VMEM(w_out.shape[1:], BF16),
            vm(outs[0]),
            vm(outs[2]),
            vm(outs[3]),
            vm(outs[4]),
            vm(outs[5]),
            pltpu.VMEM((length, LANES), BF16),
            pltpu.VMEM((length, LANES), BF16),
            pltpu.VMEM((2, length, length), BF16),
            pltpu.SemaphoreType.DMA((8,)),
        ],
        after,
        14 * 10**9,
        16 * 10**6,
    )


def forward_ff_kernel(
    layer,
    row_ref,
    first_hbm,
    full_hbm,
    cot_ref,
    seg_ref,
    later_ref,
    w_fi_hbm,
    w_fo_hbm,
    gain_ref,
    shift_ref,
    fi_b_ref,
    fo_b_ref,
    proj_ref,
    proj_b_ref,
    query_ref,
    dense_ref,
    dense_b_ref,
    cls_ref,
    cls_b_ref,
    slope_hbm,
    active_hbm,
    hat_hbm,
    h_hbm,
    spread_ref,
    d_upper_ref,
    small_ref,
    first,
    full,
    w_fi,
    w_fo,
    slope,
    active,
    hat,
    h,
    even,
    odd,
    sems,
):
    length, width = first.shape
    ff = w_fi.shape[1]
    copy = copier(sems)
    get_first = copy(first_hbm, first, 0)
    part = even.shape[1]
    get_fi = [
        copy(w_fi_hbm.at[layer, :, pl.ds(at, part)], w_fi.at[:, pl.ds(at, part)], 8 + at // part)
        for at in range(0, ff, part)
    ]
    get_full = copy(full_hbm, full, 2)
    get_fo = copy(w_fo_hbm.at[layer], w_fo, 3)
    get_first.wait()
    get_fi[0].wait()

    def multiply(at, into):
        into[...] = mm(first[...], w_fi[:, pl.ds(at, part)])

    def bend(at, source):
        bias_part = fi_b_ref[:, pl.ds(at, part)].astype(F32)[layer : layer + 1]
        for rows in chunks(length):
            out, grad = gelu_pair(source[rows, :] + bias_part)
            active[rows, pl.ds(at, part)] = out.astype(BF16)
            slope[rows, pl.ds(at, part)] = grad.astype(BF16)

    multiply(0, even)
    for made in get_fi[1:]:
        made.wait()
    steps = ff // part // 2

    def inner(number, carry):
        at = pl.multiple_of(number * (2 * part), 2 * part)
        multiply(at + part, odd)
        bend(at, even)
        later = pl.multiple_of(jnp.minimum(at + 2 * part, ff - part), part)
        multiply(later, even)
        bend(at + part, odd)
        return carry

    lax.fori_loop(0, steps, inner, 0)
    put_slope = copy(slope, slope_hbm, 4)
    put_active = copy(active, active_hbm, 5)

    get_fo.wait()
    get_full.wait()
    gain, shift = vec(gain_ref, layer, width, width), vec(shift_ref, layer, width, width)
    fo_b = vec(fo_b_ref, layer, 0, width)
    second = mm(active[...], w_fo[...])
    for rows in chunks(length):
        normed, spread = row_norm(full[rows, :] + second[rows] + fo_b)
        hat[rows, :] = normed.astype(BF16)
        h[rows, :] = (normed * gain + shift).astype(BF16)
        spread_ref[rows, :] = jnp.broadcast_to(spread, (CHUNK, LANES))
    put_hat = copy(hat, hat_hbm, 6)

    stu_width = proj_ref.shape[2]
    stu_scale = (stu_width // STU_HEADS) ** -0.5
    hidden = h[:length, :]
    upper = mm(hidden, proj_ref[layer]) + vec(proj_b_ref, layer, 0, stu_width)
    query = vec(query_ref, layer, 0, stu_width)
    lane_full = lax.broadcasted_iota(jnp.int32, (length, stu_width), 1)
    left = lane_full < stu_width // STU_HEADS

    def both(value):
        zero = jnp.zeros_like(value)
        return (
            jnp.sum(jnp.where(left, value, zero), -1, keepdims=True),
            jnp.sum(jnp.where(left, zero, value), -1, keepdims=True),
        )

    weights = []
    for score in both(upper * query):
        score = score * stu_scale
        terms = jnp.exp(score - jnp.max(score, 0, keepdims=True))
        weights.append(terms / jnp.sum(terms, 0, keepdims=True))
    weight = jnp.where(left, weights[0], weights[1])
    pooled = jnp.sum(weight * upper, 0, keepdims=True)
    dense = dense_ref[layer].astype(F32)
    cls = cls_ref[layer].astype(F32)
    eight = (8, stu_width)
    z = jnp.tanh(
        mm_high(jnp.broadcast_to(pooled, eight), dense) + vec(dense_b_ref, layer, 0, stu_width)
    )
    logits = mm_high(z, cls) + vec(cls_b_ref, layer, 0, LANES)
    below = lax.broadcasted_iota(jnp.int32, (16, length), 0)
    segments = jnp.broadcast_to(seg_ref[pl.ds(row_ref[0], 1), :].astype(F32), (16, length))
    later = jnp.broadcast_to(later_ref[pl.ds(row_ref[0], 1), :], (16, LANES))
    tail = jnp.where(below == 1, segments, 0.0)
    narrow_tail = jnp.where(below[:, :LANES] == 2, later, tail[:, :LANES])
    narrow_tail = jnp.where(below[:, :LANES] == 0, jnp.concatenate([logits, logits], 0), narrow_tail)
    h[length:, :LANES] = narrow_tail.astype(BF16)
    h[length:, LANES:length] = tail[:, LANES:].astype(BF16)
    h[length:, length:] = jnp.zeros((16, width - length), BF16)
    put_h = copy(h, h_hbm, 7)
    cot = cot_ref[pl.ds(row_ref[0], 1), :]
    d_pre = mm_high(jnp.broadcast_to(cot, (8, LANES)), cls, NT) * (1.0 - z * z)
    d_pooled = mm_high(d_pre, dense, NT)[:1]
    d_pre = d_pre[:1]

    def column(value):
        return jnp.broadcast_to(value, (value.shape[1], value.shape[1])).T

    d_scores = []
    for weight_col, d_weight in zip(weights, both(upper * d_pooled)):
        mean = jnp.sum(weight_col * d_weight, 0, keepdims=True)
        d_scores.append(weight_col * (d_weight - mean) * stu_scale)
    d_score = jnp.where(left, d_scores[0], d_scores[1])
    d_upper = (weight * d_pooled + d_score * query).astype(BF16)
    d_upper_ref[...] = d_upper
    small_ref[:width, :] = mm(hidden, d_upper, TN)
    small_ref[width : width + stu_width, :] = column(pooled) * d_pre
    small_ref[width + stu_width : width + 2 * stu_width, :] = column(z[:1]) * cot
    base = width + 2 * stu_width
    small_ref[base : base + 1, :] = jnp.sum(d_upper.astype(F32), 0, keepdims=True)
    small_ref[base + 1 : base + 2, :] = jnp.sum(d_score * upper, 0, keepdims=True)
    small_ref[base + 2 : base + 3, :] = d_pre
    small_ref[base + 3 : base + 4, :] = cot
    small_ref[base + 4 :, :] = jnp.zeros((4, LANES), F32)

    for made in (put_slope, put_active, put_hat, put_h):
        made.wait()


def forward_ff(layer, row, first, first_full, cot, seg, later, weights, after=()):
    gain, shift, w_fi, fi_b, w_fo, fo_b = weights[4:10]
    length, width = first.shape
    ff = w_fi.shape[2]
    stu = weights[10].shape[2]
    outs = (
        low(length, ff),
        low(length, ff),
        low(length, width),
        low(length + 16, width),
        full(length, LANES),
        low(length, stu),
        full(width + 2 * stu + 8, LANES),
    )
    return call(
        partial(forward_ff_kernel, layer),
        f"forward_ff{layer}",
        outs,
        (ANY,) * 4 + (WHOLE,) * 3,
        (row, first, first_full, cot, seg, later, w_fi, w_fo, gain, shift, fi_b, fo_b)
        + tuple(weights[10:]),
        [SCALAR, ANY, ANY, WHOLE, WHOLE, WHOLE, ANY, ANY] + [WHOLE] * 11,
        [
            pltpu.VMEM((length, width), BF16),
            pltpu.VMEM((length, width), F32),
            pltpu.VMEM(w_fi.shape[1:], BF16),
            pltpu.VMEM(w_fo.shape[1:], BF16),
            vm(outs[0]),
            vm(outs[1]),
            vm(outs[2]),
            vm(outs[3]),
            pltpu.VMEM((length, 512), F32),
            pltpu.VMEM((length, 512), F32),
            pltpu.SemaphoreType.DMA((8 + ff // 512,)),
        ],
        after,
        18 * 10**9,
        20 * 10**6,
    )


def backward_ff_kernel(
    layer,
    grad_ref,
    d_upper_ref,
    spread1_ref,
    spread2_ref,
    proj_ref,
    gain_ref,
    w_fi_hbm,
    w_fo_hbm,
    hat1_hbm,
    slope_hbm,
    hat2_hbm,
    second_hbm,
    inner_hbm,
    branch_hbm,
    resid_hbm,
    sums_ref,
    w_fi,
    w_fo,
    hat1,
    slope,
    hat2,
    second,
    inner,
    branch,
    d_resid,
    sems,
):
    length, width = grad_ref.shape
    ff = w_fi.shape[1]
    copy = copier(sems)
    get_hat2 = copy(hat2_hbm, hat2, 0)
    get_fo = copy(w_fo_hbm.at[layer], w_fo, 1)
    get_slope = copy(slope_hbm, slope, 2)
    get_fi = copy(w_fi_hbm.at[layer], w_fi, 3)
    get_hat1 = copy(hat1_hbm, hat1, 4)
    sums_ref[...] = jnp.zeros_like(sums_ref)
    get_hat2.wait()
    gain1, gain2 = vec(gain_ref, layer, 0, width), vec(gain_ref, layer, width, width)
    total = lambda value: jnp.sum(value.astype(F32), 0, keepdims=True)

    def through_norm(grads, hat_ref, spread_ref, gain, out_ref):
        d_gain = jnp.zeros((1, width), F32)
        d_shift = jnp.zeros((1, width), F32)
        d_bias = jnp.zeros((1, width), F32)
        for rows in chunks(length):
            grad = grads(rows)
            hat = hat_ref[rows, :].astype(F32)
            d_gain += total(grad * hat)
            d_shift += total(grad)
            moved = norm_back(grad, hat, spread_ref[rows, 0:1], gain)
            d_resid[rows, :] = moved
            out_ref[rows, :] = moved.astype(BF16)
            d_bias += total(moved.astype(BF16))
        return d_gain, d_shift, d_bias

    from_student = mm(d_upper_ref[...], proj_ref[layer], NT)
    d_gain, d_shift, d_bias = through_norm(
        lambda rows: grad_ref[rows, :].astype(F32) + from_student[rows],
        hat2,
        spread2_ref,
        gain2,
        second,
    )
    sums_ref[1:2, 3 * width : 4 * width] = d_gain
    sums_ref[2:3, width : 2 * width] = d_shift
    sums_ref[2:3, 3 * width : 4 * width] = d_bias
    put_second = copy(second, second_hbm, 5)

    get_fo.wait()
    get_slope.wait()
    part = 512

    def ff_part(number, carry):
        at = pl.multiple_of(number * part, part)
        column = jnp.zeros((1, part), F32)
        d_active = mm(second[...], w_fo[pl.ds(at, part), :], NT)
        for rows in chunks(length):
            d_inner = (d_active[rows] * slope[rows, pl.ds(at, part)].astype(F32)).astype(BF16)
            inner[rows, pl.ds(at, part)] = d_inner
            column += total(d_inner)
        sums_ref[0:1, pl.ds(at, part)] = column
        return carry

    lax.fori_loop(0, ff // part, ff_part, 0)
    put_inner = copy(inner, inner_hbm, 6)

    get_fi.wait()
    get_hat1.wait()
    d_first = mm(inner[...], w_fi[...], NT)
    d_gain, d_shift, d_bias = through_norm(
        lambda rows: d_resid[rows, :] + d_first[rows], hat1, spread1_ref, gain1, branch
    )
    sums_ref[1:2, 2 * width : 3 * width] = d_gain
    sums_ref[2:3, :width] = d_shift
    sums_ref[2:3, 2 * width : 3 * width] = d_bias
    for made in (
        put_second,
        put_inner,
        copy(branch, branch_hbm, 7),
        copy(d_resid, resid_hbm, 8),
    ):
        made.wait()


def backward_ff(layer, grad, saved1, saved2, weights, after=()):
    _, _, _, hat1, _, _, spread1 = saved1
    slope, _, hat2, _, spread2, d_upper, _ = saved2
    gain, _, w_fi, _, w_fo, _ = weights[4:10]
    length, width = grad.shape
    ff = w_fi.shape[2]
    outs = (
        low(length, width),
        low(length, ff),
        low(length, width),
        full(length, width),
        full(8, ff),
    )
    return call(
        partial(backward_ff_kernel, layer),
        f"backward_ff{layer}",
        outs,
        (ANY,) * 4 + (WHOLE,),
        (grad, d_upper, spread1, spread2, weights[10], gain, w_fi, w_fo, hat1, slope, hat2),
        [WHOLE] * 6 + [ANY] * 5,
        [
            pltpu.VMEM(w_fi.shape[1:], BF16),
            pltpu.VMEM(w_fo.shape[1:], BF16),
            vm(hat1),
            vm(slope),
            vm(hat2),
            vm(outs[0]),
            vm(outs[1]),
            vm(outs[2]),
            vm(outs[3]),
            pltpu.SemaphoreType.DMA((9,)),
        ],
        after,
        16 * 10**9,
        22 * 10**6,
    )


def backward_attention_kernel(
    layer,
    scale,
    row_ref,
    seg_ref,
    lse_ref,
    w_in_hbm,
    w_out_hbm,
    qkv_hbm,
    mixed_hbm,
    branch_hbm,
    resid_hbm,
    d_qkv_hbm,
    d_x_ref,
    sums_ref,
    w_in,
    w_out,
    qkv,
    mixed,
    branch,
    d_resid,
    d_qkv,
    d_mix,
    code_q,
    code_k,
    delta_ref,
    probs_ref,
    ds_ref,
    sems,
):
    length, width = branch.shape
    copy = copier(sems)
    get_branch = copy(branch_hbm, branch, 0)
    get_out = copy(w_out_hbm.at[layer], w_out, 1)
    get_mixed = copy(mixed_hbm, mixed, 2)
    get_qkv = copy(qkv_hbm, qkv, 3)
    get_in = copy(w_in_hbm.at[layer], w_in, 4)
    get_resid = copy(resid_hbm, d_resid, 5)
    fill_codes(seg_ref, row_ref[0], code_q, code_k)
    probs_ref[...] = jnp.zeros_like(probs_ref)
    ds_ref[...] = jnp.zeros_like(ds_ref)
    sums_ref[...] = jnp.zeros_like(sums_ref)
    total = lambda value: jnp.sum(value.astype(F32), 0, keepdims=True)
    head_of = lax.broadcasted_iota(jnp.int32, (16, width), 1) // HEAD
    ones = (head_of == lax.broadcasted_iota(jnp.int32, (16, width), 0)).astype(F32).astype(BF16)
    get_branch.wait()
    get_out.wait()
    d_mix[...] = mm(branch[...], w_out[...], NT).astype(BF16)
    get_mixed.wait()
    product = d_mix[...].astype(F32) * mixed[...].astype(F32)
    high = product.astype(BF16)
    rest = (product - high.astype(F32)).astype(BF16)
    delta_ref[...] = mm(ones, high, NT) + mm(ones, rest, NT)

    get_qkv.wait()
    low_half = lax.broadcasted_iota(jnp.int32, (length, LANES), 1) < HEAD
    low_rows = lax.broadcasted_iota(jnp.int32, (LANES, length), 0) < HEAD

    def pair(number, carry):
        at = pl.multiple_of(number * LANES, LANES)
        cols = pl.ds(at, LANES)
        key_cols = pl.ds(at + width, LANES)
        value_cols = pl.ds(at + 2 * width, LANES)
        queries, keys, values, mix = qkv[:, cols], qkv[:, key_cols], qkv[:, value_cols], d_mix[:, cols]
        keys_t = keys.T
        d_query = jnp.zeros((LANES, length), F32)
        d_keys, d_values = [], []
        zero = jnp.zeros_like(keys)
        for sub in range(2):
            head = 2 * number + sub
            lse = lse_ref[pl.ds(head, 1), :]
            delta = delta_ref[pl.ds(head, 1), :]
            mine = low_half == (sub == 0)
            scores = mm(
                jnp.where(mine, keys, code_k[...]), jnp.where(mine, queries, code_q[...]), NT
            )
            d_probs = mm(jnp.where(mine, values, zero), mix, NT)
            for rows in chunks(length):
                start, stop = window(rows.start, length)
                probs = jnp.exp(scores[rows, start:stop] - lse[:, start:stop])
                probs_ref[sub, rows, start:stop] = probs.astype(BF16)
                ds_ref[sub, rows, start:stop] = (
                    probs * (d_probs[rows, start:stop] - delta[:, start:stop])
                ).astype(BF16)
            d_values.append(mm(probs_ref[sub], mix))
            d_keys.append(mm(ds_ref[sub], queries))
            mine_t = jnp.where(low_rows == (sub == 0), keys_t, jnp.zeros_like(keys_t))
            d_query += mm(mine_t, ds_ref[sub])
        dq = (d_query.T * scale).astype(BF16)
        d_qkv[:, cols] = dq
        sums_ref[1:2, cols] = total(dq)
        d_qkv[:, key_cols] = jnp.where(low_half, d_keys[0], d_keys[1]).astype(BF16)
        dv = jnp.where(low_half, d_values[0], d_values[1]).astype(BF16)
        d_qkv[:, value_cols] = dv
        sums_ref[1:2, key_cols] = total(dv)
        return carry

    lax.fori_loop(0, HEADS * HEAD // LANES, pair, 0)
    put_qkv = copy(d_qkv, d_qkv_hbm, 6)
    get_in.wait()
    get_resid.wait()
    d_x = mm(d_qkv[...], w_in[...], NT)
    for rows in chunks(length):
        d_x_ref[rows, :] = (d_resid[rows, :] + d_x[rows]).astype(BF16)
    put_qkv.wait()


def backward_attention(layer, row, seg, saved1, branch, d_resid, weights, after=()):
    qkv, lse, mixed = saved1[:3]
    w_in, _, w_out = weights[:3]
    ff = weights[6].shape[2]
    length, width = mixed.shape
    outs = (low(length, 3 * width), low(length, width), full(8, ff))
    return call(
        partial(backward_attention_kernel, layer, HEAD**-0.5),
        f"backward_attention{layer}",
        outs,
        (ANY, WHOLE, WHOLE),
        (row, seg, lse, w_in, w_out, qkv, mixed, branch, d_resid),
        [SCALAR, WHOLE, WHOLE] + [ANY] * 6,
        [
            pltpu.VMEM(w_in.shape[1:], BF16),
            pltpu.VMEM(w_out.shape[1:], BF16),
            vm(qkv),
            vm(mixed),
            vm(branch),
            vm(d_resid),
            vm(outs[0]),
            vm(outs[1]),
            pltpu.VMEM((length, LANES), BF16),
            pltpu.VMEM((length, LANES), BF16),
            pltpu.VMEM((16, length), F32),
            pltpu.VMEM((2, length, length), BF16),
            pltpu.VMEM((2, length, length), BF16),
            pltpu.SemaphoreType.DMA((7,)),
        ],
        after,
        20 * 10**9,
        16 * 10**6,
    )


def grad_cols_kernel(half_ref, *refs, rows, steps):
    lefts, rights = refs[:rows], refs[rows : 2 * rows]
    other_ref, own_ref, turned = refs[-3:]
    length = lefts[0].shape[0]
    step = pl.program_id(0)

    @pl.when(step == 0)
    def _():
        for number, left in enumerate(lefts):
            turned[:, number * length : (number + 1) * length] = left[...].T

    found = None
    for number, right in enumerate(rights):
        part = mm(turned[:, number * length : (number + 1) * length], right[...])
        found = part if found is None else found + part
    found = found.reshape(own_ref.shape).astype(BF16)

    @pl.when(step < steps)
    def _():
        other_ref[...] = found

    @pl.when(step >= steps)
    def _():
        own_ref[...] = found


def weight_grad_cols(half, lefts, rights, narrow, after=()):
    rows = len(lefts)
    length, width = lefts[0].shape
    cols = rights[0].shape[1] // 2
    tile = next((size for size in (768, 384) if cols % size == 0), cols)
    steps = cols // tile
    shape = jax.ShapeDtypeStruct((narrow, width // narrow, cols), BF16)
    block = (narrow, width // narrow, tile)

    def right_at(j, half):
        mine = jnp.where(j < steps, 1 - half[0], half[0])
        return (0, mine * steps + jnp.where(j < steps, j, j - steps))

    return pl.pallas_call(
        partial(grad_cols_kernel, rows=rows, steps=steps),
        out_shape=(shape, shape),
        grid_spec=pltpu.PrefetchScalarGridSpec(
            num_scalar_prefetch=1,
            grid=(2 * steps,),
            in_specs=[pl.BlockSpec((length, width), lambda j, half: (0, 0))] * rows
            + [pl.BlockSpec((length, tile), right_at)] * rows
            + [ANY] * len(after),
            out_specs=(
                pl.BlockSpec(block, lambda j, half: (0, 0, jnp.minimum(j, steps - 1))),
                pl.BlockSpec(block, lambda j, half: (0, 0, jnp.maximum(j - steps, 0))),
            ),
            scratch_shapes=[pltpu.VMEM((width, rows * length), BF16)],
        ),
        compiler_params=pltpu.CompilerParams(vmem_limit_bytes=LIMIT),
        cost_estimate=BRIEF,
        name="weight_grad_cols",
    )(half, *lefts, *rights, *after)


def grad_rows_kernel(half_ref, *refs, rows, narrow):
    lefts, rights = refs[:rows], refs[rows : 2 * rows]
    other_ref, own_ref = refs[-2:]
    unit = own_ref.shape[1]
    width = rights[0].shape[1]
    found = None
    for left, right in zip(lefts, rights):
        part = mm(left[...], right[...], TN)
        found = part if found is None else found + part
    found = found.astype(BF16)

    def write(ref):
        for block in range(ref.shape[2] // width):
            ref[0, :, block * width : (block + 1) * width] = found[
                block * unit : (block + 1) * unit
            ]

    @pl.when(pl.program_id(0) < narrow)
    def _():
        write(other_ref)

    @pl.when(pl.program_id(0) >= narrow)
    def _():
        write(own_ref)


def weight_grad_rows(half, lefts, rights, narrow, after=()):
    rows = len(lefts)
    length, deep = lefts[0].shape
    width = rights[0].shape[1]
    unit = width // narrow
    part = deep // narrow // 2
    cols = part // unit * width
    shape = jax.ShapeDtypeStruct((narrow, unit, cols), BF16)

    def left_at(j, half):
        first = j < narrow
        return (0, 2 * jnp.where(first, j, j - narrow) + jnp.where(first, 1 - half[0], half[0]))

    return pl.pallas_call(
        partial(grad_rows_kernel, rows=rows, narrow=narrow),
        out_shape=(shape, shape),
        grid_spec=pltpu.PrefetchScalarGridSpec(
            num_scalar_prefetch=1,
            grid=(2 * narrow,),
            in_specs=[pl.BlockSpec((length, part), left_at)] * rows
            + [pl.BlockSpec((length, width), lambda j, half: (0, 0))] * rows
            + [ANY] * len(after),
            out_specs=(
                pl.BlockSpec((1, unit, cols), lambda j, half: (jnp.minimum(j, narrow - 1), 0, 0)),
                pl.BlockSpec((1, unit, cols), lambda j, half: (jnp.maximum(j - narrow, 0), 0, 0)),
            ),
        ),
        compiler_params=pltpu.CompilerParams(vmem_limit_bytes=LIMIT),
        cost_estimate=BRIEF,
        name="weight_grad_rows",
    )(half, *lefts, *rights, *after)


def swap(value, bit):
    size = lax.axis_size("wide")
    return lax.ppermute(value, "wide", [(i, i ^ bit) for i in range(size)])


def tie(values, on):
    return lax.optimization_barrier((values, on))[0]


def add_low(left, right):
    return (left.astype(F32) + right.astype(F32)).astype(BF16)


def halves(value, side, axis):
    half = value.shape[axis] // 2
    keep = lax.dynamic_slice_in_dim(value, side * half, half, axis)
    give = lax.dynamic_slice_in_dim(value, (1 - side) * half, half, axis)
    return keep, give


def wide_bits():
    return [1 << i for i in range((lax.axis_size("wide") - 1).bit_length())]


def bit_order(turn):
    rest = wide_bits()[1:]
    return rest[::-1] if turn else rest


class Halving:
    def __init__(self, groups):
        self.place = lax.axis_index("wide")
        self.bits = list(zip(*(bit_order(turn) for turn in range(2))))
        self.groups = groups
        self.flying = None

    def step(self, on=None):
        if self.flying is not None:
            if on is not None:
                self.flying = [(keep, tie(recv, on)) for keep, recv in self.flying]
            self.groups = [[add_low(keep, recv)] for keep, recv in self.flying]
            self.flying = None
        if not self.bits:
            return [group[0] for group in self.groups]
        flying, gives = [], []
        for bit, group in zip(self.bits.pop(0), self.groups):
            split = [halves(part, (self.place // bit) % 2, 1) for part in group]
            keep = jnp.concatenate([pair[0] for pair in split], -1)
            give = jnp.concatenate([pair[1] for pair in split], -1)
            gives.append(give)
            flying.append((keep, swap(give, bit)))
        self.flying = flying
        return gives

    def finish(self, on=None):
        mine = self.step(on)
        while self.flying is not None:
            mine = self.step()
        return jnp.concatenate(mine, -1)


def narrow_parts(mine):
    return mine.reshape((2,) * (mine.shape[0].bit_length() - 1) + mine.shape[1:])


def narrow_level(cur, level, on=None):
    size = lax.axis_size("narrow")
    depth = size.bit_length() - 1
    bit = 1 << level
    keep, give = halves(cur, (lax.axis_index("narrow") // bit) % 2, depth - 1 - level)
    recv = lax.ppermute(give, "narrow", [(i, i ^ bit) for i in range(size)])
    if on is not None:
        recv = tie(recv, on)
    return add_low(keep, recv)


def narrow_sum_swaps(mine, ons=()):
    cur = narrow_parts(mine)
    for level in range(lax.axis_size("narrow").bit_length() - 1):
        cur = narrow_level(cur, level, ons[level] if level < len(ons) else None)
    return cur.reshape(mine.shape[1:])


def wide_gather_swaps(mine, got=None):
    place = lax.axis_index("wide")
    cur = mine[None]
    for number, bit in enumerate(wide_bits()[::-1]):
        other = got[None] if number == 0 and got is not None else swap(cur, bit)
        upper = (place // bit) % 2 == 1
        cur = jnp.stack([jnp.where(upper, other, cur), jnp.where(upper, cur, other)])
        cur = cur.reshape((-1,) + mine.shape)
    return cur


def narrow_sum(mine):
    return lax.psum_scatter(mine, "narrow", scatter_dimension=0, tiled=True)[0]


def small_pack_kernel(smalls, *refs):
    small_refs, sums_refs = refs[:smalls], refs[smalls:-4]
    out_ref, small, sums, rest = refs[-4:]
    _, narrow, unit, lanes = out_ref.shape
    width = narrow * unit
    stu = lanes
    share = stu // narrow
    deep = sums.shape[1]
    small[...] = sum(ref[...] for ref in small_refs)
    sums[...] = sum(ref[...] for ref in sums_refs)
    own = width + 2 * stu
    vectors = [
        (sums, 1, 0, 2 * width),
        (sums, 2, 2 * width, width),
        (sums, 1, 2 * width, 2 * width),
        (sums, 2, 0, 2 * width),
        (sums, 0, 0, deep),
        (sums, 2, 3 * width, width),
        (small, own, 0, stu),
        (small, own + 1, 0, stu),
        (small, own + 2, 0, stu),
    ]
    for place in range(narrow):
        out_ref[0, place] = small[place * unit : (place + 1) * unit, :].astype(BF16)
        rest[...] = jnp.zeros_like(rest)
        for number in range(2):
            start = width + number * stu + place * share
            rest[number * share : (number + 1) * share, :] = small[start : start + share, :]
        row = 2 * share
        for ref, line, start, size in vectors:
            size = size // narrow
            value = ref[line : line + 1, :][:, start + place * size : start + (place + 1) * size]
            for at in range(0, size, lanes):
                part = min(lanes, size - at)
                rest[row : row + 1, :part] = value[:, at : at + part]
                row += 1
        rest[row : row + 1, :] = small[own + 3 : own + 4, :]
        out_ref[1, place] = rest[...].astype(BF16)


def small_pack(smalls, sums, narrow):
    stu = smalls[0].shape[1]
    width = smalls[0].shape[0] - 2 * stu - 8
    unit = width // narrow
    return pl.pallas_call(
        partial(small_pack_kernel, len(smalls)),
        out_shape=low(2, narrow, unit, stu),
        in_specs=[WHOLE] * (len(smalls) + len(sums)),
        out_specs=WHOLE,
        scratch_shapes=[vm(smalls[0]), vm(sums[0]), pltpu.VMEM((unit, stu), F32)],
        cost_estimate=BRIEF,
        name="small_pack",
    )(*smalls, *sums)


def place_rows(orders, place, rows):
    found = []
    for order in orders:
        at = 0
        for bit in order:
            at = 2 * at + (place // bit) % 2
        found.append(at * rows)
    return found


def turn_bits(place, total):
    count = (total - 1).bit_length()
    return sum(((place >> i) & 1) << (count - 1 - i) for i in range(count))


def place_ff_kernel(layer, orders, turned, held, got_ref, *refs):
    outs = refs[held : held + 3]
    fi, fo, ao, sems = refs[held + 3 :]
    unit, deep = fi.shape
    width = ao.shape[1]
    half = width // 2
    total, rows, _ = got_ref.shape
    blocks = fo.shape[0] // unit // 2
    for place in range(total):
        core = place % 2
        x_at, y_at = place_rows(orders, place, rows)
        at = turn_bits(place, total) if turned else place
        get = lambda start, size, at=at: got_ref[at, :, start : start + size].astype(F32)
        fi[x_at : x_at + rows, core * deep // 2 : (core + 1) * deep // 2] = get(0, deep // 2)
        for block in range(blocks):
            at = (core * blocks + block) * unit + y_at
            fo[at : at + rows, :] = get(deep // 2 + block * width, width)
        ao[y_at : y_at + rows, core * half : (core + 1) * half] = get(deep, half)
    puts = []
    for number, (src, dst) in enumerate(zip((fi, fo, ao), outs)):
        puts.append(pltpu.make_async_copy(src, dst.at[layer], sems.at[number]))
        puts[-1].start()
    for made in puts:
        made.wait()


def place_attn_kernel(layer, orders, held, got_ref, *refs):
    out, small = refs[held], refs[held + 1]
    ai, sem = refs[held + 2 :]
    total, rows, cols = got_ref.shape
    half = ai.shape[1] // 2
    cut = cols // 2
    rest = half - cut
    for place in range(total):
        core = place % 2
        x_at, y_at = place_rows(orders, place, rows)
        at = turn_bits(place, total)
        get = lambda start, size: got_ref[at, :, start : start + size].astype(F32)
        start = core * half
        ai[x_at : x_at + rows, start : start + cut] = get(0, cut)
        ai[y_at : y_at + rows, start + cut : start + half] = get(cut, rest)
        small[y_at : y_at + rows, core * LANES : (core + 1) * LANES] = get(cut + rest, LANES)
    made = pltpu.make_async_copy(ai, out.at[layer], sem)
    made.start()
    made.wait()


def place_ff(layer, got, turned, shapes, previous=()):
    held = len(previous)
    return pl.pallas_call(
        partial(place_ff_kernel, layer, [bit_order(turn) for turn in range(2)], turned, held),
        out_shape=tuple(shapes),
        in_specs=[WHOLE] + [ANY] * held,
        out_specs=(ANY,) * 3,
        scratch_shapes=[pltpu.VMEM(shape.shape[1:], F32) for shape in shapes]
        + [pltpu.SemaphoreType.DMA((3,))],
        input_output_aliases={1 + i: i for i in range(held)},
        compiler_params=pltpu.CompilerParams(vmem_limit_bytes=LIMIT),
        cost_estimate=pl.CostEstimate(flops=10**6, bytes_accessed=8 * 10**6, transcendentals=0),
        name=f"place_ff{layer}",
    )(got, *previous)


def place_attn(layer, got, shape, previous=(), after=()):
    held = len(previous)

    def body(got_ref, *refs):
        kept = refs[:held] + refs[held + len(after) :]
        place_attn_kernel(layer, orders, held, got_ref, *kept)

    orders = [bit_order(turn) for turn in range(2)]
    return pl.pallas_call(
        body,
        out_shape=(shape, full(shape.shape[1], 2 * LANES)),
        in_specs=[WHOLE] + [ANY] * (held + len(after)),
        out_specs=(ANY, WHOLE),
        scratch_shapes=[pltpu.VMEM(shape.shape[1:], F32), pltpu.SemaphoreType.DMA],
        input_output_aliases={1 + i: i for i in range(held)},
        compiler_params=pltpu.CompilerParams(vmem_limit_bytes=LIMIT),
        cost_estimate=pl.CostEstimate(flops=10**6, bytes_accessed=3 * 10**6, transcendentals=0),
        name=f"place_attn{layer}",
    )(got, *previous, *after)


def place_small_kernel(first_ref, second_ref, proj_ref, dense_ref, cls_ref, *vec_refs):
    for layer, ref in enumerate((first_ref, second_ref)):
        stu = dense_ref.shape[1]
        proj_ref[layer] = ref[:, :LANES]
        dense_ref[layer] = ref[:stu, LANES:]
        cls_ref[layer] = ref[stu : 2 * stu, LANES : LANES + cls_ref.shape[2]]
        row = 2 * stu
        for out in vec_refs:
            size = out.shape[1]
            for start in range(0, size, LANES):
                part = min(LANES, size - start)
                out[layer : layer + 1, start : start + part] = ref[
                    row : row + 1, LANES : LANES + part
                ]
                row += 1


def place_small(first, second, width, deep, classes, narrow):
    sizes = [2 * width, width, 2 * width, 2 * width, deep, width, LANES, LANES, LANES]
    stu = LANES // narrow
    outs = (
        full(2, width // narrow, LANES),
        full(2, stu, LANES),
        full(2, stu, classes),
    ) + tuple(full(2, size // narrow) for size in sizes)
    return pl.pallas_call(
        place_small_kernel,
        out_shape=outs + (full(2, classes),),
        in_specs=[WHOLE, WHOLE],
        out_specs=(WHOLE,) * 13,
        name="place_small",
    )(first, second)


def route_kernel(me_ref, *refs):
    around, out_ref, held = refs[:-2], refs[-2], refs[-1]
    me, size = me_ref[0], len(around)
    for step, ref in enumerate(around):
        held[lax.rem(me + (size - step), size)] = ref[0]
    counts = [held[i] for i in range(size)]
    flow, before = [], []
    total = jnp.int32(0)
    for value in counts:
        before.append(total)
        total = total + value - 1
        flow.append(total)
    right1 = [(f >= 1) & (c >= 1) for f, c in zip(flow, counts)]
    left1 = [(f <= -1) & (c >= 1) for f, c in zip(before, counts)]
    right2 = [(f >= 1) & ((f >= 2) | (c == 0)) for f, c in zip(flow, counts)]
    left2 = [(f <= -1) & ((f <= -2) | (c == 0)) for f, c in zip(before, counts)]

    def at(values, shift):
        found = jnp.int32(0)
        for i, value in enumerate(values):
            found = jnp.where(me + shift == i, value.astype(jnp.int32), found)
        return found

    count = at(counts, 0)
    from_left2, from_right2 = at(right2, -1), at(left2, 1)
    sent_right, sent_left = at(right1, 0), at(left1, 0)
    results = (
        at(right1, -1),
        from_left2,
        from_left2 | from_right2,
        (count == 2).astype(jnp.int32),
        ((count == 1) & (sent_right + sent_left == 0)).astype(jnp.int32),
        at(right2, 0),
        sent_left,
        (sent_right & at(right2, 1)) | (sent_left & at(left2, -1)),
        (count >= 1).astype(jnp.int32),
        (count >= 2).astype(jnp.int32),
    )
    for i, value in enumerate(results):
        out_ref[i] = value
    for i in range(len(results), out_ref.shape[0]):
        out_ref[i] = 0


def route(me, around):
    return pl.pallas_call(
        route_kernel,
        out_shape=jax.ShapeDtypeStruct((16,), jnp.int32),
        in_specs=[SCALAR] * (1 + len(around)),
        out_specs=SCALAR,
        scratch_shapes=[pltpu.SMEM((len(around),), jnp.int32)],
        name="route",
    )(me, *around)


def shards(
    tokens,
    segments,
    exit_layer,
    attn_in,
    qv_bias,
    attn_out,
    out_bias,
    ln_gain,
    ln_bias,
    ff_in,
    ff_in_bias,
    ff_out,
    ff_out_bias,
    stu_proj,
    stu_bias,
    pool_query,
    stu_dense,
    stu_dense_bias,
    stu_cls,
    stu_cls_bias,
    out_cot,
    logit_cot,
):
    row_count, length, width = tokens.shape
    classes = stu_cls.shape[-1]
    blank = LANES - classes
    narrow = lax.axis_size("narrow")
    me = lax.axis_index("narrow")
    core = lax.axis_index("wide") % 2
    weights = (
        attn_in,
        qv_bias,
        attn_out,
        out_bias,
        ln_gain,
        ln_bias,
        ff_in,
        ff_in_bias,
        ff_out,
        ff_out_bias,
        stu_proj,
        stu_bias,
        pool_query,
        stu_dense,
        stu_dense_bias,
        jnp.pad(stu_cls, ((0, 0), (0, 0), (0, blank))),
        jnp.pad(stu_cls_bias, ((0, 0), (0, blank))),
    )
    wide_cot = jnp.pad(logit_cot.astype(F32), ((0, 0), (0, 0), (0, blank)))

    alive = exit_layer == 1
    row_a = jnp.where(alive[0], 0, jnp.where(alive[1], 1, 0)).astype(jnp.int32)
    row_b = 1 - row_a

    index = lambda row: row.reshape(1)
    first_row = jnp.zeros((1,), jnp.int32)
    own = index(core)
    ia, ib = index(row_a), index(row_b)
    early_cot, late_cot = wide_cot[:, 0], wide_cot[:, 1]
    a1 = forward_attention(0, ia, tokens, segments, weights)

    mine = tie(jnp.sum(alive.astype(jnp.int32)).reshape(1), a1[4])
    around = [mine] + [
        lax.ppermute(mine, "narrow", [(i, (i + step) % narrow) for i in range(narrow)])
        for step in range(1, narrow)
    ]
    flags = route(me.reshape(1), around)
    from_left1, from_left2, use_two, use_b, use_a, on_right, sent_left, is_far, a_alive, b_alive = (
        flags[i] == 1 for i in range(10)
    )

    even = me % 2 == 0
    inner = [(i, i ^ 1) for i in range(narrow)]
    outer = []
    for i in range(lax.axis_size("wide") * narrow):
        place, line = i // narrow, i % narrow
        other = ((line + 1) ^ 1) - 1
        inside = 0 <= other < narrow
        outer.append((i, place * narrow + other if inside else (place ^ 1) * narrow + line))

    def shift(value):
        return (
            lax.ppermute(value, "narrow", inner),
            lax.ppermute(value, ("wide", "narrow"), outer),
        )

    def pick(pair, is_left):
        return jnp.where(is_left == even, pair[1], pair[0])

    def out_one(pair):
        return pick(pair, from_left1)

    def out_two(pair, one, own_a, own_b):
        two = pick(pair, from_left2)
        return jnp.where(use_b, own_b, jnp.where(use_a, own_a, jnp.where(use_two, two, one)))

    def back_one(pair):
        return pick(pair, ~on_right)

    def back_two(value, pair, pair2):
        return jnp.where(
            use_a, value, jnp.where(is_far, pick(pair2, sent_left), pick(pair, sent_left))
        )

    def row_of(value, row):
        return lax.dynamic_index_in_dim(value, row, 0, False)

    cot_a, cot_b = row_of(out_cot, row_a), row_of(out_cot, row_b)
    pair = shift(tie(cot_a, a1[4]))
    a2 = forward_ff(0, ia, a1[4], a1[5], early_cot, segments, late_cot, weights, (cot_a,))
    cot_one = out_one(tie(pair, a2[3]))
    pair = shift(a2[3])
    b1 = forward_attention(0, ib, tokens, segments, weights, (a2[3], cot_one))
    one = out_one(tie(pair, b1[4]))
    pair = shift(one)
    b2 = forward_ff(0, ib, b1[4], b1[5], early_cot, segments, late_cot, weights, (one,))
    work_in = out_two(tie(pair, b2[3]), one, a2[3], b2[3])
    work_seg = work_in[length + 1 : length + 2, :length].astype(jnp.int32)
    work_late = work_in[length + 2 : length + 3, :LANES].astype(F32)

    pair = shift(tie(cot_one, b2[3]))
    w1 = forward_attention(1, first_row, work_in[None], work_seg, weights)
    work_cot = out_two(tie(pair, w1[4]), cot_one, cot_a, cot_b)
    w2 = forward_ff(
        1, first_row, w1[4], w1[5], work_late, work_seg, work_late, weights, (work_cot,)
    )
    sent_h = w2[3]
    pair_h = shift(sent_h)
    w3 = backward_ff(1, work_cot, w1, w2, weights, (sent_h,))

    def ff_jobs(saved1, saved2, back):
        first = [s[4] for s in saved1]
        mixed = [s[2] for s in saved1]
        active = [s[1] for s in saved2]
        second, inner, branch = ([b[i] for b in back] for i in range(3))
        return (
            (weight_grad_cols, first, inner),
            (weight_grad_rows, active, second),
            (weight_grad_cols, mixed, branch),
        )

    def weight_grads(jobs, after=()):
        return [job(own, lefts, rights, narrow, after) for job, lefts, rights in jobs]

    def core_sum(pairs, on=None):
        received = [swap(other, 1) for other, _ in pairs]
        if on is not None:
            received = tie(received, on)
        return [add_low(mine, recv) for (_, mine), recv in zip(pairs, received)]

    def ff_halving(parts):
        return Halving([[parts[0]], [parts[1], parts[2]]])

    def attn_halving(part, small):
        keep, give = halves(small, core, 0)
        small = add_low(keep, swap(give, 1))[0]
        cut = (part.shape[-1] + LANES) // 2
        return Halving([[part[..., :cut]], [part[..., cut:], small]])

    halves1 = weight_grads(ff_jobs([w1], [w2], [w3]))
    sent = tuple(pair[0] for pair in halves1)
    w4 = backward_attention(1, first_row, work_seg, w1, w3[2], w3[3], weights, sent)
    pair_x = shift(w4[1])
    ff1 = ff_halving(core_sum(halves1))
    flying = ff1.step()
    half1 = weight_grads(((weight_grad_cols, [work_in[:length]], [w4[0]]),), tuple(flying))
    small1 = small_pack([w2[6]], [w3[4], w4[2]], narrow)
    forth_x = back_one(tie(pair_x, half1[0][0]))
    pair_x2 = shift(forth_x)

    base_b = jnp.where(b_alive, w4[1], row_of(out_cot, row_b))
    b3 = backward_ff(0, base_b, b1, b2, weights, (half1[0][0], forth_x, small1))
    far_x = back_two(w4[1], pair_x, tie(pair_x2, b3[2]))
    forth_h = back_one(tie(pair_h, far_x))
    pair_h2 = shift(forth_h)
    at1 = attn_halving(core_sum(half1)[0], small1)
    flying = at1.step() + ff1.step(b3[2])
    base_a = jnp.where(a_alive, far_x, row_of(out_cot, row_a))
    a3 = backward_ff(0, base_a, a1, a2, weights, (*flying, forth_h))
    mine_ff1 = ff1.finish(a3[2])
    flying = at1.step(a3[2])
    halves0 = weight_grads(ff_jobs([a1, b1], [a2, b2], [a3, b3]), (mine_ff1, *flying))
    ff0 = ff_halving(core_sum(halves0))
    flying = ff0.step()
    far_h = back_two(sent_h, pair_h, tie(pair_h2, a3[2]))
    b4 = backward_attention(
        0, ib, segments, b1, b3[2], b3[3], weights, (*flying, far_h)
    )
    flying = ff0.step(b4[1])
    sum_at1 = narrow_sum(at1.finish(b4[1]))
    a4 = backward_attention(0, ia, segments, a1, a3[2], a3[3], weights, (b4[1], *flying))
    mine_ff0 = ff0.finish(a4[1])
    sum_ff1 = narrow_sum_swaps(mine_ff1, (b4[1], a4[1]))
    half0 = weight_grads(
        (
            (
                weight_grad_cols,
                [row_of(tokens, row_a), row_of(tokens, row_b)],
                [a4[0], b4[0]],
            ),
        ),
        (mine_ff0, sum_ff1),
    )
    part_ff0 = narrow_level(narrow_parts(mine_ff0), 0, half0[0][0])
    got_ff1 = tie(swap(tie(sum_ff1, mine_ff0), wide_bits()[-1]), half0[0][0])
    half0 = [(tie(half0[0][0], (part_ff0, got_ff1)), half0[0][1])]
    all_ff1 = wide_gather_swaps(sum_ff1, got_ff1)
    small0 = small_pack([a2[6], b2[6]], [a3[4], b3[4], a4[2], b4[2]], narrow)
    for level in range(1, narrow.bit_length() - 1):
        part_ff0 = narrow_level(part_ff0, level, small0)
    sum_ff0 = part_ff0.reshape(mine_ff0.shape[1:])
    at0 = attn_halving(core_sum(half0)[0], small0)
    flying = at0.step()
    all_ff0 = lax.all_gather(sum_ff0, "wide", axis=0, tiled=False)
    all_at1 = wide_gather_swaps(tie(sum_at1, flying))
    all_at0 = wide_gather_swaps(narrow_sum_swaps(at0.finish(), (None, all_ff0)))

    deep = ff_in.shape[2]
    unit = width // narrow
    shapes = [full(2, unit, deep), full(2, deep // narrow, width), full(2, unit, width)]
    attn_shape = full(2, unit, 3 * width)
    placed = place_ff(1, all_ff1, True, shapes)
    d_attn_in, small1 = place_attn(1, all_at1, attn_shape)
    placed = place_ff(0, all_ff0, False, shapes, placed)
    d_attn_in, small0 = place_attn(0, all_at0, attn_shape, (d_attn_in,), (placed[2],))
    d_ff_in, d_ff_out, d_attn_out = placed
    (d_proj, d_dense, d_cls, d_qv, d_out_b, d_gain, d_shift, d_fi_b, d_fo_b, *rest) = place_small(
        small0, small1, width, deep, classes, narrow
    )
    d_stu_b, d_query, d_dense_b, d_cls_b = rest
    totals = (
        d_attn_in,
        d_qv,
        d_attn_out,
        d_out_b,
        d_gain,
        d_shift,
        d_ff_in,
        d_fi_b,
        d_ff_out,
        d_fo_b,
        d_proj,
        d_stu_b,
        d_query,
        d_dense,
        d_dense_b,
        d_cls,
        d_cls_b,
    )

    in_order = lambda for_a, for_b: jnp.where(
        row_a == 0, jnp.stack([for_a, for_b]), jnp.stack([for_b, for_a])
    )
    act_a = jnp.where(a_alive, far_h, a2[3])
    act_b = jnp.where(b_alive, w2[3], b2[3])
    cut = lambda value: value[length, :classes]
    logits = jnp.where(jnp.stack([a_alive, b_alive])[:, None], jnp.stack([cut(act_a), cut(act_b)]), 0)
    early = in_order(cut(a2[3]), cut(b2[3]))
    logits = jnp.stack([early, in_order(logits[0], logits[1])], 1).astype(BF16)
    act_a, act_b = act_a[:length], act_b[:length]
    return (in_order(act_a, act_b), logits, in_order(a4[1], b4[1])) + totals


def solution(mesh):
    rows = ("wide", "narrow")
    return jax.shard_map(
        shards,
        mesh=mesh,
        in_specs=(P(rows, None, None), P(rows, None), P(rows))
        + (P(),) * 17
        + (P(rows, None, None), P(rows, None, None)),
        out_specs=(P(rows, None, None),) * 3
        + (
            P(None, "narrow", None),
            P(None, "narrow"),
            P(None, "narrow", None),
            P(None, "narrow"),
            P(None, "narrow"),
            P(None, "narrow"),
            P(None, "narrow", None),
            P(None, "narrow"),
            P(None, "narrow", None),
            P(None, "narrow"),
            P(None, "narrow", None),
            P(None, "narrow"),
            P(None, "narrow"),
            P(None, "narrow", None),
            P(None, "narrow"),
            P(None, "narrow", None),
            P(),
        ),
        check_vma=False,
    )
```

```python
from functools import partial

import jax
import jax.numpy as jnp
import numpy as np
from jax import lax
from jax.experimental import pallas as pl
from jax.experimental.pallas import tpu as pltpu
from jax.sharding import PartitionSpec as P

HEADS = 12
HEAD = 64
STU_HEADS = 2
LANES = 128
CHUNK = 128
REACH = 256
EPS = 1e-12
MASKED = -1e30
SEGMENTS = 4
HIGH = lax.Precision.HIGHEST
F32 = jnp.float32
BF16 = jnp.bfloat16
LIMIT = 52 * 1024 * 1024
BRIEF = pl.CostEstimate(flops=10**6, bytes_accessed=10**5, transcendentals=0)

NN = (((1,), (0,)), ((), ()))
NT = (((1,), (1,)), ((), ()))
TN = (((0,), (0,)), ((), ()))


def mm(left, right, dims=NN):
    return lax.dot_general(left, right, dims, preferred_element_type=F32)


def mm_high(left, right, dims=NN):
    return lax.dot_general(left, right, dims, precision=HIGH, preferred_element_type=F32)


def vec(ref, layer, start, size):
    return ref[...].astype(F32)[layer : layer + 1, start : start + size]


def gelu_pair(value):
    dist = jnp.abs(value) * (0.5**0.5)
    den = 1.0 + 0.3275911 * dist
    part = pl.reciprocal(den, approx=True)
    part = part * (2.0 - den * part)
    series = 0.5 * 1.061405429
    for term in (-1.453152027, 1.421413741, -0.284496736, 0.254829592):
        series = series * part + 0.5 * term
    bell = jnp.exp(-(dist * dist))
    tail = series * part * bell
    below = jnp.where(value >= 0, 1.0 - tail, tail)
    return value * below, below + value * bell * ((2.0 * np.pi) ** -0.5)


def row_norm(value):
    mean = jnp.mean(value, -1, keepdims=True)
    centered = value - mean
    spread = lax.rsqrt(jnp.mean(centered * centered, -1, keepdims=True) + EPS)
    return centered * spread, spread


def norm_back(grad, hat, spread, gain):
    scaled = grad * gain
    low = jnp.mean(scaled, -1, keepdims=True)
    high = jnp.mean(scaled * hat, -1, keepdims=True)
    return spread * (scaled - low - hat * high)


def window(place, length):
    start = max(0, (place - REACH + 1) // CHUNK * CHUNK)
    stop = min(length, -(-(place + CHUNK + REACH - 1) // CHUNK) * CHUNK)
    return start, stop


def fill_codes(seg_ref, row, code_q, code_k):
    length = code_q.shape[0]
    seg_row = seg_ref[pl.ds(row, 1), :].astype(F32)
    seg_cols = jnp.broadcast_to(seg_row, (LANES, length)).T
    lane = lax.broadcasted_iota(jnp.int32, (length, LANES), 1) % HEAD
    same = seg_cols == lane.astype(F32)
    code_q[...] = jnp.where(same, 1.0, 0.0).astype(BF16)
    code_k[...] = jnp.where(same | (lane >= SEGMENTS), 0.0, MASKED).astype(BF16)


ANY = pl.BlockSpec(memory_space=pl.ANY)
WHOLE = pl.BlockSpec(memory_space=pltpu.VMEM)
SCALAR = pl.BlockSpec(memory_space=pltpu.SMEM)


def low(*shape):
    return jax.ShapeDtypeStruct(shape, BF16)


def full(*shape):
    return jax.ShapeDtypeStruct(shape, F32)


def vm(like):
    return pltpu.VMEM(like.shape, like.dtype)


def call(kernel, name, outs, out_specs, inputs, in_specs, scratch, after, flops, moved):
    count, extra = len(inputs), len(after)

    def body(*refs):
        kernel(*refs[:count], *refs[count + extra :])

    return pl.pallas_call(
        body,
        out_shape=outs,
        in_specs=list(in_specs) + [ANY] * extra,
        out_specs=out_specs,
        scratch_shapes=scratch,
        compiler_params=pltpu.CompilerParams(vmem_limit_bytes=LIMIT),
        cost_estimate=pl.CostEstimate(flops=flops, bytes_accessed=moved, transcendentals=0),
        name=name,
    )(*inputs, *after)


def copier(sems):
    def copy(src, dst, number):
        made = pltpu.make_async_copy(src, dst, sems.at[number])
        made.start()
        return made

    return copy


def chunks(length):
    return [slice(place, place + CHUNK) for place in range(0, length, CHUNK)]


def forward_attention_kernel(
    layer,
    scale,
    row_ref,
    x_hbm,
    seg_ref,
    w_in_hbm,
    w_out_hbm,
    qv_ref,
    out_b_ref,
    gain_ref,
    shift_ref,
    qkv_hbm,
    lse_ref,
    mixed_hbm,
    hat_hbm,
    first_hbm,
    full_hbm,
    spread_ref,
    x_ref,
    w_in,
    w_out,
    qkv,
    mixed,
    hat,
    first,
    full,
    code_q,
    code_k,
    terms_ref,
    sems,
):
    row = row_ref[0]
    length, width = x_ref.shape
    copy = copier(sems)
    get_x = copy(x_hbm.at[row, pl.ds(0, length)], x_ref, 0)
    get_in = copy(w_in_hbm.at[layer], w_in, 1)
    get_out = copy(w_out_hbm.at[layer], w_out, 2)
    fill_codes(seg_ref, row, code_q, code_k)
    terms_ref[...] = jnp.zeros_like(terms_ref)
    lse_ref[...] = jnp.zeros_like(lse_ref)
    get_x.wait()
    get_in.wait()

    x = x_ref[...]
    qkv[:, :width] = (
        (mm(x, w_in[:, :width]) + vec(qv_ref, layer, 0, width)).astype(BF16).astype(F32) * scale
    ).astype(BF16)
    qkv[:, width : 2 * width] = mm(x, w_in[:, width : 2 * width]).astype(BF16)
    qkv[:, 2 * width :] = (
        mm(x, w_in[:, 2 * width :]) + vec(qv_ref, layer, width, width)
    ).astype(BF16)
    put_qkv = copy(qkv, qkv_hbm, 3)

    low_half = lax.broadcasted_iota(jnp.int32, (length, LANES), 1) < HEAD
    low_rows = lax.broadcasted_iota(jnp.int32, (LANES, length), 0) < HEAD

    def pair(number, carry):
        at = pl.multiple_of(number * LANES, LANES)
        queries = qkv[:, pl.ds(at, LANES)]
        keys = qkv[:, pl.ds(at + width, LANES)]
        values_t = qkv[:, pl.ds(at + 2 * width, LANES)].T
        outs = []
        for sub in range(2):
            mine = low_half == (sub == 0)
            scores = mm(
                jnp.where(mine, keys, code_k[...]), jnp.where(mine, queries, code_q[...]), NT
            )
            tops = []
            for cols in chunks(length):
                start, stop = window(cols.start, length)
                part = scores[start:stop, cols]
                top = jnp.max(part, 0, keepdims=True)
                terms_ref[sub, start:stop, cols] = jnp.exp(part - top).astype(BF16)
                tops.append(top)
            mine_t = jnp.where(low_rows == (sub == 0), values_t, jnp.ones_like(values_t))
            product = mm(mine_t, terms_ref[sub])
            beside = HEAD * (1 - sub)
            total = product[beside : beside + 1, :]
            lse_ref[pl.ds(2 * number + sub, 1), :] = jnp.concatenate(tops, 1) + jnp.log(total)
            outs.append(product * (1.0 / total))
        mixed[:, pl.ds(at, LANES)] = jnp.where(low_rows, outs[0], outs[1]).T.astype(BF16)
        return carry

    lax.fori_loop(0, HEADS * HEAD // LANES, pair, 0)
    put_mixed = copy(mixed, mixed_hbm, 4)

    get_out.wait()
    gain, shift = vec(gain_ref, layer, 0, width), vec(shift_ref, layer, 0, width)
    out_b = vec(out_b_ref, layer, 0, width)
    branch = mm(mixed[...], w_out[...])
    for rows in chunks(length):
        normed, spread = row_norm(x_ref[rows, :].astype(F32) + branch[rows] + out_b)
        hat[rows, :] = normed.astype(BF16)
        normed = normed * gain + shift
        full[rows, :] = normed
        first[rows, :] = normed.astype(BF16)
        spread_ref[rows, :] = jnp.broadcast_to(spread, (CHUNK, LANES))
    puts = (copy(hat, hat_hbm, 5), copy(first, first_hbm, 6), copy(full, full_hbm, 7))
    for made in (put_qkv, put_mixed) + puts:
        made.wait()


def forward_attention(layer, row, x, seg, weights, after=()):
    w_in, qv, w_out, out_b, gain, shift = weights[:6]
    length, width = seg.shape[-1], x.shape[-1]
    outs = (
        low(length, 3 * width),
        full(16, length),
        low(length, width),
        low(length, width),
        low(length, width),
        full(length, width),
        full(length, LANES),
    )
    return call(
        partial(forward_attention_kernel, layer, HEAD**-0.5),
        f"forward_attention{layer}",
        outs,
        (ANY, WHOLE) + (ANY,) * 4 + (WHOLE,),
        (row, x, seg, w_in, w_out, qv, out_b, gain, shift),
        [SCALAR, ANY, WHOLE, ANY, ANY] + [WHOLE] * 4,
        [
            pltpu.VMEM((length, width), BF16),
            pltpu.VMEM(w_in.shape[1:], BF16),
            pltpu.VMEM(w_out.shape[1:], BF16),
            vm(outs[0]),
            vm(outs[2]),
            vm(outs[3]),
            vm(outs[4]),
            vm(outs[5]),
            pltpu.VMEM((length, LANES), BF16),
            pltpu.VMEM((length, LANES), BF16),
            pltpu.VMEM((2, length, length), BF16),
            pltpu.SemaphoreType.DMA((8,)),
        ],
        after,
        14 * 10**9,
        16 * 10**6,
    )


def forward_ff_kernel(
    layer,
    row_ref,
    first_hbm,
    full_hbm,
    cot_ref,
    seg_ref,
    later_ref,
    w_fi_hbm,
    w_fo_hbm,
    gain_ref,
    shift_ref,
    fi_b_ref,
    fo_b_ref,
    proj_ref,
    proj_b_ref,
    query_ref,
    dense_ref,
    dense_b_ref,
    cls_ref,
    cls_b_ref,
    slope_hbm,
    active_hbm,
    hat_hbm,
    h_hbm,
    spread_ref,
    d_upper_ref,
    small_ref,
    first,
    full,
    w_fi,
    w_fo,
    slope,
    active,
    hat,
    h,
    even,
    odd,
    sems,
):
    length, width = first.shape
    ff = w_fi.shape[1]
    copy = copier(sems)
    get_first = copy(first_hbm, first, 0)
    part = even.shape[1]
    get_fi = [
        copy(w_fi_hbm.at[layer, :, pl.ds(at, part)], w_fi.at[:, pl.ds(at, part)], 8 + at // part)
        for at in range(0, ff, part)
    ]
    get_full = copy(full_hbm, full, 2)
    get_fo = copy(w_fo_hbm.at[layer], w_fo, 3)
    get_first.wait()
    get_fi[0].wait()

    def multiply(at, into):
        into[...] = mm(first[...], w_fi[:, pl.ds(at, part)])

    def bend(at, source):
        bias_part = fi_b_ref[:, pl.ds(at, part)].astype(F32)[layer : layer + 1]
        for rows in chunks(length):
            out, grad = gelu_pair(source[rows, :] + bias_part)
            active[rows, pl.ds(at, part)] = out.astype(BF16)
            slope[rows, pl.ds(at, part)] = grad.astype(BF16)

    multiply(0, even)
    for made in get_fi[1:]:
        made.wait()
    steps = ff // part // 2

    def inner(number, carry):
        at = pl.multiple_of(number * (2 * part), 2 * part)
        multiply(at + part, odd)
        bend(at, even)
        later = pl.multiple_of(jnp.minimum(at + 2 * part, ff - part), part)
        multiply(later, even)
        bend(at + part, odd)
        return carry

    lax.fori_loop(0, steps, inner, 0)
    put_slope = copy(slope, slope_hbm, 4)
    put_active = copy(active, active_hbm, 5)

    get_fo.wait()
    get_full.wait()
    gain, shift = vec(gain_ref, layer, width, width), vec(shift_ref, layer, width, width)
    fo_b = vec(fo_b_ref, layer, 0, width)
    second = mm(active[...], w_fo[...])
    for rows in chunks(length):
        normed, spread = row_norm(full[rows, :] + second[rows] + fo_b)
        hat[rows, :] = normed.astype(BF16)
        h[rows, :] = (normed * gain + shift).astype(BF16)
        spread_ref[rows, :] = jnp.broadcast_to(spread, (CHUNK, LANES))
    put_hat = copy(hat, hat_hbm, 6)

    stu_width = proj_ref.shape[2]
    stu_scale = (stu_width // STU_HEADS) ** -0.5
    hidden = h[:length, :]
    upper = mm(hidden, proj_ref[layer]) + vec(proj_b_ref, layer, 0, stu_width)
    query = vec(query_ref, layer, 0, stu_width)
    lane_full = lax.broadcasted_iota(jnp.int32, (length, stu_width), 1)
    left = lane_full < stu_width // STU_HEADS

    def both(value):
        zero = jnp.zeros_like(value)
        return (
            jnp.sum(jnp.where(left, value, zero), -1, keepdims=True),
            jnp.sum(jnp.where(left, zero, value), -1, keepdims=True),
        )

    weights = []
    for score in both(upper * query):
        score = score * stu_scale
        terms = jnp.exp(score - jnp.max(score, 0, keepdims=True))
        weights.append(terms / jnp.sum(terms, 0, keepdims=True))
    weight = jnp.where(left, weights[0], weights[1])
    pooled = jnp.sum(weight * upper, 0, keepdims=True)
    dense = dense_ref[layer].astype(F32)
    cls = cls_ref[layer].astype(F32)
    eight = (8, stu_width)
    z = jnp.tanh(
        mm_high(jnp.broadcast_to(pooled, eight), dense) + vec(dense_b_ref, layer, 0, stu_width)
    )
    logits = mm_high(z, cls) + vec(cls_b_ref, layer, 0, LANES)
    below = lax.broadcasted_iota(jnp.int32, (16, length), 0)
    segments = jnp.broadcast_to(seg_ref[pl.ds(row_ref[0], 1), :].astype(F32), (16, length))
    later = jnp.broadcast_to(later_ref[pl.ds(row_ref[0], 1), :], (16, LANES))
    tail = jnp.where(below == 1, segments, 0.0)
    narrow_tail = jnp.where(below[:, :LANES] == 2, later, tail[:, :LANES])
    narrow_tail = jnp.where(below[:, :LANES] == 0, jnp.concatenate([logits, logits], 0), narrow_tail)
    h[length:, :LANES] = narrow_tail.astype(BF16)
    h[length:, LANES:length] = tail[:, LANES:].astype(BF16)
    h[length:, length:] = jnp.zeros((16, width - length), BF16)
    put_h = copy(h, h_hbm, 7)
    cot = cot_ref[pl.ds(row_ref[0], 1), :]
    d_pre = mm_high(jnp.broadcast_to(cot, (8, LANES)), cls, NT) * (1.0 - z * z)
    d_pooled = mm_high(d_pre, dense, NT)[:1]
    d_pre = d_pre[:1]

    def column(value):
        return jnp.broadcast_to(value, (value.shape[1], value.shape[1])).T

    d_scores = []
    for weight_col, d_weight in zip(weights, both(upper * d_pooled)):
        mean = jnp.sum(weight_col * d_weight, 0, keepdims=True)
        d_scores.append(weight_col * (d_weight - mean) * stu_scale)
    d_score = jnp.where(left, d_scores[0], d_scores[1])
    d_upper = (weight * d_pooled + d_score * query).astype(BF16)
    d_upper_ref[...] = d_upper
    small_ref[:width, :] = mm(hidden, d_upper, TN)
    small_ref[width : width + stu_width, :] = column(pooled) * d_pre
    small_ref[width + stu_width : width + 2 * stu_width, :] = column(z[:1]) * cot
    base = width + 2 * stu_width
    small_ref[base : base + 1, :] = jnp.sum(d_upper.astype(F32), 0, keepdims=True)
    small_ref[base + 1 : base + 2, :] = jnp.sum(d_score * upper, 0, keepdims=True)
    small_ref[base + 2 : base + 3, :] = d_pre
    small_ref[base + 3 : base + 4, :] = cot
    small_ref[base + 4 :, :] = jnp.zeros((4, LANES), F32)

    for made in (put_slope, put_active, put_hat, put_h):
        made.wait()


def forward_ff(layer, row, first, first_full, cot, seg, later, weights, after=()):
    gain, shift, w_fi, fi_b, w_fo, fo_b = weights[4:10]
    length, width = first.shape
    ff = w_fi.shape[2]
    stu = weights[10].shape[2]
    outs = (
        low(length, ff),
        low(length, ff),
        low(length, width),
        low(length + 16, width),
        full(length, LANES),
        low(length, stu),
        full(width + 2 * stu + 8, LANES),
    )
    return call(
        partial(forward_ff_kernel, layer),
        f"forward_ff{layer}",
        outs,
        (ANY,) * 4 + (WHOLE,) * 3,
        (row, first, first_full, cot, seg, later, w_fi, w_fo, gain, shift, fi_b, fo_b)
        + tuple(weights[10:]),
        [SCALAR, ANY, ANY, WHOLE, WHOLE, WHOLE, ANY, ANY] + [WHOLE] * 11,
        [
            pltpu.VMEM((length, width), BF16),
            pltpu.VMEM((length, width), F32),
            pltpu.VMEM(w_fi.shape[1:], BF16),
            pltpu.VMEM(w_fo.shape[1:], BF16),
            vm(outs[0]),
            vm(outs[1]),
            vm(outs[2]),
            vm(outs[3]),
            pltpu.VMEM((length, 512), F32),
            pltpu.VMEM((length, 512), F32),
            pltpu.SemaphoreType.DMA((8 + ff // 512,)),
        ],
        after,
        18 * 10**9,
        20 * 10**6,
    )


def backward_ff_kernel(
    layer,
    grad_ref,
    d_upper_ref,
    spread1_ref,
    spread2_ref,
    proj_ref,
    gain_ref,
    w_fi_hbm,
    w_fo_hbm,
    hat1_hbm,
    slope_hbm,
    hat2_hbm,
    second_hbm,
    inner_hbm,
    branch_hbm,
    resid_hbm,
    sums_ref,
    w_fi,
    w_fo,
    hat1,
    slope,
    hat2,
    second,
    inner,
    branch,
    d_resid,
    sems,
):
    length, width = grad_ref.shape
    ff = w_fi.shape[1]
    copy = copier(sems)
    get_hat2 = copy(hat2_hbm, hat2, 0)
    get_fo = copy(w_fo_hbm.at[layer], w_fo, 1)
    get_slope = copy(slope_hbm, slope, 2)
    get_fi = copy(w_fi_hbm.at[layer], w_fi, 3)
    get_hat1 = copy(hat1_hbm, hat1, 4)
    sums_ref[...] = jnp.zeros_like(sums_ref)
    get_hat2.wait()
    gain1, gain2 = vec(gain_ref, layer, 0, width), vec(gain_ref, layer, width, width)
    total = lambda value: jnp.sum(value.astype(F32), 0, keepdims=True)

    def through_norm(grads, hat_ref, spread_ref, gain, out_ref):
        d_gain = jnp.zeros((1, width), F32)
        d_shift = jnp.zeros((1, width), F32)
        d_bias = jnp.zeros((1, width), F32)
        for rows in chunks(length):
            grad = grads(rows)
            hat = hat_ref[rows, :].astype(F32)
            d_gain += total(grad * hat)
            d_shift += total(grad)
            moved = norm_back(grad, hat, spread_ref[rows, 0:1], gain)
            d_resid[rows, :] = moved
            out_ref[rows, :] = moved.astype(BF16)
            d_bias += total(moved.astype(BF16))
        return d_gain, d_shift, d_bias

    from_student = mm(d_upper_ref[...], proj_ref[layer], NT)
    d_gain, d_shift, d_bias = through_norm(
        lambda rows: grad_ref[rows, :].astype(F32) + from_student[rows],
        hat2,
        spread2_ref,
        gain2,
        second,
    )
    sums_ref[1:2, 3 * width : 4 * width] = d_gain
    sums_ref[2:3, width : 2 * width] = d_shift
    sums_ref[2:3, 3 * width : 4 * width] = d_bias
    put_second = copy(second, second_hbm, 5)

    get_fo.wait()
    get_slope.wait()
    part = 512

    def ff_part(number, carry):
        at = pl.multiple_of(number * part, part)
        column = jnp.zeros((1, part), F32)
        d_active = mm(second[...], w_fo[pl.ds(at, part), :], NT)
        for rows in chunks(length):
            d_inner = (d_active[rows] * slope[rows, pl.ds(at, part)].astype(F32)).astype(BF16)
            inner[rows, pl.ds(at, part)] = d_inner
            column += total(d_inner)
        sums_ref[0:1, pl.ds(at, part)] = column
        return carry

    lax.fori_loop(0, ff // part, ff_part, 0)
    put_inner = copy(inner, inner_hbm, 6)

    get_fi.wait()
    get_hat1.wait()
    d_first = mm(inner[...], w_fi[...], NT)
    d_gain, d_shift, d_bias = through_norm(
        lambda rows: d_resid[rows, :] + d_first[rows], hat1, spread1_ref, gain1, branch
    )
    sums_ref[1:2, 2 * width : 3 * width] = d_gain
    sums_ref[2:3, :width] = d_shift
    sums_ref[2:3, 2 * width : 3 * width] = d_bias
    for made in (
        put_second,
        put_inner,
        copy(branch, branch_hbm, 7),
        copy(d_resid, resid_hbm, 8),
    ):
        made.wait()


def backward_ff(layer, grad, saved1, saved2, weights, after=()):
    _, _, _, hat1, _, _, spread1 = saved1
    slope, _, hat2, _, spread2, d_upper, _ = saved2
    gain, _, w_fi, _, w_fo, _ = weights[4:10]
    length, width = grad.shape
    ff = w_fi.shape[2]
    outs = (
        low(length, width),
        low(length, ff),
        low(length, width),
        full(length, width),
        full(8, ff),
    )
    return call(
        partial(backward_ff_kernel, layer),
        f"backward_ff{layer}",
        outs,
        (ANY,) * 4 + (WHOLE,),
        (grad, d_upper, spread1, spread2, weights[10], gain, w_fi, w_fo, hat1, slope, hat2),
        [WHOLE] * 6 + [ANY] * 5,
        [
            pltpu.VMEM(w_fi.shape[1:], BF16),
            pltpu.VMEM(w_fo.shape[1:], BF16),
            vm(hat1),
            vm(slope),
            vm(hat2),
            vm(outs[0]),
            vm(outs[1]),
            vm(outs[2]),
            vm(outs[3]),
            pltpu.SemaphoreType.DMA((9,)),
        ],
        after,
        16 * 10**9,
        22 * 10**6,
    )


def backward_attention_kernel(
    layer,
    scale,
    row_ref,
    seg_ref,
    lse_ref,
    w_in_hbm,
    w_out_hbm,
    qkv_hbm,
    mixed_hbm,
    branch_hbm,
    resid_hbm,
    d_qkv_hbm,
    d_x_ref,
    sums_ref,
    w_in,
    w_out,
    qkv,
    mixed,
    branch,
    d_resid,
    d_qkv,
    d_mix,
    code_q,
    code_k,
    delta_ref,
    probs_ref,
    ds_ref,
    sems,
):
    length, width = branch.shape
    copy = copier(sems)
    get_branch = copy(branch_hbm, branch, 0)
    get_out = copy(w_out_hbm.at[layer], w_out, 1)
    get_mixed = copy(mixed_hbm, mixed, 2)
    get_qkv = copy(qkv_hbm, qkv, 3)
    get_in = copy(w_in_hbm.at[layer], w_in, 4)
    get_resid = copy(resid_hbm, d_resid, 5)
    fill_codes(seg_ref, row_ref[0], code_q, code_k)
    probs_ref[...] = jnp.zeros_like(probs_ref)
    ds_ref[...] = jnp.zeros_like(ds_ref)
    sums_ref[...] = jnp.zeros_like(sums_ref)
    total = lambda value: jnp.sum(value.astype(F32), 0, keepdims=True)
    head_of = lax.broadcasted_iota(jnp.int32, (16, width), 1) // HEAD
    ones = (head_of == lax.broadcasted_iota(jnp.int32, (16, width), 0)).astype(F32).astype(BF16)
    get_branch.wait()
    get_out.wait()
    d_mix[...] = mm(branch[...], w_out[...], NT).astype(BF16)
    get_mixed.wait()
    product = d_mix[...].astype(F32) * mixed[...].astype(F32)
    high = product.astype(BF16)
    rest = (product - high.astype(F32)).astype(BF16)
    delta_ref[...] = mm(ones, high, NT) + mm(ones, rest, NT)

    get_qkv.wait()
    low_half = lax.broadcasted_iota(jnp.int32, (length, LANES), 1) < HEAD
    low_rows = lax.broadcasted_iota(jnp.int32, (LANES, length), 0) < HEAD

    def pair(number, carry):
        at = pl.multiple_of(number * LANES, LANES)
        cols = pl.ds(at, LANES)
        key_cols = pl.ds(at + width, LANES)
        value_cols = pl.ds(at + 2 * width, LANES)
        queries, keys, values, mix = qkv[:, cols], qkv[:, key_cols], qkv[:, value_cols], d_mix[:, cols]
        keys_t = keys.T
        d_query = jnp.zeros((LANES, length), F32)
        d_keys, d_values = [], []
        zero = jnp.zeros_like(keys)
        for sub in range(2):
            head = 2 * number + sub
            lse = lse_ref[pl.ds(head, 1), :]
            delta = delta_ref[pl.ds(head, 1), :]
            mine = low_half == (sub == 0)
            scores = mm(
                jnp.where(mine, keys, code_k[...]), jnp.where(mine, queries, code_q[...]), NT
            )
            d_probs = mm(jnp.where(mine, values, zero), mix, NT)
            for rows in chunks(length):
                start, stop = window(rows.start, length)
                probs = jnp.exp(scores[rows, start:stop] - lse[:, start:stop])
                probs_ref[sub, rows, start:stop] = probs.astype(BF16)
                ds_ref[sub, rows, start:stop] = (
                    probs * (d_probs[rows, start:stop] - delta[:, start:stop])
                ).astype(BF16)
            d_values.append(mm(probs_ref[sub], mix))
            d_keys.append(mm(ds_ref[sub], queries))
            mine_t = jnp.where(low_rows == (sub == 0), keys_t, jnp.zeros_like(keys_t))
            d_query += mm(mine_t, ds_ref[sub])
        dq = (d_query.T * scale).astype(BF16)
        d_qkv[:, cols] = dq
        sums_ref[1:2, cols] = total(dq)
        d_qkv[:, key_cols] = jnp.where(low_half, d_keys[0], d_keys[1]).astype(BF16)
        dv = jnp.where(low_half, d_values[0], d_values[1]).astype(BF16)
        d_qkv[:, value_cols] = dv
        sums_ref[1:2, key_cols] = total(dv)
        return carry

    lax.fori_loop(0, HEADS * HEAD // LANES, pair, 0)
    put_qkv = copy(d_qkv, d_qkv_hbm, 6)
    get_in.wait()
    get_resid.wait()
    d_x = mm(d_qkv[...], w_in[...], NT)
    for rows in chunks(length):
        d_x_ref[rows, :] = (d_resid[rows, :] + d_x[rows]).astype(BF16)
    put_qkv.wait()


def backward_attention(layer, row, seg, saved1, branch, d_resid, weights, after=()):
    qkv, lse, mixed = saved1[:3]
    w_in, _, w_out = weights[:3]
    ff = weights[6].shape[2]
    length, width = mixed.shape
    outs = (low(length, 3 * width), low(length, width), full(8, ff))
    return call(
        partial(backward_attention_kernel, layer, HEAD**-0.5),
        f"backward_attention{layer}",
        outs,
        (ANY, WHOLE, WHOLE),
        (row, seg, lse, w_in, w_out, qkv, mixed, branch, d_resid),
        [SCALAR, WHOLE, WHOLE] + [ANY] * 6,
        [
            pltpu.VMEM(w_in.shape[1:], BF16),
            pltpu.VMEM(w_out.shape[1:], BF16),
            vm(qkv),
            vm(mixed),
            vm(branch),
            vm(d_resid),
            vm(outs[0]),
            vm(outs[1]),
            pltpu.VMEM((length, LANES), BF16),
            pltpu.VMEM((length, LANES), BF16),
            pltpu.VMEM((16, length), F32),
            pltpu.VMEM((2, length, length), BF16),
            pltpu.VMEM((2, length, length), BF16),
            pltpu.SemaphoreType.DMA((7,)),
        ],
        after,
        20 * 10**9,
        16 * 10**6,
    )


def grad_cols_kernel(half_ref, *refs, rows, steps):
    lefts, rights = refs[:rows], refs[rows : 2 * rows]
    other_ref, own_ref, turned = refs[-3:]
    length = lefts[0].shape[0]
    step = pl.program_id(0)

    @pl.when(step == 0)
    def _():
        for number, left in enumerate(lefts):
            turned[:, number * length : (number + 1) * length] = left[...].T

    found = None
    for number, right in enumerate(rights):
        part = mm(turned[:, number * length : (number + 1) * length], right[...])
        found = part if found is None else found + part
    found = found.reshape(own_ref.shape).astype(BF16)

    @pl.when(step < steps)
    def _():
        other_ref[...] = found

    @pl.when(step >= steps)
    def _():
        own_ref[...] = found


def weight_grad_cols(half, lefts, rights, narrow, after=()):
    rows = len(lefts)
    length, width = lefts[0].shape
    cols = rights[0].shape[1] // 2
    tile = next((size for size in (768, 384) if cols % size == 0), cols)
    steps = cols // tile
    shape = jax.ShapeDtypeStruct((narrow, width // narrow, cols), BF16)
    block = (narrow, width // narrow, tile)

    def right_at(j, half):
        mine = jnp.where(j < steps, 1 - half[0], half[0])
        return (0, mine * steps + jnp.where(j < steps, j, j - steps))

    return pl.pallas_call(
        partial(grad_cols_kernel, rows=rows, steps=steps),
        out_shape=(shape, shape),
        grid_spec=pltpu.PrefetchScalarGridSpec(
            num_scalar_prefetch=1,
            grid=(2 * steps,),
            in_specs=[pl.BlockSpec((length, width), lambda j, half: (0, 0))] * rows
            + [pl.BlockSpec((length, tile), right_at)] * rows
            + [ANY] * len(after),
            out_specs=(
                pl.BlockSpec(block, lambda j, half: (0, 0, jnp.minimum(j, steps - 1))),
                pl.BlockSpec(block, lambda j, half: (0, 0, jnp.maximum(j - steps, 0))),
            ),
            scratch_shapes=[pltpu.VMEM((width, rows * length), BF16)],
        ),
        compiler_params=pltpu.CompilerParams(vmem_limit_bytes=LIMIT),
        cost_estimate=BRIEF,
        name="weight_grad_cols",
    )(half, *lefts, *rights, *after)


def grad_rows_kernel(half_ref, *refs, rows, narrow):
    lefts, rights = refs[:rows], refs[rows : 2 * rows]
    other_ref, own_ref = refs[-2:]
    unit = own_ref.shape[1]
    width = rights[0].shape[1]
    found = None
    for left, right in zip(lefts, rights):
        part = mm(left[...], right[...], TN)
        found = part if found is None else found + part
    found = found.astype(BF16)

    def write(ref):
        for block in range(ref.shape[2] // width):
            ref[0, :, block * width : (block + 1) * width] = found[
                block * unit : (block + 1) * unit
            ]

    @pl.when(pl.program_id(0) < narrow)
    def _():
        write(other_ref)

    @pl.when(pl.program_id(0) >= narrow)
    def _():
        write(own_ref)


def weight_grad_rows(half, lefts, rights, narrow, after=()):
    rows = len(lefts)
    length, deep = lefts[0].shape
    width = rights[0].shape[1]
    unit = width // narrow
    part = deep // narrow // 2
    cols = part // unit * width
    shape = jax.ShapeDtypeStruct((narrow, unit, cols), BF16)

    def left_at(j, half):
        first = j < narrow
        return (0, 2 * jnp.where(first, j, j - narrow) + jnp.where(first, 1 - half[0], half[0]))

    return pl.pallas_call(
        partial(grad_rows_kernel, rows=rows, narrow=narrow),
        out_shape=(shape, shape),
        grid_spec=pltpu.PrefetchScalarGridSpec(
            num_scalar_prefetch=1,
            grid=(2 * narrow,),
            in_specs=[pl.BlockSpec((length, part), left_at)] * rows
            + [pl.BlockSpec((length, width), lambda j, half: (0, 0))] * rows
            + [ANY] * len(after),
            out_specs=(
                pl.BlockSpec((1, unit, cols), lambda j, half: (jnp.minimum(j, narrow - 1), 0, 0)),
                pl.BlockSpec((1, unit, cols), lambda j, half: (jnp.maximum(j - narrow, 0), 0, 0)),
            ),
        ),
        compiler_params=pltpu.CompilerParams(vmem_limit_bytes=LIMIT),
        cost_estimate=BRIEF,
        name="weight_grad_rows",
    )(half, *lefts, *rights, *after)


def swap(value, bit):
    size = lax.axis_size("wide")
    return lax.ppermute(value, "wide", [(i, i ^ bit) for i in range(size)])


def tie(values, on):
    return lax.optimization_barrier((values, on))[0]


def add_low(left, right):
    return (left.astype(F32) + right.astype(F32)).astype(BF16)


def halves(value, side, axis):
    half = value.shape[axis] // 2
    keep = lax.dynamic_slice_in_dim(value, side * half, half, axis)
    give = lax.dynamic_slice_in_dim(value, (1 - side) * half, half, axis)
    return keep, give


def wide_bits():
    return [1 << i for i in range((lax.axis_size("wide") - 1).bit_length())]


def bit_order(turn):
    rest = wide_bits()[1:]
    return rest[::-1] if turn else rest


class Halving:
    def __init__(self, groups):
        self.place = lax.axis_index("wide")
        self.bits = list(zip(*(bit_order(turn) for turn in range(2))))
        self.groups = groups
        self.flying = None

    def step(self, on=None):
        if self.flying is not None:
            if on is not None:
                self.flying = [(keep, tie(recv, on)) for keep, recv in self.flying]
            self.groups = [[add_low(keep, recv)] for keep, recv in self.flying]
            self.flying = None
        if not self.bits:
            return [group[0] for group in self.groups]
        flying, gives = [], []
        for bit, group in zip(self.bits.pop(0), self.groups):
            split = [halves(part, (self.place // bit) % 2, 1) for part in group]
            keep = jnp.concatenate([pair[0] for pair in split], -1)
            give = jnp.concatenate([pair[1] for pair in split], -1)
            gives.append(give)
            flying.append((keep, swap(give, bit)))
        self.flying = flying
        return gives

    def finish(self, on=None):
        mine = self.step(on)
        while self.flying is not None:
            mine = self.step()
        return jnp.concatenate(mine, -1)


def narrow_parts(mine):
    return mine.reshape((2,) * (mine.shape[0].bit_length() - 1) + mine.shape[1:])


def narrow_level(cur, level, on=None):
    size = lax.axis_size("narrow")
    depth = size.bit_length() - 1
    bit = 1 << level
    keep, give = halves(cur, (lax.axis_index("narrow") // bit) % 2, depth - 1 - level)
    recv = lax.ppermute(give, "narrow", [(i, i ^ bit) for i in range(size)])
    if on is not None:
        recv = tie(recv, on)
    return add_low(keep, recv)


def narrow_sum_swaps(mine, ons=()):
    cur = narrow_parts(mine)
    for level in range(lax.axis_size("narrow").bit_length() - 1):
        cur = narrow_level(cur, level, ons[level] if level < len(ons) else None)
    return cur.reshape(mine.shape[1:])


def wide_gather_swaps(mine, got=None, on=None):
    place = lax.axis_index("wide")
    cur = mine[None]
    for number, bit in enumerate(wide_bits()[::-1]):
        other = got[None] if number == 0 and got is not None else swap(cur, bit)
        if number > 0 and on is not None:
            other = tie(other, on)
        upper = (place // bit) % 2 == 1
        cur = jnp.stack([jnp.where(upper, other, cur), jnp.where(upper, cur, other)])
        cur = cur.reshape((-1,) + mine.shape)
    return cur


def narrow_sum(mine):
    return lax.psum_scatter(mine, "narrow", scatter_dimension=0, tiled=True)[0]


def small_pack_kernel(smalls, *refs):
    small_refs, sums_refs = refs[:smalls], refs[smalls:-4]
    out_ref, small, sums, rest = refs[-4:]
    _, narrow, unit, lanes = out_ref.shape
    width = narrow * unit
    stu = lanes
    share = stu // narrow
    deep = sums.shape[1]
    small[...] = sum(ref[...] for ref in small_refs)
    sums[...] = sum(ref[...] for ref in sums_refs)
    own = width + 2 * stu
    vectors = [
        (sums, 1, 0, 2 * width),
        (sums, 2, 2 * width, width),
        (sums, 1, 2 * width, 2 * width),
        (sums, 2, 0, 2 * width),
        (sums, 0, 0, deep),
        (sums, 2, 3 * width, width),
        (small, own, 0, stu),
        (small, own + 1, 0, stu),
        (small, own + 2, 0, stu),
    ]
    for place in range(narrow):
        out_ref[0, place] = small[place * unit : (place + 1) * unit, :].astype(BF16)
        rest[...] = jnp.zeros_like(rest)
        for number in range(2):
            start = width + number * stu + place * share
            rest[number * share : (number + 1) * share, :] = small[start : start + share, :]
        row = 2 * share
        for ref, line, start, size in vectors:
            size = size // narrow
            value = ref[line : line + 1, :][:, start + place * size : start + (place + 1) * size]
            for at in range(0, size, lanes):
                part = min(lanes, size - at)
                rest[row : row + 1, :part] = value[:, at : at + part]
                row += 1
        rest[row : row + 1, :] = small[own + 3 : own + 4, :]
        out_ref[1, place] = rest[...].astype(BF16)


def small_pack(smalls, sums, narrow):
    stu = smalls[0].shape[1]
    width = smalls[0].shape[0] - 2 * stu - 8
    unit = width // narrow
    return pl.pallas_call(
        partial(small_pack_kernel, len(smalls)),
        out_shape=low(2, narrow, unit, stu),
        in_specs=[WHOLE] * (len(smalls) + len(sums)),
        out_specs=WHOLE,
        scratch_shapes=[vm(smalls[0]), vm(sums[0]), pltpu.VMEM((unit, stu), F32)],
        cost_estimate=BRIEF,
        name="small_pack",
    )(*smalls, *sums)


def place_rows(orders, place, rows):
    found = []
    for order in orders:
        at = 0
        for bit in order:
            at = 2 * at + (place // bit) % 2
        found.append(at * rows)
    return found


def turn_bits(place, total):
    count = (total - 1).bit_length()
    return sum(((place >> i) & 1) << (count - 1 - i) for i in range(count))


def place_ff_kernel(layer, orders, turned, held, got_ref, *refs):
    outs = refs[held : held + 3]
    fi, fo, ao, sems = refs[held + 3 :]
    unit, deep = fi.shape
    width = ao.shape[1]
    half = width // 2
    total, rows, _ = got_ref.shape
    blocks = fo.shape[0] // unit // 2
    for place in range(total):
        core = place % 2
        x_at, y_at = place_rows(orders, place, rows)
        at = turn_bits(place, total) if turned else place
        get = lambda start, size, at=at: got_ref[at, :, start : start + size].astype(F32)
        fi[x_at : x_at + rows, core * deep // 2 : (core + 1) * deep // 2] = get(0, deep // 2)
        for block in range(blocks):
            at = (core * blocks + block) * unit + y_at
            fo[at : at + rows, :] = get(deep // 2 + block * width, width)
        ao[y_at : y_at + rows, core * half : (core + 1) * half] = get(deep, half)
    puts = []
    for number, (src, dst) in enumerate(zip((fi, fo, ao), outs)):
        puts.append(pltpu.make_async_copy(src, dst.at[layer], sems.at[number]))
        puts[-1].start()
    for made in puts:
        made.wait()


def place_attn_kernel(layer, orders, held, got_ref, *refs):
    out, small = refs[held], refs[held + 1]
    ai, sem = refs[held + 2 :]
    total, rows, cols = got_ref.shape
    half = ai.shape[1] // 2
    cut = cols // 2
    rest = half - cut
    for place in range(total):
        core = place % 2
        x_at, y_at = place_rows(orders, place, rows)
        at = turn_bits(place, total)
        get = lambda start, size: got_ref[at, :, start : start + size].astype(F32)
        start = core * half
        ai[x_at : x_at + rows, start : start + cut] = get(0, cut)
        ai[y_at : y_at + rows, start + cut : start + half] = get(cut, rest)
        small[y_at : y_at + rows, core * LANES : (core + 1) * LANES] = get(cut + rest, LANES)
    made = pltpu.make_async_copy(ai, out.at[layer], sem)
    made.start()
    made.wait()


def place_ff(layer, got, turned, shapes, previous=()):
    held = len(previous)
    return pl.pallas_call(
        partial(place_ff_kernel, layer, [bit_order(turn) for turn in range(2)], turned, held),
        out_shape=tuple(shapes),
        in_specs=[WHOLE] + [ANY] * held,
        out_specs=(ANY,) * 3,
        scratch_shapes=[pltpu.VMEM(shape.shape[1:], F32) for shape in shapes]
        + [pltpu.SemaphoreType.DMA((3,))],
        input_output_aliases={1 + i: i for i in range(held)},
        compiler_params=pltpu.CompilerParams(vmem_limit_bytes=LIMIT),
        cost_estimate=pl.CostEstimate(flops=10**6, bytes_accessed=8 * 10**6, transcendentals=0),
        name=f"place_ff{layer}",
    )(got, *previous)


def place_attn(layer, got, shape, previous=(), after=()):
    held = len(previous)

    def body(got_ref, *refs):
        kept = refs[:held] + refs[held + len(after) :]
        place_attn_kernel(layer, orders, held, got_ref, *kept)

    orders = [bit_order(turn) for turn in range(2)]
    return pl.pallas_call(
        body,
        out_shape=(shape, full(shape.shape[1], 2 * LANES)),
        in_specs=[WHOLE] + [ANY] * (held + len(after)),
        out_specs=(ANY, WHOLE),
        scratch_shapes=[pltpu.VMEM(shape.shape[1:], F32), pltpu.SemaphoreType.DMA],
        input_output_aliases={1 + i: i for i in range(held)},
        compiler_params=pltpu.CompilerParams(vmem_limit_bytes=LIMIT),
        cost_estimate=pl.CostEstimate(flops=10**6, bytes_accessed=3 * 10**6, transcendentals=0),
        name=f"place_attn{layer}",
    )(got, *previous, *after)


def place_small_kernel(first_ref, second_ref, proj_ref, dense_ref, cls_ref, *vec_refs):
    for layer, ref in enumerate((first_ref, second_ref)):
        stu = dense_ref.shape[1]
        proj_ref[layer] = ref[:, :LANES]
        dense_ref[layer] = ref[:stu, LANES:]
        cls_ref[layer] = ref[stu : 2 * stu, LANES : LANES + cls_ref.shape[2]]
        row = 2 * stu
        for out in vec_refs:
            size = out.shape[1]
            for start in range(0, size, LANES):
                part = min(LANES, size - start)
                out[layer : layer + 1, start : start + part] = ref[
                    row : row + 1, LANES : LANES + part
                ]
                row += 1


def place_small(first, second, width, deep, classes, narrow):
    sizes = [2 * width, width, 2 * width, 2 * width, deep, width, LANES, LANES, LANES]
    stu = LANES // narrow
    outs = (
        full(2, width // narrow, LANES),
        full(2, stu, LANES),
        full(2, stu, classes),
    ) + tuple(full(2, size // narrow) for size in sizes)
    return pl.pallas_call(
        place_small_kernel,
        out_shape=outs + (full(2, classes),),
        in_specs=[WHOLE, WHOLE],
        out_specs=(WHOLE,) * 13,
        name="place_small",
    )(first, second)


def route_kernel(me_ref, *refs):
    around, out_ref, held = refs[:-2], refs[-2], refs[-1]
    me, size = me_ref[0], len(around)
    for step, ref in enumerate(around):
        held[lax.rem(me + (size - step), size)] = ref[0]
    counts = [held[i] for i in range(size)]
    flow, before = [], []
    total = jnp.int32(0)
    for value in counts:
        before.append(total)
        total = total + value - 1
        flow.append(total)
    right1 = [(f >= 1) & (c >= 1) for f, c in zip(flow, counts)]
    left1 = [(f <= -1) & (c >= 1) for f, c in zip(before, counts)]
    right2 = [(f >= 1) & ((f >= 2) | (c == 0)) for f, c in zip(flow, counts)]
    left2 = [(f <= -1) & ((f <= -2) | (c == 0)) for f, c in zip(before, counts)]

    def at(values, shift):
        found = jnp.int32(0)
        for i, value in enumerate(values):
            found = jnp.where(me + shift == i, value.astype(jnp.int32), found)
        return found

    count = at(counts, 0)
    from_left2, from_right2 = at(right2, -1), at(left2, 1)
    sent_right, sent_left = at(right1, 0), at(left1, 0)
    results = (
        at(right1, -1),
        from_left2,
        from_left2 | from_right2,
        (count == 2).astype(jnp.int32),
        ((count == 1) & (sent_right + sent_left == 0)).astype(jnp.int32),
        at(right2, 0),
        sent_left,
        (sent_right & at(right2, 1)) | (sent_left & at(left2, -1)),
        (count >= 1).astype(jnp.int32),
        (count >= 2).astype(jnp.int32),
    )
    for i, value in enumerate(results):
        out_ref[i] = value
    for i in range(len(results), out_ref.shape[0]):
        out_ref[i] = 0


def route(me, around):
    return pl.pallas_call(
        route_kernel,
        out_shape=jax.ShapeDtypeStruct((16,), jnp.int32),
        in_specs=[SCALAR] * (1 + len(around)),
        out_specs=SCALAR,
        scratch_shapes=[pltpu.SMEM((len(around),), jnp.int32)],
        name="route",
    )(me, *around)


def shards(
    tokens,
    segments,
    exit_layer,
    attn_in,
    qv_bias,
    attn_out,
    out_bias,
    ln_gain,
    ln_bias,
    ff_in,
    ff_in_bias,
    ff_out,
    ff_out_bias,
    stu_proj,
    stu_bias,
    pool_query,
    stu_dense,
    stu_dense_bias,
    stu_cls,
    stu_cls_bias,
    out_cot,
    logit_cot,
):
    row_count, length, width = tokens.shape
    classes = stu_cls.shape[-1]
    blank = LANES - classes
    narrow = lax.axis_size("narrow")
    me = lax.axis_index("narrow")
    core = lax.axis_index("wide") % 2
    weights = (
        attn_in,
        qv_bias,
        attn_out,
        out_bias,
        ln_gain,
        ln_bias,
        ff_in,
        ff_in_bias,
        ff_out,
        ff_out_bias,
        stu_proj,
        stu_bias,
        pool_query,
        stu_dense,
        stu_dense_bias,
        jnp.pad(stu_cls, ((0, 0), (0, 0), (0, blank))),
        jnp.pad(stu_cls_bias, ((0, 0), (0, blank))),
    )
    wide_cot = jnp.pad(logit_cot.astype(F32), ((0, 0), (0, 0), (0, blank)))

    alive = exit_layer == 1
    row_a = jnp.where(alive[0], 0, jnp.where(alive[1], 1, 0)).astype(jnp.int32)
    row_b = 1 - row_a

    index = lambda row: row.reshape(1)
    first_row = jnp.zeros((1,), jnp.int32)
    own = index(core)
    ia, ib = index(row_a), index(row_b)
    early_cot, late_cot = wide_cot[:, 0], wide_cot[:, 1]
    a1 = forward_attention(0, ia, tokens, segments, weights)

    mine = tie(jnp.sum(alive.astype(jnp.int32)).reshape(1), a1[4])
    around = [mine] + [
        lax.ppermute(mine, "narrow", [(i, (i + step) % narrow) for i in range(narrow)])
        for step in range(1, narrow)
    ]
    flags = route(me.reshape(1), around)
    from_left1, from_left2, use_two, use_b, use_a, on_right, sent_left, is_far, a_alive, b_alive = (
        flags[i] == 1 for i in range(10)
    )

    even = me % 2 == 0
    inner = [(i, i ^ 1) for i in range(narrow)]
    outer = []
    for i in range(lax.axis_size("wide") * narrow):
        place, line = i // narrow, i % narrow
        other = ((line + 1) ^ 1) - 1
        inside = 0 <= other < narrow
        outer.append((i, place * narrow + other if inside else (place ^ 1) * narrow + line))

    def shift(value):
        return (
            lax.ppermute(value, "narrow", inner),
            lax.ppermute(value, ("wide", "narrow"), outer),
        )

    def pick(pair, is_left):
        return jnp.where(is_left == even, pair[1], pair[0])

    def out_one(pair):
        return pick(pair, from_left1)

    def out_two(pair, one, own_a, own_b):
        two = pick(pair, from_left2)
        return jnp.where(use_b, own_b, jnp.where(use_a, own_a, jnp.where(use_two, two, one)))

    def back_one(pair):
        return pick(pair, ~on_right)

    def back_two(value, pair, pair2):
        return jnp.where(
            use_a, value, jnp.where(is_far, pick(pair2, sent_left), pick(pair, sent_left))
        )

    def row_of(value, row):
        return lax.dynamic_index_in_dim(value, row, 0, False)

    cot_a, cot_b = row_of(out_cot, row_a), row_of(out_cot, row_b)
    pair = shift(tie(cot_a, a1[4]))
    a2 = forward_ff(0, ia, a1[4], a1[5], early_cot, segments, late_cot, weights, (cot_a,))
    cot_one = out_one(tie(pair, a2[3]))
    pair = shift(a2[3])
    b1 = forward_attention(0, ib, tokens, segments, weights, (a2[3], cot_one))
    one = out_one(tie(pair, b1[4]))
    pair = shift(one)
    b2 = forward_ff(0, ib, b1[4], b1[5], early_cot, segments, late_cot, weights, (one,))
    work_in = out_two(tie(pair, b2[3]), one, a2[3], b2[3])
    work_seg = work_in[length + 1 : length + 2, :length].astype(jnp.int32)
    work_late = work_in[length + 2 : length + 3, :LANES].astype(F32)

    pair = shift(tie(cot_one, b2[3]))
    w1 = forward_attention(1, first_row, work_in[None], work_seg, weights)
    work_cot = out_two(tie(pair, w1[4]), cot_one, cot_a, cot_b)
    w2 = forward_ff(
        1, first_row, w1[4], w1[5], work_late, work_seg, work_late, weights, (work_cot,)
    )
    sent_h = w2[3]
    pair_h = shift(sent_h)
    w3 = backward_ff(1, work_cot, w1, w2, weights, (sent_h,))

    def ff_jobs(saved1, saved2, back):
        first = [s[4] for s in saved1]
        mixed = [s[2] for s in saved1]
        active = [s[1] for s in saved2]
        second, inner, branch = ([b[i] for b in back] for i in range(3))
        return (
            (weight_grad_cols, first, inner),
            (weight_grad_rows, active, second),
            (weight_grad_cols, mixed, branch),
        )

    def weight_grads(jobs, after=()):
        return [job(own, lefts, rights, narrow, after) for job, lefts, rights in jobs]

    def core_sum(pairs, on=None):
        received = [swap(other, 1) for other, _ in pairs]
        if on is not None:
            received = tie(received, on)
        return [add_low(mine, recv) for (_, mine), recv in zip(pairs, received)]

    def ff_halving(parts):
        return Halving([[parts[0]], [parts[1], parts[2]]])

    def attn_halving(part, small):
        keep, give = halves(small, core, 0)
        small = add_low(keep, swap(give, 1))[0]
        cut = (part.shape[-1] + LANES) // 2
        return Halving([[part[..., :cut]], [part[..., cut:], small]])

    halves1 = weight_grads(ff_jobs([w1], [w2], [w3]))
    sent = tuple(pair[0] for pair in halves1)
    w4 = backward_attention(1, first_row, work_seg, w1, w3[2], w3[3], weights, sent)
    pair_x = shift(w4[1])
    ff1 = ff_halving(core_sum(halves1))
    flying = ff1.step()
    half1 = weight_grads(((weight_grad_cols, [work_in[:length]], [w4[0]]),), tuple(flying))
    small1 = small_pack([w2[6]], [w3[4], w4[2]], narrow)
    forth_x = back_one(tie(pair_x, half1[0][0]))
    pair_x2 = shift(forth_x)

    base_b = jnp.where(b_alive, w4[1], row_of(out_cot, row_b))
    b3 = backward_ff(0, base_b, b1, b2, weights, (half1[0][0], forth_x, small1))
    far_x = back_two(w4[1], pair_x, tie(pair_x2, b3[2]))
    forth_h = back_one(tie(pair_h, far_x))
    pair_h2 = shift(forth_h)
    at1 = attn_halving(core_sum(half1)[0], small1)
    flying = at1.step() + ff1.step(b3[2])
    base_a = jnp.where(a_alive, far_x, row_of(out_cot, row_a))
    a3 = backward_ff(0, base_a, a1, a2, weights, (*flying, forth_h))
    mine_ff1 = ff1.finish(a3[2])
    flying = at1.step(a3[2])
    halves0 = weight_grads(ff_jobs([a1, b1], [a2, b2], [a3, b3]), (mine_ff1, *flying))
    ff0 = ff_halving(core_sum(halves0))
    flying = ff0.step()
    far_h = back_two(sent_h, pair_h, tie(pair_h2, a3[2]))
    b4 = backward_attention(
        0, ib, segments, b1, b3[2], b3[3], weights, (*flying, far_h)
    )
    flying = ff0.step(b4[1])
    sum_at1 = narrow_sum(at1.finish(b4[1]))
    a4 = backward_attention(0, ia, segments, a1, a3[2], a3[3], weights, (b4[1], *flying))
    mine_ff0 = ff0.finish((a4[1], sum_at1))
    sum_ff1 = narrow_sum_swaps(mine_ff1, (b4[1], a4[1]))
    half0 = weight_grads(
        (
            (
                weight_grad_cols,
                [row_of(tokens, row_a), row_of(tokens, row_b)],
                [a4[0], b4[0]],
            ),
        ),
        (mine_ff0, sum_ff1),
    )
    part_ff0 = narrow_level(narrow_parts(mine_ff0), 0, half0[0][0])
    got_ff1 = tie(swap(tie(sum_ff1, mine_ff0), wide_bits()[-1]), half0[0][0])
    half0 = [(tie(half0[0][0], part_ff0), half0[0][1])]
    last_sums = tie(a4[2], half0[0][0])
    small0 = small_pack([a2[6], b2[6]], [a3[4], b3[4], last_sums, b4[2]], narrow)
    at0 = attn_halving(core_sum(half0)[0], small0)
    flying = at0.step()
    for level in range(1, narrow.bit_length() - 1):
        part_ff0 = narrow_level(part_ff0, level, flying)
    sum_ff0 = part_ff0.reshape(mine_ff0.shape[1:])
    all_ff1 = wide_gather_swaps(sum_ff1, got_ff1, flying)
    all_ff0 = lax.all_gather(sum_ff0, "wide", axis=0, tiled=False)
    all_at1 = wide_gather_swaps(tie(sum_at1, flying))
    all_at0 = wide_gather_swaps(narrow_sum_swaps(at0.finish(), (None, all_ff0)))

    deep = ff_in.shape[2]
    unit = width // narrow
    shapes = [full(2, unit, deep), full(2, deep // narrow, width), full(2, unit, width)]
    attn_shape = full(2, unit, 3 * width)
    placed = place_ff(1, all_ff1, True, shapes)
    d_attn_in, small1 = place_attn(1, all_at1, attn_shape)
    placed = place_ff(0, all_ff0, False, shapes, placed)
    d_attn_in, small0 = place_attn(0, all_at0, attn_shape, (d_attn_in,), (placed[2],))
    d_ff_in, d_ff_out, d_attn_out = placed
    (d_proj, d_dense, d_cls, d_qv, d_out_b, d_gain, d_shift, d_fi_b, d_fo_b, *rest) = place_small(
        small0, small1, width, deep, classes, narrow
    )
    d_stu_b, d_query, d_dense_b, d_cls_b = rest
    totals = (
        d_attn_in,
        d_qv,
        d_attn_out,
        d_out_b,
        d_gain,
        d_shift,
        d_ff_in,
        d_fi_b,
        d_ff_out,
        d_fo_b,
        d_proj,
        d_stu_b,
        d_query,
        d_dense,
        d_dense_b,
        d_cls,
        d_cls_b,
    )

    in_order = lambda for_a, for_b: jnp.where(
        row_a == 0, jnp.stack([for_a, for_b]), jnp.stack([for_b, for_a])
    )
    act_a = jnp.where(a_alive, far_h, a2[3])
    act_b = jnp.where(b_alive, w2[3], b2[3])
    cut = lambda value: value[length, :classes]
    logits = jnp.where(jnp.stack([a_alive, b_alive])[:, None], jnp.stack([cut(act_a), cut(act_b)]), 0)
    early = in_order(cut(a2[3]), cut(b2[3]))
    logits = jnp.stack([early, in_order(logits[0], logits[1])], 1).astype(BF16)
    act_a, act_b = act_a[:length], act_b[:length]
    return (in_order(act_a, act_b), logits, in_order(a4[1], b4[1])) + totals


def solution(mesh):
    rows = ("wide", "narrow")
    return jax.shard_map(
        shards,
        mesh=mesh,
        in_specs=(P(rows, None, None), P(rows, None), P(rows))
        + (P(),) * 17
        + (P(rows, None, None), P(rows, None, None)),
        out_specs=(P(rows, None, None),) * 3
        + (
            P(None, "narrow", None),
            P(None, "narrow"),
            P(None, "narrow", None),
            P(None, "narrow"),
            P(None, "narrow"),
            P(None, "narrow"),
            P(None, "narrow", None),
            P(None, "narrow"),
            P(None, "narrow", None),
            P(None, "narrow"),
            P(None, "narrow", None),
            P(None, "narrow"),
            P(None, "narrow"),
            P(None, "narrow", None),
            P(None, "narrow"),
            P(None, "narrow", None),
            P(),
        ),
        check_vma=False,
    )
```

```python
from functools import partial

import jax
import jax.numpy as jnp
import numpy as np
from jax import lax
from jax.experimental import pallas as pl
from jax.experimental.pallas import tpu as pltpu
from jax.sharding import PartitionSpec as P

HEADS = 12
HEAD = 64
STU_HEADS = 2
LANES = 128
CHUNK = 128
REACH = 256
EPS = 1e-12
MASKED = -1e30
SEGMENTS = 4
HIGH = lax.Precision.HIGHEST
F32 = jnp.float32
BF16 = jnp.bfloat16
LIMIT = 52 * 1024 * 1024
BRIEF = pl.CostEstimate(flops=10**6, bytes_accessed=10**5, transcendentals=0)

NN = (((1,), (0,)), ((), ()))
NT = (((1,), (1,)), ((), ()))
TN = (((0,), (0,)), ((), ()))


def mm(left, right, dims=NN):
    return lax.dot_general(left, right, dims, preferred_element_type=F32)


def mm_high(left, right, dims=NN):
    return lax.dot_general(left, right, dims, precision=HIGH, preferred_element_type=F32)


def vec(ref, layer, start, size):
    return ref[...].astype(F32)[layer : layer + 1, start : start + size]


def gelu_pair(value):
    dist = jnp.abs(value) * (0.5**0.5)
    den = 1.0 + 0.3275911 * dist
    part = pl.reciprocal(den, approx=True)
    part = part * (2.0 - den * part)
    series = 0.5 * 1.061405429
    for term in (-1.453152027, 1.421413741, -0.284496736, 0.254829592):
        series = series * part + 0.5 * term
    bell = jnp.exp(-(dist * dist))
    tail = series * part * bell
    below = jnp.where(value >= 0, 1.0 - tail, tail)
    return value * below, below + value * bell * ((2.0 * np.pi) ** -0.5)


def row_norm(value):
    mean = jnp.mean(value, -1, keepdims=True)
    centered = value - mean
    spread = lax.rsqrt(jnp.mean(centered * centered, -1, keepdims=True) + EPS)
    return centered * spread, spread


def norm_back(grad, hat, spread, gain):
    scaled = grad * gain
    low = jnp.mean(scaled, -1, keepdims=True)
    high = jnp.mean(scaled * hat, -1, keepdims=True)
    return spread * (scaled - low - hat * high)


def window(place, length):
    start = max(0, (place - REACH + 1) // CHUNK * CHUNK)
    stop = min(length, -(-(place + CHUNK + REACH - 1) // CHUNK) * CHUNK)
    return start, stop


def fill_codes(seg_ref, row, code_q, code_k):
    length = code_q.shape[0]
    seg_row = seg_ref[pl.ds(row, 1), :].astype(F32)
    seg_cols = jnp.broadcast_to(seg_row, (LANES, length)).T
    lane = lax.broadcasted_iota(jnp.int32, (length, LANES), 1) % HEAD
    same = seg_cols == lane.astype(F32)
    code_q[...] = jnp.where(same, 1.0, 0.0).astype(BF16)
    code_k[...] = jnp.where(same | (lane >= SEGMENTS), 0.0, MASKED).astype(BF16)


ANY = pl.BlockSpec(memory_space=pl.ANY)
WHOLE = pl.BlockSpec(memory_space=pltpu.VMEM)
SCALAR = pl.BlockSpec(memory_space=pltpu.SMEM)


def low(*shape):
    return jax.ShapeDtypeStruct(shape, BF16)


def full(*shape):
    return jax.ShapeDtypeStruct(shape, F32)


def vm(like):
    return pltpu.VMEM(like.shape, like.dtype)


def call(kernel, name, outs, out_specs, inputs, in_specs, scratch, after, flops, moved):
    count, extra = len(inputs), len(after)

    def body(*refs):
        kernel(*refs[:count], *refs[count + extra :])

    return pl.pallas_call(
        body,
        out_shape=outs,
        in_specs=list(in_specs) + [ANY] * extra,
        out_specs=out_specs,
        scratch_shapes=scratch,
        compiler_params=pltpu.CompilerParams(vmem_limit_bytes=LIMIT),
        cost_estimate=pl.CostEstimate(flops=flops, bytes_accessed=moved, transcendentals=0),
        name=name,
    )(*inputs, *after)


def copier(sems):
    def copy(src, dst, number):
        made = pltpu.make_async_copy(src, dst, sems.at[number])
        made.start()
        return made

    return copy


def chunks(length):
    return [slice(place, place + CHUNK) for place in range(0, length, CHUNK)]


def forward_attention_kernel(
    layer,
    scale,
    row_ref,
    x_hbm,
    seg_ref,
    w_in_hbm,
    w_out_hbm,
    qv_ref,
    out_b_ref,
    gain_ref,
    shift_ref,
    qkv_hbm,
    lse_ref,
    mixed_hbm,
    hat_hbm,
    first_hbm,
    full_hbm,
    spread_ref,
    x_ref,
    w_in,
    w_out,
    qkv,
    mixed,
    hat,
    first,
    full,
    code_q,
    code_k,
    terms_ref,
    sems,
):
    row = row_ref[0]
    length, width = x_ref.shape
    copy = copier(sems)
    get_x = copy(x_hbm.at[row, pl.ds(0, length)], x_ref, 0)
    get_in = copy(w_in_hbm.at[layer], w_in, 1)
    get_out = copy(w_out_hbm.at[layer], w_out, 2)
    fill_codes(seg_ref, row, code_q, code_k)
    terms_ref[...] = jnp.zeros_like(terms_ref)
    lse_ref[...] = jnp.zeros_like(lse_ref)
    get_x.wait()
    get_in.wait()

    x = x_ref[...]
    qkv[:, :width] = (
        (mm(x, w_in[:, :width]) + vec(qv_ref, layer, 0, width)).astype(BF16).astype(F32) * scale
    ).astype(BF16)
    qkv[:, width : 2 * width] = mm(x, w_in[:, width : 2 * width]).astype(BF16)
    qkv[:, 2 * width :] = (
        mm(x, w_in[:, 2 * width :]) + vec(qv_ref, layer, width, width)
    ).astype(BF16)
    put_qkv = copy(qkv, qkv_hbm, 3)

    low_half = lax.broadcasted_iota(jnp.int32, (length, LANES), 1) < HEAD
    low_rows = lax.broadcasted_iota(jnp.int32, (LANES, length), 0) < HEAD

    def pair(number, carry):
        at = pl.multiple_of(number * LANES, LANES)
        queries = qkv[:, pl.ds(at, LANES)]
        keys = qkv[:, pl.ds(at + width, LANES)]
        values_t = qkv[:, pl.ds(at + 2 * width, LANES)].T
        outs = []
        for sub in range(2):
            mine = low_half == (sub == 0)
            scores = mm(
                jnp.where(mine, keys, code_k[...]), jnp.where(mine, queries, code_q[...]), NT
            )
            tops = []
            for cols in chunks(length):
                start, stop = window(cols.start, length)
                part = scores[start:stop, cols]
                top = jnp.max(part, 0, keepdims=True)
                terms_ref[sub, start:stop, cols] = jnp.exp(part - top).astype(BF16)
                tops.append(top)
            mine_t = jnp.where(low_rows == (sub == 0), values_t, jnp.ones_like(values_t))
            product = mm(mine_t, terms_ref[sub])
            beside = HEAD * (1 - sub)
            total = product[beside : beside + 1, :]
            lse_ref[pl.ds(2 * number + sub, 1), :] = jnp.concatenate(tops, 1) + jnp.log(total)
            outs.append(product * (1.0 / total))
        mixed[:, pl.ds(at, LANES)] = jnp.where(low_rows, outs[0], outs[1]).T.astype(BF16)
        return carry

    lax.fori_loop(0, HEADS * HEAD // LANES, pair, 0)
    put_mixed = copy(mixed, mixed_hbm, 4)

    get_out.wait()
    gain, shift = vec(gain_ref, layer, 0, width), vec(shift_ref, layer, 0, width)
    out_b = vec(out_b_ref, layer, 0, width)
    branch = mm(mixed[...], w_out[...])
    for rows in chunks(length):
        normed, spread = row_norm(x_ref[rows, :].astype(F32) + branch[rows] + out_b)
        hat[rows, :] = normed.astype(BF16)
        normed = normed * gain + shift
        full[rows, :] = normed
        first[rows, :] = normed.astype(BF16)
        spread_ref[rows, :] = jnp.broadcast_to(spread, (CHUNK, LANES))
    puts = (copy(hat, hat_hbm, 5), copy(first, first_hbm, 6), copy(full, full_hbm, 7))
    for made in (put_qkv, put_mixed) + puts:
        made.wait()


def forward_attention(layer, row, x, seg, weights, after=()):
    w_in, qv, w_out, out_b, gain, shift = weights[:6]
    length, width = seg.shape[-1], x.shape[-1]
    outs = (
        low(length, 3 * width),
        full(16, length),
        low(length, width),
        low(length, width),
        low(length, width),
        full(length, width),
        full(length, LANES),
    )
    return call(
        partial(forward_attention_kernel, layer, HEAD**-0.5),
        f"forward_attention{layer}",
        outs,
        (ANY, WHOLE) + (ANY,) * 4 + (WHOLE,),
        (row, x, seg, w_in, w_out, qv, out_b, gain, shift),
        [SCALAR, ANY, WHOLE, ANY, ANY] + [WHOLE] * 4,
        [
            pltpu.VMEM((length, width), BF16),
            pltpu.VMEM(w_in.shape[1:], BF16),
            pltpu.VMEM(w_out.shape[1:], BF16),
            vm(outs[0]),
            vm(outs[2]),
            vm(outs[3]),
            vm(outs[4]),
            vm(outs[5]),
            pltpu.VMEM((length, LANES), BF16),
            pltpu.VMEM((length, LANES), BF16),
            pltpu.VMEM((2, length, length), BF16),
            pltpu.SemaphoreType.DMA((8,)),
        ],
        after,
        14 * 10**9,
        16 * 10**6,
    )


def forward_ff_kernel(
    layer,
    row_ref,
    first_hbm,
    full_hbm,
    cot_ref,
    seg_ref,
    later_ref,
    w_fi_hbm,
    w_fo_hbm,
    gain_ref,
    shift_ref,
    fi_b_ref,
    fo_b_ref,
    proj_ref,
    proj_b_ref,
    query_ref,
    dense_ref,
    dense_b_ref,
    cls_ref,
    cls_b_ref,
    slope_hbm,
    active_hbm,
    hat_hbm,
    h_hbm,
    spread_ref,
    d_upper_ref,
    small_ref,
    first,
    full,
    w_fi,
    w_fo,
    slope,
    active,
    hat,
    h,
    even,
    odd,
    sems,
):
    length, width = first.shape
    ff = w_fi.shape[1]
    copy = copier(sems)
    get_first = copy(first_hbm, first, 0)
    part = even.shape[1]
    get_fi = [
        copy(w_fi_hbm.at[layer, :, pl.ds(at, part)], w_fi.at[:, pl.ds(at, part)], 8 + at // part)
        for at in range(0, ff, part)
    ]
    get_full = copy(full_hbm, full, 2)
    get_fo = copy(w_fo_hbm.at[layer], w_fo, 3)
    get_first.wait()
    get_fi[0].wait()

    def multiply(at, into):
        into[...] = mm(first[...], w_fi[:, pl.ds(at, part)])

    def bend(at, source):
        bias_part = fi_b_ref[:, pl.ds(at, part)].astype(F32)[layer : layer + 1]
        for rows in chunks(length):
            out, grad = gelu_pair(source[rows, :] + bias_part)
            active[rows, pl.ds(at, part)] = out.astype(BF16)
            slope[rows, pl.ds(at, part)] = grad.astype(BF16)

    multiply(0, even)
    for made in get_fi[1:]:
        made.wait()
    steps = ff // part // 2

    def inner(number, carry):
        at = pl.multiple_of(number * (2 * part), 2 * part)
        multiply(at + part, odd)
        bend(at, even)
        later = pl.multiple_of(jnp.minimum(at + 2 * part, ff - part), part)
        multiply(later, even)
        bend(at + part, odd)
        return carry

    lax.fori_loop(0, steps, inner, 0)
    put_slope = copy(slope, slope_hbm, 4)
    put_active = copy(active, active_hbm, 5)

    get_fo.wait()
    get_full.wait()
    gain, shift = vec(gain_ref, layer, width, width), vec(shift_ref, layer, width, width)
    fo_b = vec(fo_b_ref, layer, 0, width)
    second = mm(active[...], w_fo[...])
    for rows in chunks(length):
        normed, spread = row_norm(full[rows, :] + second[rows] + fo_b)
        hat[rows, :] = normed.astype(BF16)
        h[rows, :] = (normed * gain + shift).astype(BF16)
        spread_ref[rows, :] = jnp.broadcast_to(spread, (CHUNK, LANES))
    put_hat = copy(hat, hat_hbm, 6)

    stu_width = proj_ref.shape[2]
    stu_scale = (stu_width // STU_HEADS) ** -0.5
    hidden = h[:length, :]
    upper = mm(hidden, proj_ref[layer]) + vec(proj_b_ref, layer, 0, stu_width)
    query = vec(query_ref, layer, 0, stu_width)
    lane_full = lax.broadcasted_iota(jnp.int32, (length, stu_width), 1)
    left = lane_full < stu_width // STU_HEADS

    def both(value):
        zero = jnp.zeros_like(value)
        return (
            jnp.sum(jnp.where(left, value, zero), -1, keepdims=True),
            jnp.sum(jnp.where(left, zero, value), -1, keepdims=True),
        )

    weights = []
    for score in both(upper * query):
        score = score * stu_scale
        terms = jnp.exp(score - jnp.max(score, 0, keepdims=True))
        weights.append(terms / jnp.sum(terms, 0, keepdims=True))
    weight = jnp.where(left, weights[0], weights[1])
    pooled = jnp.sum(weight * upper, 0, keepdims=True)
    dense = dense_ref[layer].astype(F32)
    cls = cls_ref[layer].astype(F32)
    eight = (8, stu_width)
    z = jnp.tanh(
        mm_high(jnp.broadcast_to(pooled, eight), dense) + vec(dense_b_ref, layer, 0, stu_width)
    )
    logits = mm_high(z, cls) + vec(cls_b_ref, layer, 0, LANES)
    below = lax.broadcasted_iota(jnp.int32, (16, length), 0)
    segments = jnp.broadcast_to(seg_ref[pl.ds(row_ref[0], 1), :].astype(F32), (16, length))
    later = jnp.broadcast_to(later_ref[pl.ds(row_ref[0], 1), :], (16, LANES))
    tail = jnp.where(below == 1, segments, 0.0)
    narrow_tail = jnp.where(below[:, :LANES] == 2, later, tail[:, :LANES])
    narrow_tail = jnp.where(below[:, :LANES] == 0, jnp.concatenate([logits, logits], 0), narrow_tail)
    h[length:, :LANES] = narrow_tail.astype(BF16)
    h[length:, LANES:length] = tail[:, LANES:].astype(BF16)
    h[length:, length:] = jnp.zeros((16, width - length), BF16)
    put_h = copy(h, h_hbm, 7)
    cot = cot_ref[pl.ds(row_ref[0], 1), :]
    d_pre = mm_high(jnp.broadcast_to(cot, (8, LANES)), cls, NT) * (1.0 - z * z)
    d_pooled = mm_high(d_pre, dense, NT)[:1]
    d_pre = d_pre[:1]

    def column(value):
        return jnp.broadcast_to(value, (value.shape[1], value.shape[1])).T

    d_scores = []
    for weight_col, d_weight in zip(weights, both(upper * d_pooled)):
        mean = jnp.sum(weight_col * d_weight, 0, keepdims=True)
        d_scores.append(weight_col * (d_weight - mean) * stu_scale)
    d_score = jnp.where(left, d_scores[0], d_scores[1])
    d_upper = (weight * d_pooled + d_score * query).astype(BF16)
    d_upper_ref[...] = d_upper
    small_ref[:width, :] = mm(hidden, d_upper, TN)
    small_ref[width : width + stu_width, :] = column(pooled) * d_pre
    small_ref[width + stu_width : width + 2 * stu_width, :] = column(z[:1]) * cot
    base = width + 2 * stu_width
    small_ref[base : base + 1, :] = jnp.sum(d_upper.astype(F32), 0, keepdims=True)
    small_ref[base + 1 : base + 2, :] = jnp.sum(d_score * upper, 0, keepdims=True)
    small_ref[base + 2 : base + 3, :] = d_pre
    small_ref[base + 3 : base + 4, :] = cot
    small_ref[base + 4 :, :] = jnp.zeros((4, LANES), F32)

    for made in (put_slope, put_active, put_hat, put_h):
        made.wait()


def forward_ff(layer, row, first, first_full, cot, seg, later, weights, after=()):
    gain, shift, w_fi, fi_b, w_fo, fo_b = weights[4:10]
    length, width = first.shape
    ff = w_fi.shape[2]
    stu = weights[10].shape[2]
    outs = (
        low(length, ff),
        low(length, ff),
        low(length, width),
        low(length + 16, width),
        full(length, LANES),
        low(length, stu),
        full(width + 2 * stu + 8, LANES),
    )
    return call(
        partial(forward_ff_kernel, layer),
        f"forward_ff{layer}",
        outs,
        (ANY,) * 4 + (WHOLE,) * 3,
        (row, first, first_full, cot, seg, later, w_fi, w_fo, gain, shift, fi_b, fo_b)
        + tuple(weights[10:]),
        [SCALAR, ANY, ANY, WHOLE, WHOLE, WHOLE, ANY, ANY] + [WHOLE] * 11,
        [
            pltpu.VMEM((length, width), BF16),
            pltpu.VMEM((length, width), F32),
            pltpu.VMEM(w_fi.shape[1:], BF16),
            pltpu.VMEM(w_fo.shape[1:], BF16),
            vm(outs[0]),
            vm(outs[1]),
            vm(outs[2]),
            vm(outs[3]),
            pltpu.VMEM((length, 512), F32),
            pltpu.VMEM((length, 512), F32),
            pltpu.SemaphoreType.DMA((8 + ff // 512,)),
        ],
        after,
        18 * 10**9,
        20 * 10**6,
    )


def backward_ff_kernel(
    layer,
    grad_ref,
    d_upper_ref,
    spread1_ref,
    spread2_ref,
    proj_ref,
    gain_ref,
    w_fi_hbm,
    w_fo_hbm,
    hat1_hbm,
    slope_hbm,
    hat2_hbm,
    second_hbm,
    inner_hbm,
    branch_hbm,
    resid_hbm,
    sums_ref,
    w_fi,
    w_fo,
    hat1,
    slope,
    hat2,
    second,
    inner,
    branch,
    d_resid,
    sems,
):
    length, width = grad_ref.shape
    ff = w_fi.shape[1]
    copy = copier(sems)
    get_hat2 = copy(hat2_hbm, hat2, 0)
    get_fo = copy(w_fo_hbm.at[layer], w_fo, 1)
    get_slope = copy(slope_hbm, slope, 2)
    get_fi = copy(w_fi_hbm.at[layer], w_fi, 3)
    get_hat1 = copy(hat1_hbm, hat1, 4)
    sums_ref[...] = jnp.zeros_like(sums_ref)
    get_hat2.wait()
    gain1, gain2 = vec(gain_ref, layer, 0, width), vec(gain_ref, layer, width, width)
    total = lambda value: jnp.sum(value.astype(F32), 0, keepdims=True)

    def through_norm(grads, hat_ref, spread_ref, gain, out_ref):
        d_gain = jnp.zeros((1, width), F32)
        d_shift = jnp.zeros((1, width), F32)
        d_bias = jnp.zeros((1, width), F32)
        for rows in chunks(length):
            grad = grads(rows)
            hat = hat_ref[rows, :].astype(F32)
            d_gain += total(grad * hat)
            d_shift += total(grad)
            moved = norm_back(grad, hat, spread_ref[rows, 0:1], gain)
            d_resid[rows, :] = moved
            out_ref[rows, :] = moved.astype(BF16)
            d_bias += total(moved.astype(BF16))
        return d_gain, d_shift, d_bias

    from_student = mm(d_upper_ref[...], proj_ref[layer], NT)
    d_gain, d_shift, d_bias = through_norm(
        lambda rows: grad_ref[rows, :].astype(F32) + from_student[rows],
        hat2,
        spread2_ref,
        gain2,
        second,
    )
    sums_ref[1:2, 3 * width : 4 * width] = d_gain
    sums_ref[2:3, width : 2 * width] = d_shift
    sums_ref[2:3, 3 * width : 4 * width] = d_bias
    put_second = copy(second, second_hbm, 5)

    get_fo.wait()
    get_slope.wait()
    part = 512

    def ff_part(number, carry):
        at = pl.multiple_of(number * part, part)
        column = jnp.zeros((1, part), F32)
        d_active = mm(second[...], w_fo[pl.ds(at, part), :], NT)
        for rows in chunks(length):
            d_inner = (d_active[rows] * slope[rows, pl.ds(at, part)].astype(F32)).astype(BF16)
            inner[rows, pl.ds(at, part)] = d_inner
            column += total(d_inner)
        sums_ref[0:1, pl.ds(at, part)] = column
        return carry

    lax.fori_loop(0, ff // part, ff_part, 0)
    put_inner = copy(inner, inner_hbm, 6)

    get_fi.wait()
    get_hat1.wait()
    d_first = mm(inner[...], w_fi[...], NT)
    d_gain, d_shift, d_bias = through_norm(
        lambda rows: d_resid[rows, :] + d_first[rows], hat1, spread1_ref, gain1, branch
    )
    sums_ref[1:2, 2 * width : 3 * width] = d_gain
    sums_ref[2:3, :width] = d_shift
    sums_ref[2:3, 2 * width : 3 * width] = d_bias
    for made in (
        put_second,
        put_inner,
        copy(branch, branch_hbm, 7),
        copy(d_resid, resid_hbm, 8),
    ):
        made.wait()


def backward_ff(layer, grad, saved1, saved2, weights, after=()):
    _, _, _, hat1, _, _, spread1 = saved1
    slope, _, hat2, _, spread2, d_upper, _ = saved2
    gain, _, w_fi, _, w_fo, _ = weights[4:10]
    length, width = grad.shape
    ff = w_fi.shape[2]
    outs = (
        low(length, width),
        low(length, ff),
        low(length, width),
        full(length, width),
        full(8, ff),
    )
    return call(
        partial(backward_ff_kernel, layer),
        f"backward_ff{layer}",
        outs,
        (ANY,) * 4 + (WHOLE,),
        (grad, d_upper, spread1, spread2, weights[10], gain, w_fi, w_fo, hat1, slope, hat2),
        [WHOLE] * 6 + [ANY] * 5,
        [
            pltpu.VMEM(w_fi.shape[1:], BF16),
            pltpu.VMEM(w_fo.shape[1:], BF16),
            vm(hat1),
            vm(slope),
            vm(hat2),
            vm(outs[0]),
            vm(outs[1]),
            vm(outs[2]),
            vm(outs[3]),
            pltpu.SemaphoreType.DMA((9,)),
        ],
        after,
        16 * 10**9,
        22 * 10**6,
    )


def backward_attention_kernel(
    layer,
    scale,
    row_ref,
    seg_ref,
    lse_ref,
    w_in_hbm,
    w_out_hbm,
    qkv_hbm,
    mixed_hbm,
    branch_hbm,
    resid_hbm,
    d_qkv_hbm,
    d_x_ref,
    sums_ref,
    w_in,
    w_out,
    qkv,
    mixed,
    branch,
    d_resid,
    d_qkv,
    d_mix,
    code_q,
    code_k,
    delta_ref,
    probs_ref,
    ds_ref,
    sems,
):
    length, width = branch.shape
    copy = copier(sems)
    get_branch = copy(branch_hbm, branch, 0)
    get_out = copy(w_out_hbm.at[layer], w_out, 1)
    get_mixed = copy(mixed_hbm, mixed, 2)
    get_qkv = copy(qkv_hbm, qkv, 3)
    get_in = copy(w_in_hbm.at[layer], w_in, 4)
    get_resid = copy(resid_hbm, d_resid, 5)
    fill_codes(seg_ref, row_ref[0], code_q, code_k)
    probs_ref[...] = jnp.zeros_like(probs_ref)
    ds_ref[...] = jnp.zeros_like(ds_ref)
    sums_ref[...] = jnp.zeros_like(sums_ref)
    total = lambda value: jnp.sum(value.astype(F32), 0, keepdims=True)
    head_of = lax.broadcasted_iota(jnp.int32, (16, width), 1) // HEAD
    ones = (head_of == lax.broadcasted_iota(jnp.int32, (16, width), 0)).astype(F32).astype(BF16)
    get_branch.wait()
    get_out.wait()
    d_mix[...] = mm(branch[...], w_out[...], NT).astype(BF16)
    get_mixed.wait()
    product = d_mix[...].astype(F32) * mixed[...].astype(F32)
    high = product.astype(BF16)
    rest = (product - high.astype(F32)).astype(BF16)
    delta_ref[...] = mm(ones, high, NT) + mm(ones, rest, NT)

    get_qkv.wait()
    low_half = lax.broadcasted_iota(jnp.int32, (length, LANES), 1) < HEAD
    low_rows = lax.broadcasted_iota(jnp.int32, (LANES, length), 0) < HEAD

    def pair(number, carry):
        at = pl.multiple_of(number * LANES, LANES)
        cols = pl.ds(at, LANES)
        key_cols = pl.ds(at + width, LANES)
        value_cols = pl.ds(at + 2 * width, LANES)
        queries, keys, values, mix = qkv[:, cols], qkv[:, key_cols], qkv[:, value_cols], d_mix[:, cols]
        keys_t = keys.T
        d_query = jnp.zeros((LANES, length), F32)
        d_keys, d_values = [], []
        zero = jnp.zeros_like(keys)
        for sub in range(2):
            head = 2 * number + sub
            lse = lse_ref[pl.ds(head, 1), :]
            delta = delta_ref[pl.ds(head, 1), :]
            mine = low_half == (sub == 0)
            scores = mm(
                jnp.where(mine, keys, code_k[...]), jnp.where(mine, queries, code_q[...]), NT
            )
            d_probs = mm(jnp.where(mine, values, zero), mix, NT)
            for rows in chunks(length):
                start, stop = window(rows.start, length)
                probs = jnp.exp(scores[rows, start:stop] - lse[:, start:stop])
                probs_ref[sub, rows, start:stop] = probs.astype(BF16)
                ds_ref[sub, rows, start:stop] = (
                    probs * (d_probs[rows, start:stop] - delta[:, start:stop])
                ).astype(BF16)
            d_values.append(mm(probs_ref[sub], mix))
            d_keys.append(mm(ds_ref[sub], queries))
            mine_t = jnp.where(low_rows == (sub == 0), keys_t, jnp.zeros_like(keys_t))
            d_query += mm(mine_t, ds_ref[sub])
        dq = (d_query.T * scale).astype(BF16)
        d_qkv[:, cols] = dq
        sums_ref[1:2, cols] = total(dq)
        d_qkv[:, key_cols] = jnp.where(low_half, d_keys[0], d_keys[1]).astype(BF16)
        dv = jnp.where(low_half, d_values[0], d_values[1]).astype(BF16)
        d_qkv[:, value_cols] = dv
        sums_ref[1:2, key_cols] = total(dv)
        return carry

    lax.fori_loop(0, HEADS * HEAD // LANES, pair, 0)
    put_qkv = copy(d_qkv, d_qkv_hbm, 6)
    get_in.wait()
    get_resid.wait()
    d_x = mm(d_qkv[...], w_in[...], NT)
    for rows in chunks(length):
        d_x_ref[rows, :] = (d_resid[rows, :] + d_x[rows]).astype(BF16)
    put_qkv.wait()


def backward_attention(layer, row, seg, saved1, branch, d_resid, weights, after=()):
    qkv, lse, mixed = saved1[:3]
    w_in, _, w_out = weights[:3]
    ff = weights[6].shape[2]
    length, width = mixed.shape
    outs = (low(length, 3 * width), low(length, width), full(8, ff))
    return call(
        partial(backward_attention_kernel, layer, HEAD**-0.5),
        f"backward_attention{layer}",
        outs,
        (ANY, WHOLE, WHOLE),
        (row, seg, lse, w_in, w_out, qkv, mixed, branch, d_resid),
        [SCALAR, WHOLE, WHOLE] + [ANY] * 6,
        [
            pltpu.VMEM(w_in.shape[1:], BF16),
            pltpu.VMEM(w_out.shape[1:], BF16),
            vm(qkv),
            vm(mixed),
            vm(branch),
            vm(d_resid),
            vm(outs[0]),
            vm(outs[1]),
            pltpu.VMEM((length, LANES), BF16),
            pltpu.VMEM((length, LANES), BF16),
            pltpu.VMEM((16, length), F32),
            pltpu.VMEM((2, length, length), BF16),
            pltpu.VMEM((2, length, length), BF16),
            pltpu.SemaphoreType.DMA((7,)),
        ],
        after,
        20 * 10**9,
        16 * 10**6,
    )


def grad_cols_kernel(half_ref, *refs, rows, steps):
    lefts, rights = refs[:rows], refs[rows : 2 * rows]
    other_ref, own_ref, turned = refs[-3:]
    length = lefts[0].shape[0]
    step = pl.program_id(0)

    @pl.when(step == 0)
    def _():
        for number, left in enumerate(lefts):
            turned[:, number * length : (number + 1) * length] = left[...].T

    found = None
    for number, right in enumerate(rights):
        part = mm(turned[:, number * length : (number + 1) * length], right[...])
        found = part if found is None else found + part
    found = found.reshape(own_ref.shape).astype(BF16)

    @pl.when(step < steps)
    def _():
        other_ref[...] = found

    @pl.when(step >= steps)
    def _():
        own_ref[...] = found


def weight_grad_cols(half, lefts, rights, narrow, after=()):
    rows = len(lefts)
    length, width = lefts[0].shape
    cols = rights[0].shape[1] // 2
    tile = next((size for size in (768, 384) if cols % size == 0), cols)
    steps = cols // tile
    shape = jax.ShapeDtypeStruct((narrow, width // narrow, cols), BF16)
    block = (narrow, width // narrow, tile)

    def right_at(j, half):
        mine = jnp.where(j < steps, 1 - half[0], half[0])
        return (0, mine * steps + jnp.where(j < steps, j, j - steps))

    return pl.pallas_call(
        partial(grad_cols_kernel, rows=rows, steps=steps),
        out_shape=(shape, shape),
        grid_spec=pltpu.PrefetchScalarGridSpec(
            num_scalar_prefetch=1,
            grid=(2 * steps,),
            in_specs=[pl.BlockSpec((length, width), lambda j, half: (0, 0))] * rows
            + [pl.BlockSpec((length, tile), right_at)] * rows
            + [ANY] * len(after),
            out_specs=(
                pl.BlockSpec(block, lambda j, half: (0, 0, jnp.minimum(j, steps - 1))),
                pl.BlockSpec(block, lambda j, half: (0, 0, jnp.maximum(j - steps, 0))),
            ),
            scratch_shapes=[pltpu.VMEM((width, rows * length), BF16)],
        ),
        compiler_params=pltpu.CompilerParams(vmem_limit_bytes=LIMIT),
        cost_estimate=BRIEF,
        name="weight_grad_cols",
    )(half, *lefts, *rights, *after)


def grad_rows_kernel(half_ref, *refs, rows, narrow):
    lefts, rights = refs[:rows], refs[rows : 2 * rows]
    other_ref, own_ref = refs[-2:]
    unit = own_ref.shape[1]
    width = rights[0].shape[1]
    found = None
    for left, right in zip(lefts, rights):
        part = mm(left[...], right[...], TN)
        found = part if found is None else found + part
    found = found.astype(BF16)

    def write(ref):
        for block in range(ref.shape[2] // width):
            ref[0, :, block * width : (block + 1) * width] = found[
                block * unit : (block + 1) * unit
            ]

    @pl.when(pl.program_id(0) < narrow)
    def _():
        write(other_ref)

    @pl.when(pl.program_id(0) >= narrow)
    def _():
        write(own_ref)


def weight_grad_rows(half, lefts, rights, narrow, after=()):
    rows = len(lefts)
    length, deep = lefts[0].shape
    width = rights[0].shape[1]
    unit = width // narrow
    part = deep // narrow // 2
    cols = part // unit * width
    shape = jax.ShapeDtypeStruct((narrow, unit, cols), BF16)

    def left_at(j, half):
        first = j < narrow
        return (0, 2 * jnp.where(first, j, j - narrow) + jnp.where(first, 1 - half[0], half[0]))

    return pl.pallas_call(
        partial(grad_rows_kernel, rows=rows, narrow=narrow),
        out_shape=(shape, shape),
        grid_spec=pltpu.PrefetchScalarGridSpec(
            num_scalar_prefetch=1,
            grid=(2 * narrow,),
            in_specs=[pl.BlockSpec((length, part), left_at)] * rows
            + [pl.BlockSpec((length, width), lambda j, half: (0, 0))] * rows
            + [ANY] * len(after),
            out_specs=(
                pl.BlockSpec((1, unit, cols), lambda j, half: (jnp.minimum(j, narrow - 1), 0, 0)),
                pl.BlockSpec((1, unit, cols), lambda j, half: (jnp.maximum(j - narrow, 0), 0, 0)),
            ),
        ),
        compiler_params=pltpu.CompilerParams(vmem_limit_bytes=LIMIT),
        cost_estimate=BRIEF,
        name="weight_grad_rows",
    )(half, *lefts, *rights, *after)


def swap(value, bit):
    size = lax.axis_size("wide")
    return lax.ppermute(value, "wide", [(i, i ^ bit) for i in range(size)])


def tie(values, on):
    return lax.optimization_barrier((values, on))[0]


def add_low(left, right):
    return (left.astype(F32) + right.astype(F32)).astype(BF16)


def halves(value, side, axis):
    half = value.shape[axis] // 2
    keep = lax.dynamic_slice_in_dim(value, side * half, half, axis)
    give = lax.dynamic_slice_in_dim(value, (1 - side) * half, half, axis)
    return keep, give


def wide_bits():
    return [1 << i for i in range((lax.axis_size("wide") - 1).bit_length())]


def bit_order(turn):
    rest = wide_bits()[1:]
    return rest[::-1] if turn else rest


class Halving:
    def __init__(self, groups):
        self.place = lax.axis_index("wide")
        self.bits = list(zip(*(bit_order(turn) for turn in range(2))))
        self.groups = groups
        self.flying = None

    def step(self, on=None):
        if self.flying is not None:
            if on is not None:
                self.flying = [(keep, tie(recv, on)) for keep, recv in self.flying]
            self.groups = [[add_low(keep, recv)] for keep, recv in self.flying]
            self.flying = None
        if not self.bits:
            return [group[0] for group in self.groups]
        flying, gives = [], []
        for bit, group in zip(self.bits.pop(0), self.groups):
            split = [halves(part, (self.place // bit) % 2, 1) for part in group]
            keep = jnp.concatenate([pair[0] for pair in split], -1)
            give = jnp.concatenate([pair[1] for pair in split], -1)
            gives.append(give)
            flying.append((keep, swap(give, bit)))
        self.flying = flying
        return gives

    def finish(self, on=None):
        mine = self.step(on)
        while self.flying is not None:
            mine = self.step()
        return jnp.concatenate(mine, -1)


def narrow_parts(mine):
    return mine.reshape((2,) * (mine.shape[0].bit_length() - 1) + mine.shape[1:])


def narrow_level(cur, level, on=None):
    size = lax.axis_size("narrow")
    depth = size.bit_length() - 1
    bit = 1 << level
    keep, give = halves(cur, (lax.axis_index("narrow") // bit) % 2, depth - 1 - level)
    recv = lax.ppermute(give, "narrow", [(i, i ^ bit) for i in range(size)])
    if on is not None:
        recv = tie(recv, on)
    return add_low(keep, recv)


def narrow_sum_swaps(mine, ons=()):
    cur = narrow_parts(mine)
    for level in range(lax.axis_size("narrow").bit_length() - 1):
        cur = narrow_level(cur, level, ons[level] if level < len(ons) else None)
    return cur.reshape(mine.shape[1:])


def wide_gather_swaps(mine, got=None, on=None):
    place = lax.axis_index("wide")
    cur = mine[None]
    for number, bit in enumerate(wide_bits()[::-1]):
        other = got[None] if number == 0 and got is not None else swap(cur, bit)
        if number > 0 and on is not None:
            other = tie(other, on)
        upper = (place // bit) % 2 == 1
        cur = jnp.stack([jnp.where(upper, other, cur), jnp.where(upper, cur, other)])
        cur = cur.reshape((-1,) + mine.shape)
    return cur


def narrow_sum(mine):
    return lax.psum_scatter(mine, "narrow", scatter_dimension=0, tiled=True)[0]


def small_pack_kernel(smalls, *refs):
    small_refs, sums_refs = refs[:smalls], refs[smalls:-4]
    out_ref, small, sums, rest = refs[-4:]
    _, narrow, unit, lanes = out_ref.shape
    width = narrow * unit
    stu = lanes
    share = stu // narrow
    deep = sums.shape[1]
    small[...] = sum(ref[...] for ref in small_refs)
    sums[...] = sum(ref[...] for ref in sums_refs)
    own = width + 2 * stu
    vectors = [
        (sums, 1, 0, 2 * width),
        (sums, 2, 2 * width, width),
        (sums, 1, 2 * width, 2 * width),
        (sums, 2, 0, 2 * width),
        (sums, 0, 0, deep),
        (sums, 2, 3 * width, width),
        (small, own, 0, stu),
        (small, own + 1, 0, stu),
        (small, own + 2, 0, stu),
    ]
    for place in range(narrow):
        out_ref[0, place] = small[place * unit : (place + 1) * unit, :].astype(BF16)
        rest[...] = jnp.zeros_like(rest)
        for number in range(2):
            start = width + number * stu + place * share
            rest[number * share : (number + 1) * share, :] = small[start : start + share, :]
        row = 2 * share
        for ref, line, start, size in vectors:
            size = size // narrow
            value = ref[line : line + 1, :][:, start + place * size : start + (place + 1) * size]
            for at in range(0, size, lanes):
                part = min(lanes, size - at)
                rest[row : row + 1, :part] = value[:, at : at + part]
                row += 1
        rest[row : row + 1, :] = small[own + 3 : own + 4, :]
        out_ref[1, place] = rest[...].astype(BF16)


def small_pack(smalls, sums, narrow):
    stu = smalls[0].shape[1]
    width = smalls[0].shape[0] - 2 * stu - 8
    unit = width // narrow
    return pl.pallas_call(
        partial(small_pack_kernel, len(smalls)),
        out_shape=low(2, narrow, unit, stu),
        in_specs=[WHOLE] * (len(smalls) + len(sums)),
        out_specs=WHOLE,
        scratch_shapes=[vm(smalls[0]), vm(sums[0]), pltpu.VMEM((unit, stu), F32)],
        cost_estimate=BRIEF,
        name="small_pack",
    )(*smalls, *sums)


def place_rows(orders, place, rows):
    found = []
    for order in orders:
        at = 0
        for bit in order:
            at = 2 * at + (place // bit) % 2
        found.append(at * rows)
    return found


def turn_bits(place, total):
    count = (total - 1).bit_length()
    return sum(((place >> i) & 1) << (count - 1 - i) for i in range(count))


def place_ff_kernel(layer, orders, turned, held, got_ref, *refs):
    outs = refs[held : held + 3]
    fi, fo, ao, sems = refs[held + 3 :]
    unit, deep = fi.shape
    width = ao.shape[1]
    half = width // 2
    total, rows, _ = got_ref.shape
    blocks = fo.shape[0] // unit // 2
    for place in range(total):
        core = place % 2
        x_at, y_at = place_rows(orders, place, rows)
        at = turn_bits(place, total) if turned else place
        get = lambda start, size, at=at: got_ref[at, :, start : start + size].astype(F32)
        fi[x_at : x_at + rows, core * deep // 2 : (core + 1) * deep // 2] = get(0, deep // 2)
        for block in range(blocks):
            at = (core * blocks + block) * unit + y_at
            fo[at : at + rows, :] = get(deep // 2 + block * width, width)
        ao[y_at : y_at + rows, core * half : (core + 1) * half] = get(deep, half)
    puts = []
    for number, (src, dst) in enumerate(zip((fi, fo, ao), outs)):
        puts.append(pltpu.make_async_copy(src, dst.at[layer], sems.at[number]))
        puts[-1].start()
    for made in puts:
        made.wait()


def place_attn_kernel(layer, orders, held, got_ref, *refs):
    out, small = refs[held], refs[held + 1]
    ai, sem = refs[held + 2 :]
    total, rows, cols = got_ref.shape
    half = ai.shape[1] // 2
    cut = cols // 2
    rest = half - cut
    for place in range(total):
        core = place % 2
        x_at, y_at = place_rows(orders, place, rows)
        at = turn_bits(place, total)
        get = lambda start, size: got_ref[at, :, start : start + size].astype(F32)
        start = core * half
        ai[x_at : x_at + rows, start : start + cut] = get(0, cut)
        ai[y_at : y_at + rows, start + cut : start + half] = get(cut, rest)
        small[y_at : y_at + rows, core * LANES : (core + 1) * LANES] = get(cut + rest, LANES)
    made = pltpu.make_async_copy(ai, out.at[layer], sem)
    made.start()
    made.wait()


def place_ff(layer, got, turned, shapes, previous=()):
    held = len(previous)
    return pl.pallas_call(
        partial(place_ff_kernel, layer, [bit_order(turn) for turn in range(2)], turned, held),
        out_shape=tuple(shapes),
        in_specs=[WHOLE] + [ANY] * held,
        out_specs=(ANY,) * 3,
        scratch_shapes=[pltpu.VMEM(shape.shape[1:], F32) for shape in shapes]
        + [pltpu.SemaphoreType.DMA((3,))],
        input_output_aliases={1 + i: i for i in range(held)},
        compiler_params=pltpu.CompilerParams(vmem_limit_bytes=LIMIT),
        cost_estimate=pl.CostEstimate(flops=10**6, bytes_accessed=8 * 10**6, transcendentals=0),
        name=f"place_ff{layer}",
    )(got, *previous)


def place_attn(layer, got, shape, previous=(), after=()):
    held = len(previous)

    def body(got_ref, *refs):
        kept = refs[:held] + refs[held + len(after) :]
        place_attn_kernel(layer, orders, held, got_ref, *kept)

    orders = [bit_order(turn) for turn in range(2)]
    return pl.pallas_call(
        body,
        out_shape=(shape, full(shape.shape[1], 2 * LANES)),
        in_specs=[WHOLE] + [ANY] * (held + len(after)),
        out_specs=(ANY, WHOLE),
        scratch_shapes=[pltpu.VMEM(shape.shape[1:], F32), pltpu.SemaphoreType.DMA],
        input_output_aliases={1 + i: i for i in range(held)},
        compiler_params=pltpu.CompilerParams(vmem_limit_bytes=LIMIT),
        cost_estimate=pl.CostEstimate(flops=10**6, bytes_accessed=3 * 10**6, transcendentals=0),
        name=f"place_attn{layer}",
    )(got, *previous, *after)


def place_small_kernel(first_ref, second_ref, proj_ref, dense_ref, cls_ref, *vec_refs):
    for layer, ref in enumerate((first_ref, second_ref)):
        stu = dense_ref.shape[1]
        proj_ref[layer] = ref[:, :LANES]
        dense_ref[layer] = ref[:stu, LANES:]
        cls_ref[layer] = ref[stu : 2 * stu, LANES : LANES + cls_ref.shape[2]]
        row = 2 * stu
        for out in vec_refs:
            size = out.shape[1]
            for start in range(0, size, LANES):
                part = min(LANES, size - start)
                out[layer : layer + 1, start : start + part] = ref[
                    row : row + 1, LANES : LANES + part
                ]
                row += 1


def place_small(first, second, width, deep, classes, narrow):
    sizes = [2 * width, width, 2 * width, 2 * width, deep, width, LANES, LANES, LANES]
    stu = LANES // narrow
    outs = (
        full(2, width // narrow, LANES),
        full(2, stu, LANES),
        full(2, stu, classes),
    ) + tuple(full(2, size // narrow) for size in sizes)
    return pl.pallas_call(
        place_small_kernel,
        out_shape=outs + (full(2, classes),),
        in_specs=[WHOLE, WHOLE],
        out_specs=(WHOLE,) * 13,
        name="place_small",
    )(first, second)


def route_kernel(me_ref, *refs):
    around, out_ref, held = refs[:-2], refs[-2], refs[-1]
    me, size = me_ref[0], len(around)
    for step, ref in enumerate(around):
        held[lax.rem(me + (size - step), size)] = ref[0]
    counts = [held[i] for i in range(size)]
    flow, before = [], []
    total = jnp.int32(0)
    for value in counts:
        before.append(total)
        total = total + value - 1
        flow.append(total)
    right1 = [(f >= 1) & (c >= 1) for f, c in zip(flow, counts)]
    left1 = [(f <= -1) & (c >= 1) for f, c in zip(before, counts)]
    right2 = [(f >= 1) & ((f >= 2) | (c == 0)) for f, c in zip(flow, counts)]
    left2 = [(f <= -1) & ((f <= -2) | (c == 0)) for f, c in zip(before, counts)]

    def at(values, shift):
        found = jnp.int32(0)
        for i, value in enumerate(values):
            found = jnp.where(me + shift == i, value.astype(jnp.int32), found)
        return found

    count = at(counts, 0)
    from_left2, from_right2 = at(right2, -1), at(left2, 1)
    sent_right, sent_left = at(right1, 0), at(left1, 0)
    results = (
        at(right1, -1),
        from_left2,
        from_left2 | from_right2,
        (count == 2).astype(jnp.int32),
        ((count == 1) & (sent_right + sent_left == 0)).astype(jnp.int32),
        at(right2, 0),
        sent_left,
        (sent_right & at(right2, 1)) | (sent_left & at(left2, -1)),
        (count >= 1).astype(jnp.int32),
        (count >= 2).astype(jnp.int32),
    )
    for i, value in enumerate(results):
        out_ref[i] = value
    for i in range(len(results), out_ref.shape[0]):
        out_ref[i] = 0


def route(me, around):
    return pl.pallas_call(
        route_kernel,
        out_shape=jax.ShapeDtypeStruct((16,), jnp.int32),
        in_specs=[SCALAR] * (1 + len(around)),
        out_specs=SCALAR,
        scratch_shapes=[pltpu.SMEM((len(around),), jnp.int32)],
        name="route",
    )(me, *around)


def shards(
    tokens,
    segments,
    exit_layer,
    attn_in,
    qv_bias,
    attn_out,
    out_bias,
    ln_gain,
    ln_bias,
    ff_in,
    ff_in_bias,
    ff_out,
    ff_out_bias,
    stu_proj,
    stu_bias,
    pool_query,
    stu_dense,
    stu_dense_bias,
    stu_cls,
    stu_cls_bias,
    out_cot,
    logit_cot,
):
    row_count, length, width = tokens.shape
    classes = stu_cls.shape[-1]
    blank = LANES - classes
    narrow = lax.axis_size("narrow")
    me = lax.axis_index("narrow")
    core = lax.axis_index("wide") % 2
    weights = (
        attn_in,
        qv_bias,
        attn_out,
        out_bias,
        ln_gain,
        ln_bias,
        ff_in,
        ff_in_bias,
        ff_out,
        ff_out_bias,
        stu_proj,
        stu_bias,
        pool_query,
        stu_dense,
        stu_dense_bias,
        jnp.pad(stu_cls, ((0, 0), (0, 0), (0, blank))),
        jnp.pad(stu_cls_bias, ((0, 0), (0, blank))),
    )
    wide_cot = jnp.pad(logit_cot.astype(F32), ((0, 0), (0, 0), (0, blank)))

    alive = exit_layer == 1
    row_a = jnp.where(alive[0], 0, jnp.where(alive[1], 1, 0)).astype(jnp.int32)
    row_b = 1 - row_a

    index = lambda row: row.reshape(1)
    first_row = jnp.zeros((1,), jnp.int32)
    own = index(core)
    ia, ib = index(row_a), index(row_b)
    early_cot, late_cot = wide_cot[:, 0], wide_cot[:, 1]
    a1 = forward_attention(0, ia, tokens, segments, weights)

    mine = tie(jnp.sum(alive.astype(jnp.int32)).reshape(1), a1[4])
    around = [mine] + [
        lax.ppermute(mine, "narrow", [(i, (i + step) % narrow) for i in range(narrow)])
        for step in range(1, narrow)
    ]
    flags = route(me.reshape(1), around)
    from_left1, from_left2, use_two, use_b, use_a, on_right, sent_left, is_far, a_alive, b_alive = (
        flags[i] == 1 for i in range(10)
    )

    even = me % 2 == 0
    inner = [(i, i ^ 1) for i in range(narrow)]
    outer = []
    for i in range(lax.axis_size("wide") * narrow):
        place, line = i // narrow, i % narrow
        other = ((line + 1) ^ 1) - 1
        inside = 0 <= other < narrow
        outer.append((i, place * narrow + other if inside else (place ^ 1) * narrow + line))

    def shift(value):
        return (
            lax.ppermute(value, "narrow", inner),
            lax.ppermute(value, ("wide", "narrow"), outer),
        )

    def pick(pair, is_left):
        return jnp.where(is_left == even, pair[1], pair[0])

    def out_one(pair):
        return pick(pair, from_left1)

    def out_two(pair, one, own_a, own_b):
        two = pick(pair, from_left2)
        return jnp.where(use_b, own_b, jnp.where(use_a, own_a, jnp.where(use_two, two, one)))

    def back_one(pair):
        return pick(pair, ~on_right)

    def back_two(value, pair, pair2):
        return jnp.where(
            use_a, value, jnp.where(is_far, pick(pair2, sent_left), pick(pair, sent_left))
        )

    def row_of(value, row):
        return lax.dynamic_index_in_dim(value, row, 0, False)

    cot_a, cot_b = row_of(out_cot, row_a), row_of(out_cot, row_b)
    pair = shift(tie(cot_a, a1[4]))
    a2 = forward_ff(0, ia, a1[4], a1[5], early_cot, segments, late_cot, weights, (cot_a,))
    cot_one = out_one(tie(pair, a2[3]))
    pair = shift(a2[3])
    b1 = forward_attention(0, ib, tokens, segments, weights, (a2[3], cot_one))
    one = out_one(tie(pair, b1[4]))
    pair = shift(one)
    b2 = forward_ff(0, ib, b1[4], b1[5], early_cot, segments, late_cot, weights, (one,))
    work_in = out_two(tie(pair, b2[3]), one, a2[3], b2[3])
    work_seg = work_in[length + 1 : length + 2, :length].astype(jnp.int32)
    work_late = work_in[length + 2 : length + 3, :LANES].astype(F32)

    pair = shift(tie(cot_one, b2[3]))
    w1 = forward_attention(1, first_row, work_in[None], work_seg, weights)
    work_cot = out_two(tie(pair, w1[4]), cot_one, cot_a, cot_b)
    w2 = forward_ff(
        1, first_row, w1[4], w1[5], work_late, work_seg, work_late, weights, (work_cot,)
    )
    sent_h = w2[3]
    pair_h = shift(sent_h)
    w3 = backward_ff(1, work_cot, w1, w2, weights, (sent_h,))

    def ff_jobs(saved1, saved2, back):
        first = [s[4] for s in saved1]
        mixed = [s[2] for s in saved1]
        active = [s[1] for s in saved2]
        second, inner, branch = ([b[i] for b in back] for i in range(3))
        return (
            (weight_grad_cols, first, inner),
            (weight_grad_rows, active, second),
            (weight_grad_cols, mixed, branch),
        )

    def weight_grads(jobs, after=()):
        return [job(own, lefts, rights, narrow, after) for job, lefts, rights in jobs]

    def core_sum(pairs, on=None):
        received = [swap(other, 1) for other, _ in pairs]
        if on is not None:
            received = tie(received, on)
        return [add_low(mine, recv) for (_, mine), recv in zip(pairs, received)]

    def ff_halving(parts):
        return Halving([[parts[0]], [parts[1], parts[2]]])

    def attn_halving(part, small):
        keep, give = halves(small, core, 0)
        small = add_low(keep, swap(give, 1))[0]
        cut = (part.shape[-1] + LANES) // 2
        return Halving([[part[..., :cut]], [part[..., cut:], small]])

    halves1 = weight_grads(ff_jobs([w1], [w2], [w3]))
    sent = tuple(pair[0] for pair in halves1)
    w4 = backward_attention(1, first_row, work_seg, w1, w3[2], w3[3], weights, sent)
    pair_x = shift(w4[1])
    ff1 = ff_halving(core_sum(halves1))
    flying = ff1.step()
    half1 = weight_grads(((weight_grad_cols, [work_in[:length]], [w4[0]]),), tuple(flying))
    small1 = small_pack([w2[6]], [w3[4], w4[2]], narrow)
    forth_x = back_one(tie(pair_x, half1[0][0]))
    pair_x2 = shift(forth_x)

    base_b = jnp.where(b_alive, w4[1], row_of(out_cot, row_b))
    b3 = backward_ff(0, base_b, b1, b2, weights, (half1[0][0], forth_x, small1))
    far_x = back_two(w4[1], pair_x, tie(pair_x2, b3[2]))
    forth_h = back_one(tie(pair_h, far_x))
    pair_h2 = shift(forth_h)
    at1 = attn_halving(core_sum(half1)[0], small1)
    flying = at1.step() + ff1.step(b3[2])
    base_a = jnp.where(a_alive, far_x, row_of(out_cot, row_a))
    a3 = backward_ff(0, base_a, a1, a2, weights, (*flying, forth_h))
    mine_ff1 = ff1.finish(a3[2])
    flying = at1.step(a3[2])
    halves0 = weight_grads(ff_jobs([a1, b1], [a2, b2], [a3, b3]), (mine_ff1, *flying))
    ff0 = ff_halving(core_sum(halves0))
    flying = ff0.step()
    far_h = back_two(sent_h, pair_h, tie(pair_h2, a3[2]))
    b4 = backward_attention(
        0, ib, segments, b1, b3[2], b3[3], weights, (*flying, far_h)
    )
    flying = ff0.step(b4[1])
    sum_at1 = narrow_sum(at1.finish(b4[1]))
    a4 = backward_attention(0, ia, segments, a1, a3[2], a3[3], weights, (b4[1], *flying))
    mine_ff0 = ff0.finish((a4[1], sum_at1))
    sum_ff1 = narrow_sum_swaps(mine_ff1, (b4[1], a4[1]))
    half0 = weight_grads(
        (
            (
                weight_grad_cols,
                [row_of(tokens, row_a), row_of(tokens, row_b)],
                [a4[0], b4[0]],
            ),
        ),
        (mine_ff0, sum_ff1),
    )
    part_ff0 = narrow_level(narrow_parts(mine_ff0), 0, half0[0][0])
    got_ff1 = tie(swap(tie(sum_ff1, mine_ff0), wide_bits()[-1]), half0[0][0])
    half0 = [(tie(half0[0][0], part_ff0), half0[0][1])]
    last_sums = tie(a4[2], half0[0][0])
    small0 = small_pack([a2[6], b2[6]], [a3[4], b3[4], last_sums, b4[2]], narrow)
    at0 = attn_halving(core_sum(half0)[0], small0)
    flying = at0.step()
    for level in range(1, narrow.bit_length() - 1):
        part_ff0 = narrow_level(part_ff0, level, flying)
    sum_ff0 = part_ff0.reshape(mine_ff0.shape[1:])
    all_ff1 = wide_gather_swaps(sum_ff1, got_ff1, flying)
    all_ff0 = lax.all_gather(sum_ff0, "wide", axis=0, tiled=False)
    all_at1 = wide_gather_swaps(tie(sum_at1, flying))
    sum_at0 = narrow_sum_swaps(at0.finish(), (None, all_ff0))

    deep = ff_in.shape[2]
    unit = width // narrow
    shapes = [full(2, unit, deep), full(2, deep // narrow, width), full(2, unit, width)]
    attn_shape = full(2, unit, 3 * width)
    placed = place_ff(1, all_ff1, True, shapes)
    all_at0 = wide_gather_swaps(sum_at0, None, placed[2])
    d_attn_in, small1 = place_attn(1, all_at1, attn_shape)
    placed = place_ff(0, all_ff0, False, shapes, placed)
    d_attn_in, small0 = place_attn(0, all_at0, attn_shape, (d_attn_in,), (placed[2],))
    d_ff_in, d_ff_out, d_attn_out = placed
    (d_proj, d_dense, d_cls, d_qv, d_out_b, d_gain, d_shift, d_fi_b, d_fo_b, *rest) = place_small(
        small0, small1, width, deep, classes, narrow
    )
    d_stu_b, d_query, d_dense_b, d_cls_b = rest
    totals = (
        d_attn_in,
        d_qv,
        d_attn_out,
        d_out_b,
        d_gain,
        d_shift,
        d_ff_in,
        d_fi_b,
        d_ff_out,
        d_fo_b,
        d_proj,
        d_stu_b,
        d_query,
        d_dense,
        d_dense_b,
        d_cls,
        d_cls_b,
    )

    in_order = lambda for_a, for_b: jnp.where(
        row_a == 0, jnp.stack([for_a, for_b]), jnp.stack([for_b, for_a])
    )
    act_a = jnp.where(a_alive, far_h, a2[3])
    act_b = jnp.where(b_alive, w2[3], b2[3])
    cut = lambda value: value[length, :classes]
    logits = jnp.where(jnp.stack([a_alive, b_alive])[:, None], jnp.stack([cut(act_a), cut(act_b)]), 0)
    early = in_order(cut(a2[3]), cut(b2[3]))
    logits = jnp.stack([early, in_order(logits[0], logits[1])], 1).astype(BF16)
    act_a, act_b = act_a[:length], act_b[:length]
    return (in_order(act_a, act_b), logits, in_order(a4[1], b4[1])) + totals


def solution(mesh):
    rows = ("wide", "narrow")
    return jax.shard_map(
        shards,
        mesh=mesh,
        in_specs=(P(rows, None, None), P(rows, None), P(rows))
        + (P(),) * 17
        + (P(rows, None, None), P(rows, None, None)),
        out_specs=(P(rows, None, None),) * 3
        + (
            P(None, "narrow", None),
            P(None, "narrow"),
            P(None, "narrow", None),
            P(None, "narrow"),
            P(None, "narrow"),
            P(None, "narrow"),
            P(None, "narrow", None),
            P(None, "narrow"),
            P(None, "narrow", None),
            P(None, "narrow"),
            P(None, "narrow", None),
            P(None, "narrow"),
            P(None, "narrow"),
            P(None, "narrow", None),
            P(None, "narrow"),
            P(None, "narrow", None),
            P(),
        ),
        check_vma=False,
    )
```
